32 devices in a mesh: dp: 4 (over y, x), ctx: 8 (over z, core).
Axes of the slice: x: 2, y: 2, z: 4, core: 2. Of those that a mesh axis runs over, the one named last changes fastest.
Arguments:
- tokens: bfloat16 [8, 1536, 2304], P('dp', 'ctx'), may hold values from -7 to 7
- span_start: int32 [8, 2], P('dp'), may hold values from 0 to 1408, as said below
- span_len: int32 [8, 2], P('dp'), may hold values from 128 to 256, as said below
- query_weight: bfloat16 [2048, 2304], P('ctx'), may hold values from -1 to 1
- key_weight: bfloat16 [1024, 2304], P('ctx'), may hold values from -1 to 1
- value_weight: bfloat16 [1024, 2304], P('ctx'), may hold values from -0.125 to 0.125
- output_weight: bfloat16 [2048, 2304], P('ctx'), may hold values from -0.125 to 0.125
- gate_weight: bfloat16 [9216, 2304], P('ctx'), may hold values from -0.125 to 0.125
- up_weight: bfloat16 [9216, 2304], P('ctx'), may hold values from -0.125 to 0.125
- down_weight: bfloat16 [9216, 2304], P('ctx'), may hold values from -0.0625 to 0.0625
- inbound_gain: bfloat16 [2304], P('ctx'), may hold values from 0.099609375 to 1.8984375
- attended_gain: bfloat16 [2304], P('ctx'), may hold values from 0.099609375 to 1.8984375
- prefeed_gain: bfloat16 [2304], P('ctx'), may hold values from 0.099609375 to 1.8984375
- postfeed_gain: bfloat16 [2304], P('ctx'), may hold values from 0.099609375 to 1.8984375
- cotangent: bfloat16 [8, 1536, 2304], P('dp', 'ctx'), may hold values from -6 to 6
Outputs:
- layer_output: bfloat16 [8, 1536, 2304], P('dp', 'ctx')
- tokens_grad: bfloat16 [8, 1536, 2304], P('dp', 'ctx')
- query_grad: float32 [2048, 2304], P('ctx')
- key_grad: float32 [1024, 2304], P('ctx')
- value_grad: float32 [1024, 2304], P('ctx')
- output_grad: float32 [2048, 2304], P('ctx')
- gate_grad: float32 [9216, 2304], P('ctx')
- up_grad: float32 [9216, 2304], P('ctx')
- down_grad: float32 [9216, 2304], P('ctx')
- inbound_grad: float32 [2304], P('ctx')
- attended_grad: float32 [2304], P('ctx')
- prefeed_grad: float32 [2304], P('ctx')
- postfeed_grad: float32 [2304], P('ctx')
The draws below stay inside these ranges and needn't reach their ends.
Inputs may be any that keep to these rules, and one draw needn't show every extreme that they name: `span_start`: in each sequence the 2 spans lie in order without intersection; span s lies within positions s * 768 to (s + 1) * 768 - 1. `span_len`: one span of each sequence has exactly 256 tokens.
All inputs are finite; a program needn't handle non-finite values.
Results may differ from the reference program's by a relative error of at most 0.025.
Values may be sent and summed in bfloat16 or wider, within the bound.
No kernel may reach another device: no remote copies, remote signals or barrier semaphores. Data moves between devices by JAX's collectives and lax.ppermute only.
A program may use at most 576 MiB of HBM per device.

```python
import jax
import jax.numpy as jnp
from jax import lax

D = 2304
FF = 9216
HEADS = 8
KV_HEADS = 4
HEAD_DIM = 256
LEN = 1536
SPANS = 2
PIC = 256
QW = 2048
KW = 1024
SEQS = 8


token_share = 0.75


row_share = 9.8


def span_table(key):
    length_key, pick_key, offset_key = jax.random.split(key, 3)
    lengths = jax.random.randint(length_key, (SEQS, SPANS), PIC // 2, PIC + 1)
    chosen = jax.random.randint(pick_key, (SEQS, 1), 0, SPANS)
    lengths = jnp.where(jnp.arange(SPANS)[None, :] == chosen, PIC, lengths)
    region = LEN // SPANS
    offsets = jax.random.randint(offset_key, (SEQS, SPANS), 0, 1 << 20) % (region - lengths + 1)
    starts = jnp.arange(SPANS)[None, :] * region + offsets
    return (starts.astype(jnp.int32), lengths.astype(jnp.int32))


def draw_span_start(key, part):
    return span_table(key)[0]


def draw_span_len(key, part):
    return span_table(key)[1]


def common_parts(key):
    vector_key, head_key = jax.random.split(jax.random.fold_in(key, 97))
    direction = jnp.clip(jax.random.normal(vector_key, (D,), jnp.float32), -4.0, 4.0)
    picked = jax.random.randint(head_key, (), 0, KV_HEADS)
    return (direction, picked)


def feature_rows(row_count, heads_per_key):
    rows = jnp.arange(row_count)
    features = rows % HEAD_DIM
    half_width = HEAD_DIM // 2
    pairs = max(2, HEAD_DIM // 32)
    slow = features % half_width >= half_width - pairs
    owner = rows // HEAD_DIM // heads_per_key
    return (slow, owner)


def projection_draw(key, row_count, heads_per_key):
    direction, picked = common_parts(key)
    slow, owner = feature_rows(row_count, heads_per_key)
    noise = jnp.clip(jax.random.normal(key, (row_count, D), jnp.float32), -3.5, 3.5) * D ** (-0.5)
    lifted = jnp.where(slow & (owner == picked), row_share / D, 0.0)
    return noise + lifted[:, None] * direction[None, :]


def draw_tokens(key, part):
    direction, picked = common_parts(key)
    key = jax.random.fold_in(key, 11)
    noise = jnp.clip(jax.random.normal(key, (SEQS, LEN, D), jnp.float32), -4.0, 4.0)
    return (noise + token_share * direction[None, None, :]).astype(jnp.bfloat16)


def draw_query_weight(key, part):
    return projection_draw(jax.random.fold_in(key, 23), HEADS * HEAD_DIM, HEADS // KV_HEADS).astype(jnp.bfloat16)


def draw_key_weight(key, part):
    return projection_draw(jax.random.fold_in(key, 37), KV_HEADS * HEAD_DIM, 1).astype(jnp.bfloat16)


def block_levels(stream_key, extent, pieces, low, high):
    def one(position, parts):
        heights = jax.random.uniform(jax.random.fold_in(jax.random.fold_in(stream_key, 6), position), (parts,), jnp.float32, low / len(pieces), high / len(pieces))
        return jnp.repeat(jnp.exp(heights), extent[position] // parts).reshape((-1,) + (1,) * (len(extent) - position - 1))

    factor_of = one(*pieces[0])
    for cut in pieces[1:]:
        factor_of = factor_of * one(*cut)
    return factor_of


def normal_values(own_key, extent, width, bound, shards=(), kind=jnp.bfloat16):
    drawn = jax.random.normal(own_key, extent, jnp.float32) * width
    if len(shards) > 0:
        drawn = block_levels(own_key, extent, shards, -0.22, 0.18) * drawn
    return jnp.clip(drawn, min=-bound, max=bound).astype(kind)


def setup_inputs(seed: int = 0) -> dict:
    streams_of = jax.random.split(jax.random.key(seed), 16)
    return {
        "tokens": draw_tokens(jax.random.fold_in(streams_of[15], 71), 0),
        "span_start": draw_span_start(jax.random.fold_in(streams_of[15], 71), 0),
        "span_len": draw_span_len(jax.random.fold_in(streams_of[15], 71), 0),
        "query_weight": draw_query_weight(jax.random.fold_in(streams_of[15], 71), 0),
        "key_weight": draw_key_weight(jax.random.fold_in(streams_of[15], 71), 0),
        "value_weight": normal_values(streams_of[5], (KW, D), D ** -0.5, 0.125, ((0, 8),)),
        "output_weight": normal_values(streams_of[6], (QW, D), QW ** -0.5, 0.125, ((0, 8),)),
        "gate_weight": normal_values(streams_of[7], (FF, D), D ** -0.5, 0.125, ((0, 8),)),
        "up_weight": normal_values(streams_of[8], (FF, D), D ** -0.5, 0.125, ((0, 8),)),
        "down_weight": normal_values(streams_of[9], (FF, D), FF ** -0.5, 0.0625, ((0, 8),)),
        "inbound_gain": jnp.clip(1.0 + 0.18 * jax.random.normal(streams_of[10], (D,), jnp.float32), 0.099609375, 1.8984375).astype(jnp.bfloat16),
        "attended_gain": jnp.clip(1.0 + 0.18 * jax.random.normal(streams_of[11], (D,), jnp.float32), 0.099609375, 1.8984375).astype(jnp.bfloat16),
        "prefeed_gain": jnp.clip(1.0 + 0.18 * jax.random.normal(streams_of[12], (D,), jnp.float32), 0.099609375, 1.8984375).astype(jnp.bfloat16),
        "postfeed_gain": jnp.clip(1.0 + 0.18 * jax.random.normal(streams_of[13], (D,), jnp.float32), 0.099609375, 1.8984375).astype(jnp.bfloat16),
        "cotangent": normal_values(streams_of[14], (SEQS, LEN, D), 1.0, 6.0, ((0, 4), (1, 8))),
    }


epsilon = 1e-06
soft_cap = 50.0
masked_score = -1e+30
rope_base = 10000.0
highest = lax.Precision.HIGHEST

@jax.custom_vjp
def low(v):
    return lax.optimization_barrier(v.astype(jnp.bfloat16)).astype(jnp.float32)

@jax.custom_vjp
def low_back(v):
    return v

def low_keep(v):
    return (low(v), None)

def low_pass(kept, grad):
    return (grad,)

def back_keep(v):
    return (v, None)

def back_low(kept, grad):
    return (low(grad),)
low.defvjp(low_keep, low_pass)
low_back.defvjp(back_keep, back_low)

def root_norm(values, gain_vector):
    return values * lax.rsqrt(lax.optimization_barrier(jnp.mean(values * values, axis=-1, keepdims=True)) + epsilon) * gain_vector

def project(left_side, weight):
    return jnp.dot(left_side, weight.T, precision=highest, preferred_element_type=jnp.float32)

def rope_tables(places):
    half_width = HEAD_DIM // 2
    inverse = rope_base ** (-(jnp.arange(half_width, dtype=jnp.float32) * 2.0 / HEAD_DIM))
    angles = places.astype(jnp.float32)[:, None] * inverse[None, :]
    return (jnp.cos(angles)[:, None, :], jnp.sin(angles)[:, None, :])

def rotate(head_vectors, cosine, sine_table):
    half_width = HEAD_DIM // 2
    first_half = head_vectors[..., :half_width]
    second_half = head_vectors[..., half_width:]
    return jnp.concatenate([first_half * cosine - second_half * sine_table, second_half * cosine + first_half * sine_table], axis=-1)

def span_labels(places, starts, lengths):
    inside = (places[:, None] >= starts[None, :]) & (places[:, None] < (starts + lengths)[None, :])
    labels = jnp.arange(1, SPANS + 1, dtype=jnp.int32)
    return lax.optimization_barrier(jnp.sum(jnp.where(inside, labels[None, :], 0), axis=1)).astype(jnp.int32) - 1

def visible(query_place, key_place, starts, lengths):
    query_span = span_labels(query_place, starts, lengths)
    key_span = span_labels(key_place, starts, lengths)
    causal = key_place[None, :] <= query_place[:, None]
    shared = (query_span[:, None] == key_span[None, :]) & (query_span[:, None] >= 0)
    return causal | shared

def attention(queries, keys, values, allowed):
    group_size = HEADS // KV_HEADS
    query_heads = queries.reshape(LEN, KV_HEADS, group_size, HEAD_DIM)
    key_heads = keys.reshape(LEN, KV_HEADS, HEAD_DIM)
    value_heads = values.reshape(LEN, KV_HEADS, HEAD_DIM)
    raw_scores = low_back(jnp.einsum('ikgd,jkd->kgij', query_heads, key_heads, precision=highest))
    capped = soft_cap * jnp.tanh(raw_scores / soft_cap)
    masked = jnp.where(allowed, capped, masked_score)
    row_peak = lax.optimization_barrier(jnp.max(masked, axis=-1, keepdims=True))
    unscaled = jnp.where(allowed, jnp.exp(masked - row_peak), 0.0)
    softmax_rows = unscaled / lax.optimization_barrier(jnp.sum(unscaled, axis=-1, keepdims=True))
    attended = jnp.einsum('kgij,jkd->ikgd', low(softmax_rows), value_heads, precision=highest)
    return attended.reshape(LEN, HEADS * HEAD_DIM)

def layer(tokens, query_weight, key_weight, value_weight, output_weight, gate_weight, up_weight, down_weight, inbound_gain, attended_gain, prefeed_gain, postfeed_gain, allowed, cosine, sine_table):
    hidden_in = low(root_norm(tokens, inbound_gain))
    queries_raw = low_back(project(hidden_in, query_weight))
    keys_raw = low_back(project(hidden_in, key_weight))
    values_raw = low_back(project(hidden_in, value_weight))
    queries = low(rotate(queries_raw.reshape(LEN, HEADS, HEAD_DIM), cosine, sine_table) * HEAD_DIM ** (-0.5)).reshape(LEN, HEADS * HEAD_DIM)
    keys = low(rotate(keys_raw.reshape(LEN, KV_HEADS, HEAD_DIM), cosine, sine_table)).reshape(LEN, KV_HEADS * HEAD_DIM)
    values = low(values_raw)
    attended = low(low_back(attention(queries, keys, values, allowed)))
    branch = low_back(jnp.dot(attended, output_weight, precision=highest, preferred_element_type=jnp.float32))
    middle = tokens + root_norm(branch, attended_gain)
    hidden_ff = low(root_norm(middle, prefeed_gain))
    gate_value = low_back(project(hidden_ff, gate_weight))
    up_value = low_back(project(hidden_ff, up_weight))
    product = low(jax.nn.gelu(gate_value, approximate=True) * up_value)
    feed_out = low_back(jnp.dot(product, down_weight, precision=highest, preferred_element_type=jnp.float32))
    return middle + root_norm(feed_out, postfeed_gain)

def reference(tokens, span_start, span_len, query_weight, key_weight, value_weight, output_weight, gate_weight, up_weight, down_weight, inbound_gain, attended_gain, prefeed_gain, postfeed_gain, cotangent):
    weights = tuple((matrix.astype(jnp.float32) for matrix in (query_weight, key_weight, value_weight, output_weight, gate_weight, up_weight, down_weight, inbound_gain, attended_gain, prefeed_gain, postfeed_gain)))
    places = jnp.arange(LEN, dtype=jnp.int32)
    cosine, sine_table = rope_tables(places)

    def seq_step(running, seq_items):
        seq_tokens, seq_cotangent, starts, lengths = seq_items
        allowed = visible(places, places, starts, lengths)

        def forward(seq_input, *params):
            return layer(seq_input, *params, allowed, cosine, sine_table)
        output, backward = jax.vjp(forward, seq_tokens.astype(jnp.float32), *weights)
        gradients = backward(seq_cotangent.astype(jnp.float32))
        running = tuple((earlier + fresh_grad for earlier, fresh_grad in zip(running, gradients[1:])))
        return (running, (output.astype(jnp.bfloat16), gradients[0].astype(jnp.bfloat16)))
    zero_init = tuple((jnp.zeros_like(matrix) for matrix in weights))
    totals, (outputs, token_grads) = lax.scan(seq_step, zero_init, (tokens, cotangent, span_start, span_len))
    return (outputs, token_grads, totals[0], totals[1], totals[2], totals[3], totals[4], totals[5], totals[6], totals[7], totals[8], totals[9], totals[10])
```

```python
import functools

import jax
import jax.numpy as jnp
from jax import lax
from jax.experimental import pallas as pl
from jax.experimental.pallas import tpu as pltpu
from jax.sharding import PartitionSpec as P

HEADS = 8
KV_HEADS = 4
HEAD_DIM = 256
HALF = HEAD_DIM // 2

epsilon = 1e-06
soft_cap = 50.0
rope_base = 10000.0
gelu_a = 0.7978845608028654
gelu_b = 0.044715

bf16 = jnp.bfloat16
f32 = jnp.float32


def nt(left_side, right_side):
    return lax.dot_general(
        left_side, right_side, (((1,), (1,)), ((), ())), preferred_element_type=f32
    )


def nn(left_side, right_side):
    return lax.dot_general(
        left_side, right_side, (((1,), (0,)), ((), ())), preferred_element_type=f32
    )


def tn(left_side, right_side):
    return lax.dot_general(
        left_side, right_side, (((0,), (0,)), ((), ())), preferred_element_type=f32
    )


class Line:
    def __init__(self, size, index):
        self.chips = size // 2
        self.z = index // 2
        self.c = index % 2
        self.core_pairs = [(i, i ^ 1) for i in range(size)]

    def pairs(self, step, low, high):
        return [
            (2 * z + c, 2 * (z + step) + c)
            for z in range(low, high)
            for c in range(2)
            if 0 <= z + step < self.chips
        ]

    def right(self, block, low, high):
        return lax.ppermute(block, "ctx", self.pairs(1, low, high))

    def left(self, block, low, high):
        n = self.chips
        return lax.ppermute(block, "ctx", self.pairs(-1, n - high, n - low))

    def swap(self, block):
        return lax.ppermute(block, "ctx", self.core_pairs)

    def exchange(self, own=None, parts=None):
        n, z = self.chips, self.z
        mirror = n - 1 - z
        gathers, sums = own is not None, parts is not None
        from_left, from_right = [own], [own]
        sum_left = sum_right = None
        lag = 1 if gathers else 0
        last = n if gathers and sums else n - 1
        for s in range(1, last + 1):
            to_right = to_left = None
            low, high = 0, n
            if gathers and s <= n - 1:
                to_right, to_left = from_left[s - 1], from_right[s - 1]
                low = s - 1
            j = s - lag
            if sums and j >= 1:
                sum_r, sum_l = parts[n - j], parts[j]
                if sum_left is not None:
                    sum_r = (sum_r.astype(f32) + sum_left.astype(f32)).astype(bf16)
                    sum_l = (sum_l.astype(f32) + sum_right.astype(f32)).astype(bf16)
                if to_right is None:
                    to_right, to_left, high = sum_r, sum_l, j
                else:
                    to_right = jnp.where(z >= s - 1, to_right, sum_r)
                    to_left = jnp.where(mirror >= s - 1, to_left, sum_l)
                    low = 0
            got_left = self.right(to_right, low, high)
            got_right = self.left(to_left, low, high)
            if gathers and s <= n - 1:
                from_left.append(got_left)
                from_right.append(got_right)
            if sums and j >= 1:
                sum_left, sum_right = got_left, got_right
        blocks = None
        if gathers:
            blocks = [own]
            for k in range(1, n):
                blocks.append(jnp.where(z + k < n, from_right[k], from_left[n - k]))
        terms = None
        if sums:
            terms = (parts[0], sum_left, sum_right)
        return blocks, terms


def total(terms):
    return sum(t.astype(f32) for t in terms[1:]) + terms[0].astype(f32)


def spans_of(place, info, spans, none):
    label = jnp.full(place.shape, none, jnp.int32)
    for s in range(spans):
        start, stop = info[2 + s], info[2 + spans + s]
        label = jnp.where((place >= start) & (place < stop), s, label)
    return label


def seen_block(query_block, key_block, width, info, spans):
    seen = key_block <= query_block
    for s in range(spans):
        start, stop = info[2 + s], info[2 + spans + s]
        seen = seen | ((start < (query_block + 1) * width) & (stop > key_block * width))
    return seen


def block_mask(query_block, key_block, rows, info, spans):
    c = info[1]
    width = 2 * rows
    query_place = (
        query_block * width + c * rows + lax.broadcasted_iota(jnp.int32, (rows, 1), 0)
    )
    j = lax.broadcasted_iota(jnp.int32, (1, width), 1)
    key_place = key_block * width + j + jnp.where(j < rows, c * rows, -c * rows)
    query_span = spans_of(query_place, info, spans, -2)
    key_span = spans_of(key_place, info, spans, -1)
    return (key_place <= query_place) | (key_span == query_span)


def forward_kernel(spans, heads, info, q_ref, k_ref, v_ref, o_ref, acc_ref, sum_ref):
    chips, width, _ = k_ref.shape
    rows = width // 2
    query_block = lax.rem(info[0] + pl.program_id(0), chips)
    acc_ref[...] = jnp.zeros_like(acc_ref)
    sum_ref[...] = jnp.zeros_like(sum_ref)
    for kk in range(chips):
        key_block = lax.rem(info[0] + kk, chips)

        @pl.when(seen_block(query_block, key_block, width, info, spans))
        def _():
            allowed = block_mask(query_block, key_block, rows, info, spans)
            keys, values = k_ref[kk], v_ref[kk]
            for h in range(heads):
                scores = nt(q_ref[0, :, h * HEAD_DIM : (h + 1) * HEAD_DIM], keys)
                weights = jnp.where(
                    allowed, jnp.exp(soft_cap * jnp.tanh(scores * (1.0 / soft_cap))), 0.0
                )
                sum_ref[h] += jnp.sum(weights, axis=1, keepdims=True)
                acc_ref[h] += nn(weights.astype(bf16), values)

    for h in range(heads):
        o_ref[0, :, h * HEAD_DIM : (h + 1) * HEAD_DIM] = (acc_ref[h] / sum_ref[h]).astype(bf16)


def backward_kernel(
    spans,
    heads,
    info,
    q_ref,
    k_ref,
    v_ref,
    g_ref,
    dq_ref,
    dk_ref,
    dv_ref,
    p_ref,
    r_ref,
    t_ref,
    sum_ref,
    inner_ref,
    acc_ref,
):
    chips, width, _ = k_ref.shape
    rows = width // 2
    query_block = lax.rem(info[0] + pl.program_id(0), chips)

    @pl.when(pl.program_id(0) == 0)
    def _():
        dk_ref[...] = jnp.zeros_like(dk_ref)
        dv_ref[...] = jnp.zeros_like(dv_ref)

    acc_ref[...] = jnp.zeros_like(acc_ref)
    sum_ref[...] = jnp.zeros_like(sum_ref)
    inner_ref[...] = jnp.zeros_like(inner_ref)
    for kk in range(chips):
        key_block = lax.rem(info[0] + kk, chips)

        @pl.when(seen_block(query_block, key_block, width, info, spans))
        def _():
            allowed = block_mask(query_block, key_block, rows, info, spans)
            keys, values = k_ref[kk], v_ref[kk]
            for h in range(heads):
                head = slice(h * HEAD_DIM, (h + 1) * HEAD_DIM)
                squashed = jnp.tanh(nt(q_ref[0, :, head], keys) * (1.0 / soft_cap))
                weights = jnp.where(allowed, jnp.exp(soft_cap * squashed), 0.0)
                row_grad = nt(g_ref[0, :, head], values)
                sum_ref[h] += jnp.sum(weights, axis=1, keepdims=True)
                inner_ref[h] += jnp.sum(weights * row_grad, axis=1, keepdims=True)
                p_ref[kk, h] = weights
                r_ref[kk, h] = row_grad
                t_ref[kk, h] = 1.0 - squashed * squashed

    for kk in range(chips):
        key_block = lax.rem(info[0] + kk, chips)

        @pl.when(seen_block(query_block, key_block, width, info, spans))
        def _():
            keys = k_ref[kk]
            for h in range(heads):
                head = slice(h * HEAD_DIM, (h + 1) * HEAD_DIM)
                inverse = 1.0 / sum_ref[h]
                weights = p_ref[kk, h] * inverse
                inner = inner_ref[h] * inverse
                score_grad = (weights * (r_ref[kk, h] - inner) * t_ref[kk, h]).astype(bf16)
                acc_ref[h] += nn(score_grad, keys)
                dk_ref[kk] += tn(score_grad, q_ref[0, :, head])
                dv_ref[kk] += tn(weights.astype(bf16), g_ref[0, :, head])

    for h in range(heads):
        dq_ref[0, :, h * HEAD_DIM : (h + 1) * HEAD_DIM] = acc_ref[h]


def block_spec(shape):
    return pl.BlockSpec((1,) + tuple(shape[1:]), lambda i, info: (i, 0, 0))


def whole_spec(shape):
    return pl.BlockSpec(tuple(shape), lambda i, info: (0,) * len(shape))


def attend_forward(info, queries, keys, values, spans):
    chips, rows, features = queries.shape
    heads = features // HEAD_DIM
    flops = 4 * chips * rows * heads * chips * 2 * rows * HEAD_DIM
    return pl.pallas_call(
        functools.partial(forward_kernel, spans, heads),
        out_shape=jax.ShapeDtypeStruct(queries.shape, bf16),
        grid_spec=pltpu.PrefetchScalarGridSpec(
            num_scalar_prefetch=1,
            grid=(chips,),
            in_specs=[block_spec(queries.shape), whole_spec(keys.shape), whole_spec(values.shape)],
            out_specs=block_spec(queries.shape),
            scratch_shapes=[
                pltpu.VMEM((heads, rows, HEAD_DIM), f32),
                pltpu.VMEM((heads, rows, 1), f32),
            ],
        ),
        compiler_params=pltpu.CompilerParams(vmem_limit_bytes=32 * 1024 * 1024),
        cost_estimate=pl.CostEstimate(
            flops=flops, bytes_accessed=6 * 1024 * 1024, transcendentals=flops // 512
        ),
    )(info, queries, keys, values)


def attend_backward(info, queries, keys, values, grads, spans):
    chips, rows, features = queries.shape
    heads = features // HEAD_DIM
    flops = 10 * chips * rows * heads * chips * 2 * rows * HEAD_DIM
    square = pltpu.VMEM((chips, heads, rows, 2 * rows), f32)
    return pl.pallas_call(
        functools.partial(backward_kernel, spans, heads),
        out_shape=(
            jax.ShapeDtypeStruct(queries.shape, f32),
            jax.ShapeDtypeStruct(keys.shape, f32),
            jax.ShapeDtypeStruct(values.shape, f32),
        ),
        grid_spec=pltpu.PrefetchScalarGridSpec(
            num_scalar_prefetch=1,
            grid=(chips,),
            in_specs=[
                block_spec(queries.shape),
                whole_spec(keys.shape),
                whole_spec(values.shape),
                block_spec(queries.shape),
            ],
            out_specs=(
                block_spec(queries.shape),
                whole_spec(keys.shape),
                whole_spec(values.shape),
            ),
            scratch_shapes=[
                square,
                square,
                square,
                pltpu.VMEM((heads, rows, 1), f32),
                pltpu.VMEM((heads, rows, 1), f32),
                pltpu.VMEM((heads, rows, HEAD_DIM), f32),
            ],
        ),
        compiler_params=pltpu.CompilerParams(vmem_limit_bytes=40 * 1024 * 1024),
        cost_estimate=pl.CostEstimate(
            flops=flops, bytes_accessed=12 * 1024 * 1024, transcendentals=flops // 1280
        ),
    )(info, queries, keys, values, grads)


def rotate(vectors, cosine, sine):
    first, second = vectors[..., :HALF], vectors[..., HALF:]
    return jnp.concatenate(
        [first * cosine - second * sine, second * cosine + first * sine], axis=-1
    )


def inverse_root(values):
    return lax.rsqrt(jnp.mean(values * values, axis=-1, keepdims=True) + epsilon)


def norm_backward(normed, root, gain, grad):
    scaled = grad * gain
    return root * (scaled - normed * jnp.mean(scaled * normed, axis=-1, keepdims=True))


def on_device(
    tokens,
    span_start,
    span_len,
    query_weight,
    key_weight,
    value_weight,
    output_weight,
    gate_weight,
    up_weight,
    down_weight,
    inbound_gain,
    attended_gain,
    prefeed_gain,
    postfeed_gain,
    cotangent,
):
    seq_count, rows, width = tokens.shape
    size = lax.axis_size("ctx")
    index = lax.axis_index("ctx")
    line = Line(size, index)
    chips, z, c = line.chips, line.z, line.c
    spans = span_start.shape[1]
    group = size // KV_HEADS
    member = index % group
    every = chips * rows

    def pair_rows(block):
        other = line.swap(block)
        return jnp.concatenate([jnp.where(c == 0, block, other), jnp.where(c == 0, other, block)])

    def shifted(block, k):
        pairs = [(i, i - i % group + (i % group + k) % group) for i in range(size)]
        return lax.ppermute(block, "ctx", pairs)

    def group_rows(block):
        if group == 2:
            return pair_rows(block)
        count = block.shape[0]
        out = jnp.zeros((group * count, width), block.dtype)
        out = lax.dynamic_update_slice(out, block, (member * count, 0))
        for k in range(1, group):
            place = lax.rem(member + group - k, group) * count
            out = lax.dynamic_update_slice(out, shifted(block, k), (place, 0))
        return out

    def group_sum(grad):
        count = grad.shape[0] // group
        own = lax.dynamic_slice(grad, (member * count, 0), (count, width))
        for k in range(1, group):
            place = lax.rem(member + k, group) * count
            sent = lax.dynamic_slice(grad, (place, 0), (count, width))
            own = own + shifted(sent.astype(bf16), k).astype(f32)
        return own

    def pair_sum(grad):
        count = grad.shape[0] // 2
        own = lax.dynamic_slice(grad, (c * count, 0), (count, width))
        sent = lax.dynamic_slice(grad, ((1 - c) * count, 0), (count, width))
        return own + line.swap(sent.astype(bf16)).astype(f32)

    gains_own = jnp.stack([inbound_gain, attended_gain, prefeed_gain, postfeed_gain])
    gains = lax.all_gather(gains_own, "ctx", axis=1, tiled=True).astype(f32)
    inbound, attended_g, prefeed, postfeed = (gains[i][None, :] for i in range(4))

    qkv_weight = jnp.concatenate(
        [pair_rows(query_weight), group_rows(key_weight), group_rows(value_weight)]
    )
    out_weight = pair_rows(output_weight)
    gate_rows = (gate_weight, line.swap(gate_weight))
    up_rows = (up_weight, line.swap(up_weight))
    down_rows = (down_weight, line.swap(down_weight))

    query_width = out_weight.shape[0]
    heads = query_width // HEAD_DIM

    block_of = lax.rem(z + jnp.arange(chips, dtype=jnp.int32), chips)
    places = (
        block_of[:, None] * (2 * rows) + c * rows + jnp.arange(rows, dtype=jnp.int32)[None, :]
    ).reshape(every)
    inverse = rope_base ** (-(jnp.arange(HALF, dtype=f32) * 2.0 / HEAD_DIM))
    angles = places.astype(f32)[:, None] * inverse[None, :]
    cosine, sine = jnp.cos(angles)[:, None, :], jnp.sin(angles)[:, None, :]
    query_scale = HEAD_DIM ** (-0.5)

    def split(block_rows):
        return [block_rows[k * rows : (k + 1) * rows] for k in range(chips)]

    def join(blocks):
        return jnp.concatenate(blocks)

    infos = [
        jnp.concatenate(
            [jnp.stack([z, c]), span_start[s], span_start[s] + span_len[s]]
        ).astype(jnp.int32)
        for s in range(seq_count)
    ]

    class Sequence:
        def __init__(self, s):
            self.s = s
            self.own = tokens[s]

        def attention(self, blocks):
            self.tokens = join(blocks)
            values = self.tokens.astype(f32)
            self.root_in = inverse_root(values)
            self.hidden = (values * self.root_in * inbound).astype(bf16)
            raw = nt(self.hidden, qkv_weight)
            queries = raw[:, :query_width].reshape(every, heads, HEAD_DIM)
            queries = (rotate(queries, cosine, sine) * query_scale).astype(bf16)
            keys = raw[:, query_width : query_width + HEAD_DIM].reshape(every, 1, HEAD_DIM)
            keys = rotate(keys, cosine, sine).astype(bf16).reshape(every, HEAD_DIM)
            values = raw[:, query_width + HEAD_DIM :].astype(bf16)
            mine = jnp.concatenate([keys, values], axis=1).reshape(chips, rows, 2 * HEAD_DIM)
            both = jnp.concatenate([mine, line.swap(mine)], axis=1)
            self.queries = queries.reshape(chips, rows, query_width)
            self.keys, self.values = both[:, :, :HEAD_DIM], both[:, :, HEAD_DIM:]
            self.attended = attend_forward(
                infos[self.s], self.queries, self.keys, self.values, spans
            ).reshape(every, query_width)
            return split(nn(self.attended, out_weight).astype(bf16))

        def after_branch(self, terms):
            branch = total(terms)
            self.root_branch = inverse_root(branch)
            self.normed_branch = branch * self.root_branch
            self.middle = self.own.astype(f32) + self.normed_branch * attended_g
            self.root_middle = inverse_root(self.middle)
            return (self.middle * self.root_middle * prefeed).astype(bf16)

        def feed(self, blocks):
            self.hidden_ff = join(blocks)
            self.product, self.slope, self.gelu = [], [], []
            out = None
            for gate_w, up_w, down_w in zip(gate_rows, up_rows, down_rows):
                gate = nt(self.hidden_ff, gate_w)
                up = nt(self.hidden_ff, up_w)
                tanh = jnp.tanh(gelu_a * (gate + gelu_b * gate * gate * gate))
                half = 0.5 * (1.0 + tanh)
                gelu = gate * half
                slope = half + 0.5 * gate * (1.0 - tanh * tanh) * (
                    gelu_a * (1.0 + 3.0 * gelu_b * gate * gate)
                )
                self.product.append((gelu * up).astype(bf16))
                self.gelu.append(gelu.astype(bf16))
                self.slope.append((up * slope).astype(bf16))
            out = sum(nn(p, w) for p, w in zip(self.product, down_rows))
            return split(out.astype(bf16))

        def after_feed(self, terms):
            feed = total(terms)
            root = inverse_root(feed)
            normed = feed * root
            self.upstream = cotangent[self.s].astype(f32)
            self.output = (self.middle + normed * postfeed).astype(bf16)
            self.postfeed_term = jnp.sum(self.upstream * normed, axis=0)
            return norm_backward(normed, root, postfeed, self.upstream).astype(bf16)

        def feed_back(self, blocks):
            self.feed_low = join(blocks)
            self.gate_back, self.up_back = [], []
            for down_w, gelu, slope in zip(down_rows, self.gelu, self.slope):
                grad = nt(self.feed_low, down_w)
                self.gate_back.append((grad * slope.astype(f32)).astype(bf16))
                self.up_back.append((grad * gelu.astype(f32)).astype(bf16))
            out = sum(
                nn(g, w)
                for g, w in zip(self.gate_back + self.up_back, list(gate_rows) + list(up_rows))
            )
            return split(out.astype(bf16))

        def after_feed_back(self, terms):
            grad = total(terms)
            normed = self.middle * self.root_middle
            self.prefeed_term = jnp.sum(grad * normed, axis=0)
            self.middle_grad = self.upstream + norm_backward(
                normed, self.root_middle, prefeed, grad
            )
            self.attended_term = jnp.sum(self.middle_grad * self.normed_branch, axis=0)
            return norm_backward(
                self.normed_branch, self.root_branch, attended_g, self.middle_grad
            ).astype(bf16)

        def attention_back(self, blocks):
            self.branch_low = join(blocks)
            mixed = nt(self.branch_low, out_weight).astype(bf16)
            query_rot, key_rot, value_sum = attend_backward(
                infos[self.s],
                self.queries,
                self.keys,
                self.values,
                mixed.reshape(chips, rows, query_width),
                spans,
            )
            sums = jnp.concatenate([key_rot, value_sum], axis=2)
            sums = sums[:, :rows] + line.swap(sums[:, rows:].astype(bf16)).astype(f32)
            sums = sums.reshape(every, 2 * HEAD_DIM)
            query_rot = query_rot.reshape(every, heads, HEAD_DIM)
            query_back = (rotate(query_rot, cosine, -sine) * query_scale).astype(bf16)
            key_back = rotate(sums[:, :HEAD_DIM].reshape(every, 1, HEAD_DIM), cosine, -sine)
            self.back = jnp.concatenate(
                [
                    query_back.reshape(every, query_width),
                    key_back.reshape(every, HEAD_DIM).astype(bf16),
                    sums[:, HEAD_DIM:].astype(bf16),
                ],
                axis=1,
            )
            grad = nn(self.back, qkv_weight)
            self.inbound_term = jnp.sum(grad * (self.tokens.astype(f32) * self.root_in), axis=0)
            return split(grad.astype(bf16))

        def after_attention_back(self, terms):
            grad = total(terms)
            values = self.own.astype(f32)
            root = inverse_root(values)
            return (self.middle_grad + norm_backward(values * root, root, inbound, grad)).astype(
                bf16
            )

    a, b = (Sequence(s) for s in range(seq_count))

    blocks, _ = line.exchange(own=a.own)
    parts_a = a.attention(blocks)
    blocks, terms = line.exchange(own=b.own, parts=parts_a)
    hidden_a = a.after_branch(terms)
    parts_b = b.attention(blocks)
    blocks, terms = line.exchange(own=hidden_a, parts=parts_b)
    hidden_b = b.after_branch(terms)
    parts_a = a.feed(blocks)
    blocks, terms = line.exchange(own=hidden_b, parts=parts_a)
    low_a = a.after_feed(terms)
    parts_b = b.feed(blocks)
    blocks, terms = line.exchange(own=low_a, parts=parts_b)
    low_b = b.after_feed(terms)
    parts_a = a.feed_back(blocks)
    blocks, terms = line.exchange(own=low_b, parts=parts_a)
    branch_a = a.after_feed_back(terms)
    parts_b = b.feed_back(blocks)
    blocks, terms = line.exchange(own=branch_a, parts=parts_b)
    branch_b = b.after_feed_back(terms)
    parts_a = a.attention_back(blocks)
    blocks, terms = line.exchange(own=branch_b, parts=parts_a)
    tokens_grad_a = a.after_attention_back(terms)
    parts_b = b.attention_back(blocks)
    _, terms = line.exchange(parts=parts_b)
    tokens_grad_b = b.after_attention_back(terms)

    def feed_grad(left_name, right_name):
        halves = []
        right = join([getattr(s, right_name) for s in (a, b)])
        for i in range(2):
            left = join([getattr(s, left_name)[i] for s in (a, b)])
            halves.append(tn(left, right))
        return halves[0] + line.swap(halves[1].astype(bf16)).astype(f32)

    down_grad = feed_grad("product", "feed_low")
    gate_grad = feed_grad("gate_back", "hidden_ff")
    up_grad = feed_grad("up_back", "hidden_ff")
    feed_sums = lax.psum((down_grad.astype(bf16), gate_grad.astype(bf16), up_grad.astype(bf16)), "dp")
    output_grad = pair_sum(
        tn(join([a.attended, b.attended]), join([a.branch_low, b.branch_low]))
    ).astype(bf16)
    qkv_grad = tn(join([a.back, b.back]), join([a.hidden, b.hidden]))
    query_grad = pair_sum(qkv_grad[:query_width]).astype(bf16)
    key_grad = group_sum(qkv_grad[query_width : query_width + HEAD_DIM]).astype(bf16)
    value_grad = group_sum(qkv_grad[query_width + HEAD_DIM :]).astype(bf16)
    feed_sums, late = lax.optimization_barrier(
        (feed_sums, (query_grad, key_grad, value_grad, output_grad))
    )
    late_sums = lax.psum(late, "dp")

    gain_terms = jnp.stack(
        [
            a.inbound_term + b.inbound_term,
            a.attended_term + b.attended_term,
            a.prefeed_term + b.prefeed_term,
            a.postfeed_term + b.postfeed_term,
        ]
    )
    gain_sums = lax.psum(gain_terms, ("dp", "ctx"))
    count = inbound_gain.shape[0]
    gain_sums = lax.dynamic_slice(gain_sums, (0, index * count), (4, count))

    return (
        jnp.stack([a.output, b.output]),
        jnp.stack([tokens_grad_a, tokens_grad_b]),
        late_sums[0].astype(f32),
        late_sums[1].astype(f32),
        late_sums[2].astype(f32),
        late_sums[3].astype(f32),
        feed_sums[1].astype(f32),
        feed_sums[2].astype(f32),
        feed_sums[0].astype(f32),
        gain_sums[0],
        gain_sums[1],
        gain_sums[2],
        gain_sums[3],
    )


def solution(mesh):
    rows = P("ctx", None)
    gain = P("ctx")
    tokens = P("dp", "ctx", None)
    spans = P("dp", None)
    return jax.shard_map(
        on_device,
        mesh=mesh,
        in_specs=(tokens, spans, spans) + (rows,) * 7 + (gain,) * 4 + (tokens,),
        out_specs=(tokens, tokens) + (rows,) * 7 + (gain,) * 4,
        check_vma=False,
    )
```

```python
import functools

import jax
import jax.numpy as jnp
from jax import lax
from jax.experimental import pallas as pl
from jax.experimental.pallas import tpu as pltpu
from jax.sharding import PartitionSpec as P

HEADS = 8
KV_HEADS = 4
HEAD_DIM = 256
HALF = HEAD_DIM // 2

epsilon = 1e-06
soft_cap = 50.0
rope_base = 10000.0
gelu_a = 0.7978845608028654
gelu_b = 0.044715

bf16 = jnp.bfloat16
f32 = jnp.float32


def nt(left_side, right_side):
    return lax.dot_general(
        left_side, right_side, (((1,), (1,)), ((), ())), preferred_element_type=f32
    )


def nn(left_side, right_side):
    return lax.dot_general(
        left_side, right_side, (((1,), (0,)), ((), ())), preferred_element_type=f32
    )


def tn(left_side, right_side):
    return lax.dot_general(
        left_side, right_side, (((0,), (0,)), ((), ())), preferred_element_type=f32
    )


class Line:
    def __init__(self, size, index):
        self.chips = size // 2
        self.z = index // 2
        self.c = index % 2
        self.core_pairs = [(i, i ^ 1) for i in range(size)]

    def pairs(self, step, low, high):
        return [
            (2 * z + c, 2 * (z + step) + c)
            for z in range(low, high)
            for c in range(2)
            if 0 <= z + step < self.chips
        ]

    def right(self, block, low, high):
        return lax.ppermute(block, "ctx", self.pairs(1, low, high))

    def left(self, block, low, high):
        n = self.chips
        return lax.ppermute(block, "ctx", self.pairs(-1, n - high, n - low))

    def swap(self, block):
        return lax.ppermute(block, "ctx", self.core_pairs)

    def shift(self, block, k):
        return jnp.roll(block, k, axis=0)


def tied(*values):
    return lax.optimization_barrier(values)


class Exchange:
    def __init__(self, line, own=None, sums=True):
        self.line, self.own, self.sums = line, own, sums
        self.parts = None
        self.s = 0
        self.from_left, self.from_right = [own], [own]
        self.sum_left = self.sum_right = None

    def step(self, work=None, inputs=()):
        line, n, z = self.line, self.line.chips, self.line.z
        gathers = self.own is not None
        self.s += 1
        s = self.s
        to_right = to_left = None
        low, high = 0, n
        if gathers and s <= n - 1:
            to_right, to_left = self.from_left[s - 1], self.from_right[s - 1]
            low = s - 1
        j = s - 1 if gathers else s
        if self.sums and j >= 1:
            sum_r, sum_l = self.parts[n - j], self.parts[j]
            if self.sum_left is not None:
                sum_r = (sum_r.astype(f32) + self.sum_left.astype(f32)).astype(bf16)
                sum_l = (sum_l.astype(f32) + self.sum_right.astype(f32)).astype(bf16)
            if to_right is None:
                to_right, to_left, high = sum_r, sum_l, j
            else:
                to_right = jnp.where(z >= s - 1, to_right, sum_r)
                to_left = jnp.where(n - 1 - z >= s - 1, to_left, sum_l)
                low = 0
        to_right, to_left, inputs = tied(to_right, to_left, inputs)
        got_left = line.right(to_right, low, high)
        got_right = line.left(to_left, low, high)
        outs = work(*inputs) if work is not None else ()
        got_left, got_right, outs = tied(got_left, got_right, outs)
        if gathers and s <= n - 1:
            self.from_left.append(got_left)
            self.from_right.append(got_right)
        if self.sums and j >= 1:
            self.sum_left, self.sum_right = got_left, got_right
        return outs

    def blocks(self):
        n, z = self.line.chips, self.line.z
        return [self.own] + [
            jnp.where(z + k < n, self.from_right[k], self.from_left[n - k]) for k in range(1, n)
        ]

    def terms(self):
        return (self.parts[0], self.sum_left, self.sum_right)


def total(terms):
    return sum(t.astype(f32) for t in terms)


def spans_of(place, info, spans, none):
    label = jnp.full(place.shape, none, jnp.int32)
    for s in range(spans):
        start, stop = info[2 + s], info[2 + spans + s]
        label = jnp.where((place >= start) & (place < stop), s, label)
    return label


def seen_block(query_block, key_block, width, info, spans):
    seen = key_block <= query_block
    for s in range(spans):
        start, stop = info[2 + s], info[2 + spans + s]
        seen = seen | ((start < (query_block + 1) * width) & (stop > key_block * width))
    return seen


def block_mask(query_block, key_block, rows, info, spans):
    c = info[1]
    width = 2 * rows
    query_place = (
        query_block * width + c * rows + lax.broadcasted_iota(jnp.int32, (rows, 1), 0)
    )
    j = lax.broadcasted_iota(jnp.int32, (1, width), 1)
    key_place = key_block * width + j + jnp.where(j < rows, c * rows, -c * rows)
    query_span = spans_of(query_place, info, spans, -2)
    key_span = spans_of(key_place, info, spans, -1)
    return (key_place <= query_place) | (key_span == query_span)


def forward_kernel(spans, heads, info, q_ref, k_ref, v_ref, o_ref, acc_ref, sum_ref):
    chips, width, _ = k_ref.shape
    rows = width // 2
    query_block = lax.rem(info[0] + pl.program_id(0), chips)
    acc_ref[...] = jnp.zeros_like(acc_ref)
    sum_ref[...] = jnp.zeros_like(sum_ref)
    for kk in range(chips):
        key_block = lax.rem(info[0] + kk, chips)

        @pl.when(seen_block(query_block, key_block, width, info, spans))
        def _():
            allowed = block_mask(query_block, key_block, rows, info, spans)
            keys, values = k_ref[kk], v_ref[kk]
            for h in range(heads):
                scores = nt(q_ref[0, :, h * HEAD_DIM : (h + 1) * HEAD_DIM], keys)
                weights = jnp.where(
                    allowed, jnp.exp(soft_cap * jnp.tanh(scores * (1.0 / soft_cap))), 0.0
                )
                sum_ref[h] += jnp.sum(weights, axis=1, keepdims=True)
                acc_ref[h] += nn(weights.astype(bf16), values)

    for h in range(heads):
        o_ref[0, :, h * HEAD_DIM : (h + 1) * HEAD_DIM] = (acc_ref[h] / sum_ref[h]).astype(bf16)


def backward_kernel(
    spans,
    heads,
    info,
    q_ref,
    k_ref,
    v_ref,
    g_ref,
    dq_ref,
    dk_ref,
    dv_ref,
    p_ref,
    r_ref,
    t_ref,
    sum_ref,
    inner_ref,
    acc_ref,
):
    chips, width, _ = k_ref.shape
    rows = width // 2
    query_block = lax.rem(info[0] + pl.program_id(0), chips)

    @pl.when(pl.program_id(0) == 0)
    def _():
        dk_ref[...] = jnp.zeros_like(dk_ref)
        dv_ref[...] = jnp.zeros_like(dv_ref)

    acc_ref[...] = jnp.zeros_like(acc_ref)
    sum_ref[...] = jnp.zeros_like(sum_ref)
    inner_ref[...] = jnp.zeros_like(inner_ref)
    for kk in range(chips):
        key_block = lax.rem(info[0] + kk, chips)

        @pl.when(seen_block(query_block, key_block, width, info, spans))
        def _():
            allowed = block_mask(query_block, key_block, rows, info, spans)
            keys, values = k_ref[kk], v_ref[kk]
            for h in range(heads):
                head = slice(h * HEAD_DIM, (h + 1) * HEAD_DIM)
                squashed = jnp.tanh(nt(q_ref[0, :, head], keys) * (1.0 / soft_cap))
                weights = jnp.where(allowed, jnp.exp(soft_cap * squashed), 0.0)
                row_grad = nt(g_ref[0, :, head], values)
                sum_ref[h] += jnp.sum(weights, axis=1, keepdims=True)
                inner_ref[h] += jnp.sum(weights * row_grad, axis=1, keepdims=True)
                p_ref[kk, h] = weights
                r_ref[kk, h] = row_grad
                t_ref[kk, h] = 1.0 - squashed * squashed

    for kk in range(chips):
        key_block = lax.rem(info[0] + kk, chips)

        @pl.when(seen_block(query_block, key_block, width, info, spans))
        def _():
            keys = k_ref[kk]
            for h in range(heads):
                head = slice(h * HEAD_DIM, (h + 1) * HEAD_DIM)
                inverse = 1.0 / sum_ref[h]
                weights = p_ref[kk, h] * inverse
                inner = inner_ref[h] * inverse
                score_grad = (weights * (r_ref[kk, h] - inner) * t_ref[kk, h]).astype(bf16)
                acc_ref[h] += nn(score_grad, keys)
                dk_ref[kk] += tn(score_grad, q_ref[0, :, head])
                dv_ref[kk] += tn(weights.astype(bf16), g_ref[0, :, head])

    for h in range(heads):
        dq_ref[0, :, h * HEAD_DIM : (h + 1) * HEAD_DIM] = acc_ref[h]


def block_spec(shape):
    return pl.BlockSpec((1,) + tuple(shape[1:]), lambda i, info: (i, 0, 0))


def whole_spec(shape):
    return pl.BlockSpec(tuple(shape), lambda i, info: (0,) * len(shape))


def attend_forward(info, queries, keys, values, spans):
    chips, rows, features = queries.shape
    heads = features // HEAD_DIM
    flops = 4 * chips * rows * heads * chips * 2 * rows * HEAD_DIM
    return pl.pallas_call(
        functools.partial(forward_kernel, spans, heads),
        out_shape=jax.ShapeDtypeStruct(queries.shape, bf16),
        grid_spec=pltpu.PrefetchScalarGridSpec(
            num_scalar_prefetch=1,
            grid=(chips,),
            in_specs=[block_spec(queries.shape), whole_spec(keys.shape), whole_spec(values.shape)],
            out_specs=block_spec(queries.shape),
            scratch_shapes=[
                pltpu.VMEM((heads, rows, HEAD_DIM), f32),
                pltpu.VMEM((heads, rows, 1), f32),
            ],
        ),
        compiler_params=pltpu.CompilerParams(vmem_limit_bytes=32 * 1024 * 1024),
        cost_estimate=pl.CostEstimate(
            flops=flops, bytes_accessed=6 * 1024 * 1024, transcendentals=flops // 512
        ),
    )(info, queries, keys, values)


def attend_backward(info, queries, keys, values, grads, spans):
    chips, rows, features = queries.shape
    heads = features // HEAD_DIM
    flops = 10 * chips * rows * heads * chips * 2 * rows * HEAD_DIM
    square = pltpu.VMEM((chips, heads, rows, 2 * rows), f32)
    return pl.pallas_call(
        functools.partial(backward_kernel, spans, heads),
        out_shape=(
            jax.ShapeDtypeStruct(queries.shape, f32),
            jax.ShapeDtypeStruct(keys.shape, f32),
            jax.ShapeDtypeStruct(values.shape, f32),
        ),
        grid_spec=pltpu.PrefetchScalarGridSpec(
            num_scalar_prefetch=1,
            grid=(chips,),
            in_specs=[
                block_spec(queries.shape),
                whole_spec(keys.shape),
                whole_spec(values.shape),
                block_spec(queries.shape),
            ],
            out_specs=(
                block_spec(queries.shape),
                whole_spec(keys.shape),
                whole_spec(values.shape),
            ),
            scratch_shapes=[
                square,
                square,
                square,
                pltpu.VMEM((heads, rows, 1), f32),
                pltpu.VMEM((heads, rows, 1), f32),
                pltpu.VMEM((heads, rows, HEAD_DIM), f32),
            ],
        ),
        compiler_params=pltpu.CompilerParams(vmem_limit_bytes=40 * 1024 * 1024),
        cost_estimate=pl.CostEstimate(
            flops=flops, bytes_accessed=12 * 1024 * 1024, transcendentals=flops // 1280
        ),
    )(info, queries, keys, values, grads)


def gate_up_kernel(h_ref, gate_ref, up_ref, product_ref, gelu_ref, slope_ref):
    gate = nt(h_ref[...], gate_ref[...])
    up = nt(h_ref[...], up_ref[...])
    square = gate * gate
    tanh = jnp.tanh(gate * (gelu_a + (gelu_a * gelu_b) * square))
    half = 0.5 + 0.5 * tanh
    gelu = gate * half
    slope = half + gate * (0.5 - 0.5 * tanh * tanh) * (gelu_a + (3.0 * gelu_a * gelu_b) * square)
    product_ref[...] = (gelu * up).astype(bf16)
    gelu_ref[...] = gelu.astype(bf16)
    slope_ref[...] = (up * slope).astype(bf16)


def gate_up(hidden, gate_w, up_w):
    m, width = hidden.shape
    n = gate_w.shape[0]
    tile = next(t for t in (768, 384, 256, 128) if n % t == 0)
    weight_spec = pl.BlockSpec((tile, width), lambda i: (i, 0))
    out_spec = pl.BlockSpec((m, tile), lambda i: (0, i))
    return pl.pallas_call(
        gate_up_kernel,
        out_shape=(jax.ShapeDtypeStruct((m, n), bf16),) * 3,
        grid=(n // tile,),
        in_specs=[pl.BlockSpec((m, width), lambda i: (0, 0)), weight_spec, weight_spec],
        out_specs=(out_spec,) * 3,
        compiler_params=pltpu.CompilerParams(vmem_limit_bytes=56 * 1024 * 1024),
        cost_estimate=pl.CostEstimate(
            flops=4 * m * n * width,
            bytes_accessed=4 * n * width + 2 * m * width + 6 * m * n,
            transcendentals=m * n,
        ),
    )(hidden, gate_w, up_w)


def rotate(vectors, cosine, sine):
    first, second = vectors[..., :HALF], vectors[..., HALF:]
    return jnp.concatenate(
        [first * cosine - second * sine, second * cosine + first * sine], axis=-1
    )


def inverse_root(values):
    return lax.rsqrt(jnp.mean(values * values, axis=-1, keepdims=True) + epsilon)


def norm_backward(normed, root, gain, grad):
    scaled = grad * gain
    return root * (scaled - normed * jnp.mean(scaled * normed, axis=-1, keepdims=True))


def on_device(
    tokens,
    span_start,
    span_len,
    query_weight,
    key_weight,
    value_weight,
    output_weight,
    gate_weight,
    up_weight,
    down_weight,
    inbound_gain,
    attended_gain,
    prefeed_gain,
    postfeed_gain,
    cotangent,
):
    seq_count, rows, width = tokens.shape
    size = lax.axis_size("ctx")
    index = lax.axis_index("ctx")
    line = Line(size, index)
    chips, z, c = line.chips, line.z, line.c
    spans = span_start.shape[1]
    group = size // KV_HEADS
    member = index % group
    every = chips * rows

    def pair_rows(block):
        other = line.swap(block)
        return jnp.concatenate([jnp.where(c == 0, block, other), jnp.where(c == 0, other, block)])

    def shifted(block, k):
        pairs = [(i, i - i % group + (i % group + k) % group) for i in range(size)]
        return lax.ppermute(block, "ctx", pairs)

    def group_rows(block):
        if group == 2:
            return pair_rows(block)
        count = block.shape[0]
        out = jnp.zeros((group * count, width), block.dtype)
        out = lax.dynamic_update_slice(out, block, (member * count, 0))
        for k in range(1, group):
            place = lax.rem(member + group - k, group) * count
            out = lax.dynamic_update_slice(out, shifted(block, k), (place, 0))
        return out

    def group_sum(grad):
        count = grad.shape[0] // group
        own = lax.dynamic_slice(grad, (member * count, 0), (count, width)).astype(f32)
        for k in range(1, group):
            place = lax.rem(member + k, group) * count
            sent = lax.dynamic_slice(grad, (place, 0), (count, width))
            own = own + shifted(sent.astype(bf16), k).astype(f32)
        return own

    def pair_sum(grad):
        count = grad.shape[0] // 2
        own = lax.dynamic_slice(grad, (c * count, 0), (count, width)).astype(f32)
        sent = lax.dynamic_slice(grad, ((1 - c) * count, 0), (count, width))
        return own + line.swap(sent.astype(bf16)).astype(f32)

    def both_rows(block):
        return jnp.concatenate([block, line.swap(block)])

    qkv_weight = jnp.concatenate(
        [pair_rows(query_weight), group_rows(key_weight), group_rows(value_weight)]
    )
    out_weight = pair_rows(output_weight)
    gate_rows, up_rows, down_rows = map(both_rows, (gate_weight, up_weight, down_weight))

    count = inbound_gain.shape[0]
    pad = 16
    gains_own = jnp.stack([inbound_gain, attended_gain, prefeed_gain, postfeed_gain])
    gains_other = line.swap(gains_own)
    gains_row = jnp.where(
        c == 0,
        jnp.concatenate([gains_own, gains_other]),
        jnp.concatenate([gains_other, gains_own]),
    ).reshape(1, 8 * count)
    gains_rows = jnp.pad(gains_row, ((0, pad - 1), (0, width - 8 * count)))

    query_width = out_weight.shape[0]
    heads = query_width // HEAD_DIM

    block_of = lax.rem(z + jnp.arange(chips, dtype=jnp.int32), chips)
    places = (
        block_of[:, None] * (2 * rows) + c * rows + jnp.arange(rows, dtype=jnp.int32)[None, :]
    ).reshape(every)
    inverse = rope_base ** (-(jnp.arange(HALF, dtype=f32) * 2.0 / HEAD_DIM))
    angles = places.astype(f32)[:, None] * inverse[None, :]
    cosine, sine = jnp.cos(angles)[:, None, :], jnp.sin(angles)[:, None, :]
    query_scale = HEAD_DIM ** (-0.5)

    def split(block_rows):
        return [block_rows[k * rows : (k + 1) * rows] for k in range(chips)]

    def join(blocks):
        return jnp.concatenate(blocks)

    infos = [
        jnp.concatenate(
            [jnp.stack([z, c]), span_start[s], span_start[s] + span_len[s]]
        ).astype(jnp.int32)
        for s in range(seq_count)
    ]

    class Sequence:
        def __init__(self, s):
            self.s = s
            self.own = tokens[s]

        def project(self, *blocks):
            merged = join(blocks)
            values = merged.astype(f32)
            root_in = inverse_root(values)
            hidden = (values * root_in * gain[0]).astype(bf16)
            raw = nt(hidden, qkv_weight)
            queries = raw[:, :query_width].reshape(every, heads, HEAD_DIM)
            queries = (rotate(queries, cosine, sine) * query_scale).astype(bf16)
            keys = raw[:, query_width : query_width + HEAD_DIM].reshape(every, 1, HEAD_DIM)
            keys = rotate(keys, cosine, sine).astype(bf16).reshape(every, HEAD_DIM)
            values = raw[:, query_width + HEAD_DIM :].astype(bf16)
            mine = jnp.concatenate([keys, values], axis=1).reshape(chips, rows, 2 * HEAD_DIM)
            both = jnp.concatenate([mine, line.swap(mine)], axis=1)
            queries = queries.reshape(chips, rows, query_width)
            return merged, root_in, hidden, queries, both[:, :, :HEAD_DIM], both[:, :, HEAD_DIM:]

        def attend(self, queries, keys, values):
            attended = attend_forward(infos[self.s], queries, keys, values, spans)
            attended = attended.reshape(every, query_width)
            return attended, nn(attended, out_weight).astype(bf16)

        def after_branch(self, terms):
            branch = total(terms)
            self.root_branch = inverse_root(branch)
            self.normed_branch = branch * self.root_branch
            self.middle = self.own.astype(f32) + self.normed_branch * gain[1]
            self.root_middle = inverse_root(self.middle)
            return (self.middle * self.root_middle * gain[2]).astype(bf16)

        def feed(self, *blocks):
            hidden_ff = join(blocks)
            return (hidden_ff,) + tuple(gate_up(hidden_ff, gate_rows, up_rows))

        def feed_down(self, product):
            return nn(product, down_rows).astype(bf16)

        def after_feed(self, terms):
            feed = total(terms)
            root = inverse_root(feed)
            normed = feed * root
            self.upstream = cotangent[self.s].astype(f32)
            self.output = (self.middle + normed * gain[3]).astype(bf16)
            self.postfeed_term = jnp.sum(self.upstream * normed, axis=0)
            return norm_backward(normed, root, gain[3], self.upstream).astype(bf16)

        def feed_back(self, feed_low, gelu, slope):
            grad = nt(feed_low, down_rows)
            return (grad * slope.astype(f32)).astype(bf16), (grad * gelu.astype(f32)).astype(bf16)

        def feed_in(self, gate_back, up_back):
            return (nn(gate_back, gate_rows) + nn(up_back, up_rows)).astype(bf16)

        def after_feed_back(self, terms):
            grad = total(terms)
            normed = self.middle * self.root_middle
            self.prefeed_term = jnp.sum(grad * normed, axis=0)
            self.middle_grad = self.upstream + norm_backward(
                normed, self.root_middle, gain[2], grad
            )
            self.attended_term = jnp.sum(self.middle_grad * self.normed_branch, axis=0)
            return norm_backward(
                self.normed_branch, self.root_branch, gain[1], self.middle_grad
            ).astype(bf16)

        def attend_back(self, branch_low, queries, keys, values):
            mixed = nt(branch_low, out_weight).astype(bf16)
            query_rot, key_rot, value_sum = attend_backward(
                infos[self.s],
                queries,
                keys,
                values,
                mixed.reshape(chips, rows, query_width),
                spans,
            )
            sums = jnp.concatenate([key_rot, value_sum], axis=2)
            sums = sums[:, :rows] + line.swap(sums[:, rows:].astype(bf16)).astype(f32)
            sums = sums.reshape(every, 2 * HEAD_DIM)
            query_rot = query_rot.reshape(every, heads, HEAD_DIM)
            query_back = (rotate(query_rot, cosine, -sine) * query_scale).astype(bf16)
            key_back = rotate(sums[:, :HEAD_DIM].reshape(every, 1, HEAD_DIM), cosine, -sine)
            return jnp.concatenate(
                [
                    query_back.reshape(every, query_width),
                    key_back.reshape(every, HEAD_DIM).astype(bf16),
                    sums[:, HEAD_DIM:].astype(bf16),
                ],
                axis=1,
            )

        def project_back(self, back, merged, root_in):
            grad = nn(back, qkv_weight)
            inbound_term = jnp.sum(grad * (merged.astype(f32) * root_in), axis=0)
            return grad.astype(bf16), inbound_term

        def after_project_back(self, terms):
            grad = total(terms)
            values = self.own.astype(f32)
            root = inverse_root(values)
            return (self.middle_grad + norm_backward(values * root, root, gain[0], grad)).astype(
                bf16
            )

    def weight_grad(left_a, left_b, right_a, right_b):
        return tn(join([left_a, left_b]), join([right_a, right_b])).astype(bf16)

    def group_of(own, first, first_inputs, middle, last):
        ex = Exchange(line, own)
        firsts = ex.step(first, first_inputs)
        ex.parts = split(firsts[0])
        middles = []
        for i in range(chips - 2):
            middles.append(ex.step(*(middle[i] if i < len(middle) else ())))
        lasts = ex.step(*last(ex.blocks()))
        return firsts, middles, lasts, ex.terms()

    data = lax.axis_size("dp")

    def data_sum(values, order):
        groups = [[(i + order) % data for i in range(data)]]
        return lax.psum(values, "dp", axis_index_groups=groups)

    def core_sum(grad):
        count = grad.shape[0] // 2
        return (grad[:count].astype(f32) + line.swap(grad[count:]).astype(f32)).astype(bf16)

    a, b = (Sequence(s) for s in range(seq_count))

    ex = Exchange(line, jnp.concatenate([a.own, gains_rows]), sums=False)
    for _ in range(chips - 1):
        ex.step()
    blocks = ex.blocks()
    gain = jnp.stack([block[rows, : 8 * count] for block in blocks])
    gain = line.shift(gain, z).reshape(chips, 2, 4, count)
    gain = gain.transpose(2, 0, 1, 3).reshape(4, 1, width).astype(f32)

    def a_attention(*blocks):
        projected = a.project(*blocks)
        attended, out = a.attend(*projected[3:])
        return (out, attended) + projected

    firsts, _, lasts, terms = group_of(
        b.own,
        a_attention,
        [block[:rows] for block in blocks],
        [],
        lambda blocks: (b.project, blocks),
    )
    _, a.attended, a.tokens, a.root_in, a.hidden, a.queries, a.keys, a.values = firsts
    b.tokens, b.root_in, b.hidden, b.queries, b.keys, b.values = lasts
    hidden_a = a.after_branch(terms)

    def b_attention(*projected):
        attended, out = b.attend(*projected)
        return out, attended

    firsts, _, lasts, terms = group_of(
        hidden_a,
        b_attention,
        (b.queries, b.keys, b.values),
        [],
        lambda blocks: (a.feed, blocks),
    )
    b.attended = firsts[1]
    a.hidden_ff, a.product, a.gelu, a.slope = lasts
    hidden_b = b.after_branch(terms)

    firsts, _, lasts, terms = group_of(
        hidden_b,
        lambda product: (a.feed_down(product),),
        (a.product,),
        [],
        lambda blocks: (b.feed, blocks),
    )
    b.hidden_ff, b.product, b.gelu, b.slope = lasts
    low_a = a.after_feed(terms)

    def a_feed_back(*blocks):
        feed_low = join(blocks)
        return (feed_low,) + a.feed_back(feed_low, a.gelu, a.slope)

    firsts, _, lasts, terms = group_of(
        low_a,
        lambda product: (b.feed_down(product),),
        (b.product,),
        [],
        lambda blocks: (a_feed_back, blocks),
    )
    a.feed_low, a.gate_back, a.up_back = lasts
    low_b = b.after_feed(terms)

    def b_feed_back(*blocks):
        feed_low = join(blocks)
        down_grad = weight_grad(a.product, b.product, a.feed_low, feed_low)
        return (feed_low, down_grad) + b.feed_back(feed_low, b.gelu, b.slope)

    firsts, _, lasts, terms = group_of(
        low_b,
        lambda gate_back, up_back: (a.feed_in(gate_back, up_back),),
        (a.gate_back, a.up_back),
        [],
        lambda blocks: (b_feed_back, blocks),
    )
    b.feed_low, down_grad, b.gate_back, b.up_back = lasts
    down_sum = data_sum(core_sum(down_grad), 0)
    branch_a = a.after_feed_back(terms)

    def a_attention_back(*blocks):
        branch_low = join(blocks)
        return branch_low, a.attend_back(branch_low, a.queries, a.keys, a.values)

    def left_grad(left_a, left_b):
        return (weight_grad(left_a, left_b, a.hidden_ff, b.hidden_ff),)

    firsts, middles, lasts, terms = group_of(
        branch_a,
        lambda gate_back, up_back: (b.feed_in(gate_back, up_back),),
        (b.gate_back, b.up_back),
        [(left_grad, (a.gate_back, b.gate_back)), (left_grad, (a.up_back, b.up_back))],
        lambda blocks: (a_attention_back, blocks),
    )
    gate_grad, up_grad = middles[0][0], middles[1][0]
    gate_sum, up_sum = data_sum((core_sum(gate_grad), core_sum(up_grad)), 1)
    a.branch_low, a.back = lasts
    branch_b = b.after_feed_back(terms)

    def b_attention_back(*blocks):
        branch_low = join(blocks)
        return branch_low, b.attend_back(branch_low, b.queries, b.keys, b.values)

    firsts, _, lasts, terms = group_of(
        branch_b,
        a.project_back,
        (a.back, a.tokens, a.root_in),
        [],
        lambda blocks: (b_attention_back, blocks),
    )
    a.inbound_term = firsts[1]
    b.branch_low, b.back = lasts
    tokens_grad_a = a.after_project_back(terms)

    grad, b.inbound_term = b.project_back(b.back, b.tokens, b.root_in)
    gain_terms = jnp.stack(
        [
            a.inbound_term + b.inbound_term,
            a.attended_term + b.attended_term,
            a.prefeed_term + b.prefeed_term,
            a.postfeed_term + b.postfeed_term,
        ]
    ).astype(bf16)
    gain_terms = gain_terms.reshape(4, chips, 2, count).transpose(1, 2, 0, 3)
    gain_terms = line.shift(gain_terms.reshape(chips, 1, 8 * count), -z)
    gain_terms = jnp.pad(gain_terms, ((0, 0), (0, pad - 1), (0, width - 8 * count)))
    ex = Exchange(line)
    ex.parts = [jnp.concatenate([part, gain_terms[k]]) for k, part in enumerate(split(grad))]

    def attention_grads(back_a, back_b):
        qkv_grad = weight_grad(back_a, back_b, a.hidden, b.hidden)
        output_grad = weight_grad(a.attended, b.attended, a.branch_low, b.branch_low)
        return qkv_grad, output_grad

    qkv_grad, output_grad = ex.step(attention_grads, (a.back, b.back))
    for _ in range(chips - 2):
        ex.step()
    grad = total(ex.terms())
    tokens_grad_b = b.after_project_back([grad[:rows]])

    late_sums = data_sum(
        tuple(
            value.astype(bf16)
            for value in (
                pair_sum(qkv_grad[:query_width]),
                group_sum(qkv_grad[query_width : query_width + HEAD_DIM]),
                group_sum(qkv_grad[query_width + HEAD_DIM :]),
                pair_sum(output_grad),
            )
        ),
        2,
    )
    row = grad[rows, : 8 * count].reshape(2, 4, count)
    mine = jnp.where(c == 0, row[0], row[1])
    other = jnp.where(c == 0, row[1], row[0])
    gain_sums = lax.psum(mine + line.swap(other.astype(bf16)).astype(f32), "dp")

    return (
        jnp.stack([a.output, b.output]),
        jnp.stack([tokens_grad_a, tokens_grad_b]),
        late_sums[0].astype(f32),
        late_sums[1].astype(f32),
        late_sums[2].astype(f32),
        late_sums[3].astype(f32),
        gate_sum.astype(f32),
        up_sum.astype(f32),
        down_sum.astype(f32),
        gain_sums[0],
        gain_sums[1],
        gain_sums[2],
        gain_sums[3],
    )


def solution(mesh):
    rows = P("ctx", None)
    gain = P("ctx")
    tokens = P("dp", "ctx", None)
    spans = P("dp", None)
    return jax.shard_map(
        on_device,
        mesh=mesh,
        in_specs=(tokens, spans, spans) + (rows,) * 7 + (gain,) * 4 + (tokens,),
        out_specs=(tokens, tokens) + (rows,) * 7 + (gain,) * 4,
        check_vma=False,
    )
```

```python
import functools

import jax
import jax.numpy as jnp
from jax import lax
from jax.experimental import pallas as pl
from jax.experimental.pallas import tpu as pltpu
from jax.sharding import PartitionSpec as P

HEADS = 8
KV_HEADS = 4
HEAD_DIM = 256
HALF = HEAD_DIM // 2

epsilon = 1e-06
soft_cap = 50.0
rope_base = 10000.0
gelu_a = 0.7978845608028654
gelu_b = 0.044715

bf16 = jnp.bfloat16
f32 = jnp.float32


def nt(left_side, right_side):
    return lax.dot_general(
        left_side, right_side, (((1,), (1,)), ((), ())), preferred_element_type=f32
    )


def nn(left_side, right_side):
    return lax.dot_general(
        left_side, right_side, (((1,), (0,)), ((), ())), preferred_element_type=f32
    )


def tn(left_side, right_side):
    return lax.dot_general(
        left_side, right_side, (((0,), (0,)), ((), ())), preferred_element_type=f32
    )


class Line:
    def __init__(self, size, index):
        self.chips = size // 2
        self.z = index // 2
        self.c = index % 2
        self.core_pairs = [(i, i ^ 1) for i in range(size)]

    def pairs(self, step, low, high):
        return [
            (2 * z + c, 2 * (z + step) + c)
            for z in range(low, high)
            for c in range(2)
            if 0 <= z + step < self.chips
        ]

    def right(self, block, low, high):
        return lax.ppermute(block, "ctx", self.pairs(1, low, high))

    def left(self, block, low, high):
        n = self.chips
        return lax.ppermute(block, "ctx", self.pairs(-1, n - high, n - low))

    def swap(self, block):
        return lax.ppermute(block, "ctx", self.core_pairs)

    def exchanged(self, items):
        last = self.z == self.chips - 1
        items = list(items)
        first, final = items[1], items[-1]
        items[1] = jnp.where(last, final, first)
        items[-1] = jnp.where(last, first, final)
        return items

    def table(self):
        order = self.exchanged([jnp.int32(k) for k in range(self.chips)])
        return [lax.rem(self.z + k, self.chips) for k in order]


def tied(*values):
    return lax.optimization_barrier(values)


class Exchange:
    def __init__(self, line, own=None, sums=True):
        self.line, self.own, self.sums = line, own, sums
        self.parts = None
        self.s = 0
        self.from_left, self.from_right = [own], [own]
        self.sum_left = self.sum_right = None

    def step(self, work=None, inputs=(), held=()):
        line, n, z = self.line, self.line.chips, self.line.z
        gathers = self.own is not None
        self.s += 1
        s = self.s
        to_right = to_left = None
        low, high = 0, n
        if gathers and s <= n - 1:
            to_right, to_left = self.from_left[s - 1], self.from_right[s - 1]
            low = s - 1
        j = s - 1 if gathers else s
        if self.sums and j >= 1:
            sum_r, sum_l = self.parts[n - j], self.parts[n - 1 if j == 1 else j]
            if j == n - 1:
                sum_l = jnp.where(z == n - 1, self.parts[1], self.parts[n - 1])
            if self.sum_left is not None:
                sum_r = (sum_r.astype(f32) + self.sum_left.astype(f32)).astype(bf16)
                sum_l = (sum_l.astype(f32) + self.sum_right.astype(f32)).astype(bf16)
            if to_right is None:
                to_right, to_left, high = sum_r, sum_l, j
            else:
                to_right = jnp.where(z >= s - 1, to_right, sum_r)
                to_left = jnp.where(n - 1 - z >= s - 1, to_left, sum_l)
                low = 0
        to_right, to_left, inputs, self.held = tied(to_right, to_left, inputs, held)
        got_left = line.right(to_right, low, high)
        got_right = line.left(to_left, low, high)
        outs = work(*inputs) if work is not None else ()
        got_left, got_right, outs = tied(got_left, got_right, outs)
        if gathers and s <= n - 1:
            self.from_left.append(got_left)
            self.from_right.append(got_right)
        if self.sums and j >= 1:
            self.sum_left, self.sum_right = got_left, got_right
        return outs

    def near(self):
        last = self.line.z == self.line.chips - 1
        return [self.own, jnp.where(last, self.from_left[1], self.from_right[1])]

    def far(self):
        n, z = self.line.chips, self.line.z
        blocks = [
            jnp.where(z + k < n, self.from_right[k], self.from_left[n - k])
            for k in range(2, n - 1)
        ]
        final = jnp.where(z == 0, self.from_right[n - 1], self.from_left[1])
        return blocks + [jnp.where(z == n - 1, self.from_left[n - 1], final)]

    def terms(self):
        return (self.parts[0], self.sum_left, self.sum_right)


def total(terms):
    return sum(t.astype(f32) for t in terms)


def spans_of(place, info, spans, none):
    label = jnp.full(place.shape, none, jnp.int32)
    for s in range(spans):
        start, stop = info[1 + s], info[1 + spans + s]
        label = jnp.where((place >= start) & (place < stop), s, label)
    return label


def seen_block(query_block, key_block, width, info, spans):
    seen = key_block <= query_block
    for s in range(spans):
        start, stop = info[1 + s], info[1 + spans + s]
        seen = seen | ((start < (query_block + 1) * width) & (stop > key_block * width))
    return seen


def block_mask(query_block, key_block, rows, info, spans):
    c = info[0]
    width = 2 * rows
    query_place = (
        query_block * width + c * rows + lax.broadcasted_iota(jnp.int32, (rows, 1), 0)
    )
    j = lax.broadcasted_iota(jnp.int32, (1, width), 1)
    key_place = key_block * width + j + jnp.where(j < rows, c * rows, -c * rows)
    query_span = spans_of(query_place, info, spans, -2)
    key_span = spans_of(key_place, info, spans, -1)
    return (key_place <= query_place) | (key_span == query_span)


def forward_kernel(spans, heads, info, q_ref, k_ref, v_ref, o_ref, acc_ref, sum_ref):
    chips, width, _ = k_ref.shape
    rows = width // 2
    query_block = info[1 + 2 * spans + pl.program_id(0)]
    acc_ref[...] = jnp.zeros_like(acc_ref)
    sum_ref[...] = jnp.zeros_like(sum_ref)
    for kk in range(chips):
        key_block = info[1 + 2 * spans + kk]

        @pl.when(seen_block(query_block, key_block, width, info, spans))
        def _():
            allowed = block_mask(query_block, key_block, rows, info, spans)
            keys, values = k_ref[kk], v_ref[kk]
            for h in range(heads):
                scores = nt(q_ref[0, :, h * HEAD_DIM : (h + 1) * HEAD_DIM], keys)
                weights = jnp.where(
                    allowed, jnp.exp(soft_cap * jnp.tanh(scores * (1.0 / soft_cap))), 0.0
                )
                sum_ref[h] += jnp.sum(weights, axis=1, keepdims=True)
                acc_ref[h] += nn(weights.astype(bf16), values)

    for h in range(heads):
        o_ref[0, :, h * HEAD_DIM : (h + 1) * HEAD_DIM] = (acc_ref[h] / sum_ref[h]).astype(bf16)


def backward_kernel(
    spans,
    heads,
    info,
    q_ref,
    k_ref,
    v_ref,
    g_ref,
    dq_ref,
    dk_ref,
    dv_ref,
    p_ref,
    r_ref,
    t_ref,
    sum_ref,
    inner_ref,
    acc_ref,
):
    chips, width, _ = k_ref.shape
    rows = width // 2
    query_block = info[1 + 2 * spans + pl.program_id(0)]

    @pl.when(pl.program_id(0) == 0)
    def _():
        dk_ref[...] = jnp.zeros_like(dk_ref)
        dv_ref[...] = jnp.zeros_like(dv_ref)

    acc_ref[...] = jnp.zeros_like(acc_ref)
    sum_ref[...] = jnp.zeros_like(sum_ref)
    inner_ref[...] = jnp.zeros_like(inner_ref)
    for kk in range(chips):
        key_block = info[1 + 2 * spans + kk]

        @pl.when(seen_block(query_block, key_block, width, info, spans))
        def _():
            allowed = block_mask(query_block, key_block, rows, info, spans)
            keys, values = k_ref[kk], v_ref[kk]
            for h in range(heads):
                head = slice(h * HEAD_DIM, (h + 1) * HEAD_DIM)
                squashed = jnp.tanh(nt(q_ref[0, :, head], keys) * (1.0 / soft_cap))
                weights = jnp.where(allowed, jnp.exp(soft_cap * squashed), 0.0)
                row_grad = nt(g_ref[0, :, head], values)
                sum_ref[h] += jnp.sum(weights, axis=1, keepdims=True)
                inner_ref[h] += jnp.sum(weights * row_grad, axis=1, keepdims=True)
                p_ref[kk, h] = weights
                r_ref[kk, h] = row_grad
                t_ref[kk, h] = 1.0 - squashed * squashed

    for kk in range(chips):
        key_block = info[1 + 2 * spans + kk]

        @pl.when(seen_block(query_block, key_block, width, info, spans))
        def _():
            keys = k_ref[kk]
            for h in range(heads):
                head = slice(h * HEAD_DIM, (h + 1) * HEAD_DIM)
                inverse = 1.0 / sum_ref[h]
                weights = p_ref[kk, h] * inverse
                inner = inner_ref[h] * inverse
                score_grad = (weights * (r_ref[kk, h] - inner) * t_ref[kk, h]).astype(bf16)
                acc_ref[h] += nn(score_grad, keys)
                dk_ref[kk] += tn(score_grad, q_ref[0, :, head])
                dv_ref[kk] += tn(weights.astype(bf16), g_ref[0, :, head])

    for h in range(heads):
        dq_ref[0, :, h * HEAD_DIM : (h + 1) * HEAD_DIM] = acc_ref[h]


def block_spec(shape):
    return pl.BlockSpec((1,) + tuple(shape[1:]), lambda i, info: (i, 0, 0))


def whole_spec(shape):
    return pl.BlockSpec(tuple(shape), lambda i, info: (0,) * len(shape))


def attend_forward(info, queries, keys, values, spans):
    chips, rows, features = queries.shape
    heads = features // HEAD_DIM
    flops = 4 * chips * rows * heads * chips * 2 * rows * HEAD_DIM
    return pl.pallas_call(
        functools.partial(forward_kernel, spans, heads),
        out_shape=jax.ShapeDtypeStruct(queries.shape, bf16),
        grid_spec=pltpu.PrefetchScalarGridSpec(
            num_scalar_prefetch=1,
            grid=(chips,),
            in_specs=[block_spec(queries.shape), whole_spec(keys.shape), whole_spec(values.shape)],
            out_specs=block_spec(queries.shape),
            scratch_shapes=[
                pltpu.VMEM((heads, rows, HEAD_DIM), f32),
                pltpu.VMEM((heads, rows, 1), f32),
            ],
        ),
        compiler_params=pltpu.CompilerParams(vmem_limit_bytes=32 * 1024 * 1024),
        cost_estimate=pl.CostEstimate(
            flops=flops, bytes_accessed=6 * 1024 * 1024, transcendentals=flops // 512
        ),
    )(info, queries, keys, values)


def attend_backward(info, queries, keys, values, grads, spans):
    chips, rows, features = queries.shape
    heads = features // HEAD_DIM
    flops = 10 * chips * rows * heads * chips * 2 * rows * HEAD_DIM
    square = pltpu.VMEM((chips, heads, rows, 2 * rows), f32)
    return pl.pallas_call(
        functools.partial(backward_kernel, spans, heads),
        out_shape=(
            jax.ShapeDtypeStruct(queries.shape, f32),
            jax.ShapeDtypeStruct(keys.shape, f32),
            jax.ShapeDtypeStruct(values.shape, f32),
        ),
        grid_spec=pltpu.PrefetchScalarGridSpec(
            num_scalar_prefetch=1,
            grid=(chips,),
            in_specs=[
                block_spec(queries.shape),
                whole_spec(keys.shape),
                whole_spec(values.shape),
                block_spec(queries.shape),
            ],
            out_specs=(
                block_spec(queries.shape),
                whole_spec(keys.shape),
                whole_spec(values.shape),
            ),
            scratch_shapes=[
                square,
                square,
                square,
                pltpu.VMEM((heads, rows, 1), f32),
                pltpu.VMEM((heads, rows, 1), f32),
                pltpu.VMEM((heads, rows, HEAD_DIM), f32),
            ],
        ),
        compiler_params=pltpu.CompilerParams(vmem_limit_bytes=40 * 1024 * 1024),
        cost_estimate=pl.CostEstimate(
            flops=flops, bytes_accessed=12 * 1024 * 1024, transcendentals=flops // 1280
        ),
    )(info, queries, keys, values, grads)


def gate_up_kernel(h_ref, gate_ref, up_ref, product_ref, gelu_ref, slope_ref):
    gate = nt(h_ref[...], gate_ref[...])
    up = nt(h_ref[...], up_ref[...])
    square = gate * gate
    tanh = jnp.tanh(gate * (gelu_a + (gelu_a * gelu_b) * square))
    half = 0.5 + 0.5 * tanh
    gelu = gate * half
    slope = half + gate * (0.5 - 0.5 * tanh * tanh) * (gelu_a + (3.0 * gelu_a * gelu_b) * square)
    product_ref[...] = (gelu * up).astype(bf16)
    gelu_ref[...] = gelu.astype(bf16)
    slope_ref[...] = (up * slope).astype(bf16)


def gate_up(hidden, gate_w, up_w):
    m, width = hidden.shape
    n = gate_w.shape[0]
    tile = next(t for t in (768, 384, 256, 128) if n % t == 0)
    weight_spec = pl.BlockSpec((tile, width), lambda i: (i, 0))
    out_spec = pl.BlockSpec((m, tile), lambda i: (0, i))
    return pl.pallas_call(
        gate_up_kernel,
        out_shape=(jax.ShapeDtypeStruct((m, n), bf16),) * 3,
        grid=(n // tile,),
        in_specs=[pl.BlockSpec((m, width), lambda i: (0, 0)), weight_spec, weight_spec],
        out_specs=(out_spec,) * 3,
        compiler_params=pltpu.CompilerParams(vmem_limit_bytes=56 * 1024 * 1024),
        cost_estimate=pl.CostEstimate(
            flops=4 * m * n * width,
            bytes_accessed=4 * n * width + 2 * m * width + 6 * m * n,
            transcendentals=m * n,
        ),
    )(hidden, gate_w, up_w)


def feed_back_kernel(low_ref, down_ref, gelu_ref, slope_ref, gate_back_ref, up_back_ref):
    grad = nt(low_ref[...], down_ref[...])
    gate_back_ref[...] = (grad * slope_ref[...].astype(f32)).astype(bf16)
    up_back_ref[...] = (grad * gelu_ref[...].astype(f32)).astype(bf16)


def feed_back(low, down_w, gelu, slope):
    m, width = low.shape
    n = down_w.shape[0]
    tile = next(t for t in (768, 384, 256, 128) if n % t == 0)
    spec = pl.BlockSpec((m, tile), lambda i: (0, i))
    return pl.pallas_call(
        feed_back_kernel,
        out_shape=(jax.ShapeDtypeStruct((m, n), bf16),) * 2,
        grid=(n // tile,),
        in_specs=[
            pl.BlockSpec((m, width), lambda i: (0, 0)),
            pl.BlockSpec((tile, width), lambda i: (i, 0)),
            spec,
            spec,
        ],
        out_specs=(spec,) * 2,
        compiler_params=pltpu.CompilerParams(vmem_limit_bytes=56 * 1024 * 1024),
        cost_estimate=pl.CostEstimate(
            flops=2 * m * n * width,
            bytes_accessed=2 * n * width + 2 * m * width + 8 * m * n,
            transcendentals=0,
        ),
    )(low, down_w, gelu, slope)


def rotate(vectors, cosine, sine):
    first, second = vectors[..., :HALF], vectors[..., HALF:]
    return jnp.concatenate(
        [first * cosine - second * sine, second * cosine + first * sine], axis=-1
    )


def inverse_root(values):
    return lax.rsqrt(jnp.mean(values * values, axis=-1, keepdims=True) + epsilon)


def norm_backward(normed, root, gain, grad):
    scaled = grad * gain
    return root * (scaled - normed * jnp.mean(scaled * normed, axis=-1, keepdims=True))


def on_device(
    tokens,
    span_start,
    span_len,
    query_weight,
    key_weight,
    value_weight,
    output_weight,
    gate_weight,
    up_weight,
    down_weight,
    inbound_gain,
    attended_gain,
    prefeed_gain,
    postfeed_gain,
    cotangent,
):
    seq_count, rows, width = tokens.shape
    size = lax.axis_size("ctx")
    index = lax.axis_index("ctx")
    line = Line(size, index)
    chips, z, c = line.chips, line.z, line.c
    spans = span_start.shape[1]
    group = size // KV_HEADS
    member = index % group
    every = chips * rows

    def pair_rows(block):
        other = line.swap(block)
        return jnp.concatenate([jnp.where(c == 0, block, other), jnp.where(c == 0, other, block)])

    def shifted(block, k):
        pairs = [(i, i - i % group + (i % group + k) % group) for i in range(size)]
        return lax.ppermute(block, "ctx", pairs)

    def group_rows(block):
        if group == 2:
            return pair_rows(block)
        count = block.shape[0]
        out = jnp.zeros((group * count, width), block.dtype)
        out = lax.dynamic_update_slice(out, block, (member * count, 0))
        for k in range(1, group):
            place = lax.rem(member + group - k, group) * count
            out = lax.dynamic_update_slice(out, shifted(block, k), (place, 0))
        return out

    def group_sum(grad):
        count = grad.shape[0] // group
        own = lax.dynamic_slice(grad, (member * count, 0), (count, width)).astype(f32)
        for k in range(1, group):
            place = lax.rem(member + k, group) * count
            sent = lax.dynamic_slice(grad, (place, 0), (count, width))
            own = own + shifted(sent.astype(bf16), k).astype(f32)
        return own

    def pair_sum(grad):
        count = grad.shape[0] // 2
        own = lax.dynamic_slice(grad, (c * count, 0), (count, width)).astype(f32)
        sent = lax.dynamic_slice(grad, ((1 - c) * count, 0), (count, width))
        return own + line.swap(sent.astype(bf16)).astype(f32)

    def both_rows(block):
        return jnp.concatenate([block, line.swap(block)])

    count = inbound_gain.shape[0]
    pad = 16
    gains_own = jnp.concatenate([inbound_gain, attended_gain, prefeed_gain, postfeed_gain])
    gains_rows = jnp.pad(gains_own[None, :], ((0, pad - 1), (0, width - 4 * count)))

    query_width = 2 * output_weight.shape[0]
    heads = query_width // HEAD_DIM

    table = jnp.stack(line.table()).astype(jnp.int32)
    places = (
        table[:, None] * (2 * rows) + c * rows + jnp.arange(rows, dtype=jnp.int32)[None, :]
    ).reshape(every)
    inverse = rope_base ** (-(jnp.arange(HALF, dtype=f32) * 2.0 / HEAD_DIM))
    angles = places.astype(f32)[:, None] * inverse[None, :]
    cosine, sine = jnp.cos(angles)[:, None, :], jnp.sin(angles)[:, None, :]
    query_scale = HEAD_DIM ** (-0.5)

    def split(block_rows):
        return [
            block_rows[k * rows : (k + 1) * rows] for k in range(block_rows.shape[0] // rows)
        ]

    def join(blocks):
        return jnp.concatenate(blocks)

    infos = [
        jnp.concatenate(
            [c[None], span_start[s], span_start[s] + span_len[s], table]
        ).astype(jnp.int32)
        for s in range(seq_count)
    ]

    class Sequence:
        def __init__(self, s):
            self.s = s
            self.own = tokens[s]

        def project(self, places, *blocks):
            count = len(blocks)
            merged = join(blocks)
            cos, sin = (t[places.start * rows : places.stop * rows] for t in (cosine, sine))
            values = merged.astype(f32)
            root_in = inverse_root(values)
            hidden = (values * root_in * gain[0]).astype(bf16)
            raw = nt(hidden, qkv_weight)
            queries = raw[:, :query_width].reshape(count * rows, heads, HEAD_DIM)
            queries = (rotate(queries, cos, sin) * query_scale).astype(bf16)
            keys = raw[:, query_width : query_width + HEAD_DIM].reshape(count * rows, 1, HEAD_DIM)
            keys = rotate(keys, cos, sin).astype(bf16).reshape(count * rows, HEAD_DIM)
            values = raw[:, query_width + HEAD_DIM :].astype(bf16)
            mine = jnp.concatenate([keys, values], axis=1).reshape(count, rows, 2 * HEAD_DIM)
            both = jnp.concatenate([mine, line.swap(mine)], axis=1)
            queries = queries.reshape(count, rows, query_width)
            return merged, root_in, hidden, queries, both[:, :, :HEAD_DIM], both[:, :, HEAD_DIM:]

        def attend(self, queries, keys, values):
            attended = attend_forward(infos[self.s], queries, keys, values, spans)
            attended = attended.reshape(every, query_width)
            return attended, nn(attended, out_weight).astype(bf16)

        def after_branch(self, terms):
            branch = total(terms)
            self.root_branch = inverse_root(branch)
            self.normed_branch = branch * self.root_branch
            self.middle = self.own.astype(f32) + self.normed_branch * gain[1]
            self.root_middle = inverse_root(self.middle)
            return (self.middle * self.root_middle * gain[2]).astype(bf16)

        def feed(self, *blocks):
            hidden_ff = join(blocks)
            return (hidden_ff,) + tuple(gate_up(hidden_ff, gate_rows, up_rows))

        def feed_down(self, product):
            return (nn(product, down_rows).astype(bf16),)

        def after_feed(self, terms):
            feed = total(terms)
            root = inverse_root(feed)
            normed = feed * root
            self.upstream = cotangent[self.s].astype(f32)
            self.output = (self.middle + normed * gain[3]).astype(bf16)
            self.postfeed_term = jnp.sum(self.upstream * normed, axis=0)
            return norm_backward(normed, root, gain[3], self.upstream).astype(bf16)

        def feed_back(self, gelu, slope, *blocks):
            feed_low = join(blocks)
            return (feed_low,) + tuple(feed_back(feed_low, down_rows, gelu, slope))

        def feed_in(self, gate_back, up_back):
            return ((nn(gate_back, gate_rows) + nn(up_back, up_rows)).astype(bf16),)

        def after_feed_back(self, terms):
            grad = total(terms)
            normed = self.middle * self.root_middle
            self.prefeed_term = jnp.sum(grad * normed, axis=0)
            self.middle_grad = self.upstream + norm_backward(
                normed, self.root_middle, gain[2], grad
            )
            self.attended_term = jnp.sum(self.middle_grad * self.normed_branch, axis=0)
            return norm_backward(
                self.normed_branch, self.root_branch, gain[1], self.middle_grad
            ).astype(bf16)

        def attend_back(self, branch_low, queries, keys, values):
            mixed = nt(branch_low, out_weight).astype(bf16)
            return attend_backward(
                infos[self.s],
                queries,
                keys,
                values,
                mixed.reshape(chips, rows, query_width),
                spans,
            )

        def turn_back(self, query_rot, key_rot, value_sum):
            sums = jnp.concatenate([key_rot, value_sum], axis=2)
            sums = sums[:, :rows] + line.swap(sums[:, rows:].astype(bf16)).astype(f32)
            sums = sums.reshape(every, 2 * HEAD_DIM)
            query_rot = query_rot.reshape(every, heads, HEAD_DIM)
            query_back = (rotate(query_rot, cosine, -sine) * query_scale).astype(bf16)
            key_back = rotate(sums[:, :HEAD_DIM].reshape(every, 1, HEAD_DIM), cosine, -sine)
            return jnp.concatenate(
                [
                    query_back.reshape(every, query_width),
                    key_back.reshape(every, HEAD_DIM).astype(bf16),
                    sums[:, HEAD_DIM:].astype(bf16),
                ],
                axis=1,
            )

        def project_back(self, near_tokens, far_tokens, near_root, far_root, *sums):
            back = self.turn_back(*sums)
            grad = nn(back, qkv_weight)
            normed = join([near_tokens, far_tokens]).astype(f32) * join([near_root, far_root])
            inbound_term = jnp.sum(grad * normed, axis=0)
            return grad.astype(bf16), inbound_term, back

        def after_project_back(self, terms):
            grad = total(terms)
            values = self.own.astype(f32)
            root = inverse_root(values)
            return (self.middle_grad + norm_backward(values * root, root, gain[0], grad)).astype(
                bf16
            )

    def weight_grad(left_count, *pieces):
        return (tn(join(pieces[:left_count]), join(pieces[left_count:])).astype(bf16),)

    data = lax.axis_size("dp")

    def data_sum(values, order):
        groups = [[(i + order) % data for i in range(data)]]
        return lax.psum(values, "dp", axis_index_groups=groups)

    def core_sum(grad):
        count = grad.shape[0] // 2
        return (grad[:count].astype(f32) + line.swap(grad[count:]).astype(f32)).astype(bf16)

    near, far = slice(0, 2), slice(2, chips)

    def parts_of(*halves):
        return [block for half in halves for block in split(half)]

    a, b = (Sequence(s) for s in range(seq_count))

    ex = Exchange(line, jnp.concatenate([a.own, gains_rows]), sums=False)
    def attention_weights(query_w, key_w, value_w, out_w):
        merged = jnp.concatenate([pair_rows(query_w), group_rows(key_w), group_rows(value_w)])
        return merged, pair_rows(out_w)

    ex.step()
    qkv_weight, out_weight = ex.step(
        attention_weights, (query_weight, key_weight, value_weight, output_weight)
    )
    gate_rows = ex.step(both_rows, (gate_weight,))
    for _ in range(chips - 4):
        ex.step()
    blocks = ex.near() + ex.far()
    gain = jnp.stack([block[rows, : 4 * count] for block in blocks])
    gain_other = line.swap(gain)
    gain = jnp.stack(
        [jnp.where(c == 0, gain, gain_other), jnp.where(c == 0, gain_other, gain)], axis=1
    ).reshape(chips, 8 * count)
    gain = line.exchanged([gain[k] for k in range(chips)])
    gain = jnp.roll(jnp.stack(gain), z, axis=0).reshape(chips, 2, 4, count)
    gain = gain.transpose(2, 0, 1, 3).reshape(4, 1, width).astype(f32)

    def a_attention(*blocks):
        halves = [a.project(near, *blocks[near]), a.project(far, *blocks[far])]
        queries, keys, values = (join([half[i] for half in halves]) for i in range(3, 6))
        attended, out = a.attend(queries, keys, values)
        stored = [[half[i] for half in halves] for i in range(3)]
        return out, (attended, queries, keys, values), stored

    ex = Exchange(line, b.own)
    out, a_kept, (a.tokens, a.root_in, a.hidden) = ex.step(
        a_attention, [block[:rows] for block in blocks]
    )
    a.attended, a.queries, a.keys, a.values = a_kept
    ex.parts = split(out)

    def b_project_near(up_w, *blocks):
        return b.project(near, *blocks), both_rows(up_w)

    b_near, up_rows = ex.step(b_project_near, [up_weight] + ex.near())
    down_rows = ex.step(both_rows, (down_weight,))
    for _ in range(chips - 4):
        ex.step()
    b_far = ex.step(functools.partial(b.project, far), ex.far())
    b.tokens, b.root_in, b.hidden = ([b_near[i], b_far[i]] for i in range(3))
    hidden_a = a.after_branch(ex.terms())

    def b_attention(*halves):
        queries, keys, values = (join(halves[i::3]) for i in range(3))
        attended, out = b.attend(queries, keys, values)
        return out, attended, queries, keys, values

    def feed_phase(x, own, first, inputs):
        ex = Exchange(line, own)
        firsts = ex.step(first, inputs)
        yield firsts, ex
        hidden, product, gelu, slope = ex.step(x.feed, ex.near())
        (out,) = ex.step(x.feed_down, (product,))
        for _ in range(chips - 4):
            ex.step()
        x.out_near = out
        lasts = ex.step(x.feed, ex.far())
        x.hidden_ff, x.product, x.gelu, x.slope = (
            [u, v] for u, v in zip((hidden, product, gelu, slope), lasts)
        )
        yield lasts, ex

    steps = feed_phase(a, hidden_a, b_attention, b_near[3:] + b_far[3:])
    (out, b.attended, b.queries, b.keys, b.values), ex = next(steps)
    ex.parts = split(out)
    next(steps)
    hidden_b = b.after_branch(ex.terms())

    steps = feed_phase(b, hidden_b, a.feed_down, (a.product[1],))
    (out,), ex = next(steps)
    ex.parts = parts_of(a.out_near, out)
    next(steps)
    low_a = a.after_feed(ex.terms())

    def back_phase(x, own, first, inputs, also):
        ex = Exchange(line, own)
        firsts = ex.step(first, inputs)
        yield firsts, ex
        low, gate_back, up_back = ex.step(
            functools.partial(x.feed_back, x.gelu[0], x.slope[0]), ex.near()
        )
        (x.out_near,) = ex.step(x.feed_in, (gate_back, up_back))
        for _ in range(chips - 4):
            ex.step()

        def last(*blocks):
            outs = x.feed_back(x.gelu[1], x.slope[1], *blocks)
            return outs, also(low, outs[0])

        lasts, more = ex.step(last, ex.far())
        x.feed_low, x.gate_back, x.up_back = (
            [u, v] for u, v in zip((low, gate_back, up_back), lasts)
        )
        yield more, ex

    steps = back_phase(a, low_a, b.feed_down, (b.product[1],), lambda low, high: ())
    (out,), ex = next(steps)
    ex.parts = parts_of(b.out_near, out)
    next(steps)
    low_b = b.after_feed(ex.terms())

    def down_work(low, high):
        return weight_grad(4, *a.product, *b.product, *a.feed_low, low, high)

    steps = back_phase(b, low_b, a.feed_in, (a.gate_back[1], a.up_back[1]), down_work)
    (out,), ex = next(steps)
    ex.parts = parts_of(a.out_near, out)
    (down_grad,), _ = next(steps)
    branch_a = a.after_feed_back(ex.terms())

    def b_feed_in(gate_back, up_back, down_grad):
        return b.feed_in(gate_back, up_back) + (core_sum(down_grad),)

    def a_attention_back(*blocks):
        branch_low = join(blocks)
        return (branch_low,) + tuple(a.attend_back(branch_low, a.queries, a.keys, a.values))

    ex = Exchange(line, branch_a)
    out, down_grad = ex.step(b_feed_in, (b.gate_back[1], b.up_back[1], down_grad))
    ex.parts = parts_of(b.out_near, out)
    left_grad = functools.partial(weight_grad, 4)
    hidden_ff = a.hidden_ff + b.hidden_ff
    (gate_grad,) = ex.step(left_grad, a.gate_back + b.gate_back + hidden_ff)
    gate_grad = ex.step(core_sum, (gate_grad,))
    early_sums = data_sum((down_grad, gate_grad), 0)
    for _ in range(chips - 4):
        ex.step()
    a.branch_low, *a_sums = ex.step(a_attention_back, ex.near() + ex.far())
    branch_b = b.after_feed_back(ex.terms())

    def b_attention_back(*blocks):
        branch_low = join(blocks)
        return (branch_low,) + tuple(b.attend_back(branch_low, b.queries, b.keys, b.values))

    ex = Exchange(line, branch_b)
    out, a.inbound_term, a.back = ex.step(a.project_back, a.tokens + a.root_in + a_sums)
    ex.parts = split(out)
    (up_grad,) = ex.step(left_grad, a.up_back + b.up_back + hidden_ff)
    up_grad = ex.step(core_sum, (up_grad,))
    up_sum = data_sum(up_grad, 1)
    for _ in range(chips - 4):
        ex.step()
    b.branch_low, *b_sums = ex.step(b_attention_back, ex.near() + ex.far())
    tokens_grad_a = a.after_project_back(ex.terms())

    grad, b.inbound_term, b.back = b.project_back(*b.tokens, *b.root_in, *b_sums)
    gain_terms = jnp.stack(
        [
            a.inbound_term + b.inbound_term,
            a.attended_term + b.attended_term,
            a.prefeed_term + b.prefeed_term,
            a.postfeed_term + b.postfeed_term,
        ]
    ).astype(bf16)
    gain_terms = gain_terms.reshape(4, chips, 2, count).transpose(1, 2, 0, 3)
    gain_terms = jnp.roll(gain_terms.reshape(chips, 1, 8 * count), -z, axis=0)
    gain_terms = jnp.stack(line.exchanged([gain_terms[k] for k in range(chips)]))
    gain_terms = jnp.pad(gain_terms, ((0, 0), (0, pad - 1), (0, width - 8 * count)))
    ex = Exchange(line)
    ex.parts = [jnp.concatenate([part, gain_terms[k]]) for k, part in enumerate(split(grad))]

    def attention_grads(back_a, back_b):
        return weight_grad(2, back_a, back_b, *a.hidden, *b.hidden) + weight_grad(
            2, a.attended, b.attended, a.branch_low, b.branch_low
        )

    def attention_sums(qkv_grad, output_grad):
        return tuple(
            value.astype(bf16)
            for value in (
                pair_sum(qkv_grad[:query_width]),
                group_sum(qkv_grad[query_width : query_width + HEAD_DIM]),
                group_sum(qkv_grad[query_width + HEAD_DIM :]),
                pair_sum(output_grad),
            )
        )

    late = ex.step(attention_grads, (a.back, b.back), held=early_sums)
    down_sum, gate_sum = ex.held
    late = ex.step(attention_sums, late)
    ex.step(held=(up_sum,))
    (up_sum,) = ex.held
    for _ in range(chips - 4):
        ex.step()
    late_sums = data_sum(late, 2)
    grad = total(ex.terms())
    tokens_grad_b = b.after_project_back([grad[:rows]])

    row = grad[rows, : 8 * count].reshape(2, 4, count)
    mine = jnp.where(c == 0, row[0], row[1])
    other = jnp.where(c == 0, row[1], row[0])
    gain_sums = lax.psum(mine + line.swap(other.astype(bf16)).astype(f32), "dp")

    return (
        jnp.stack([a.output, b.output]),
        jnp.stack([tokens_grad_a, tokens_grad_b]),
        late_sums[0].astype(f32),
        late_sums[1].astype(f32),
        late_sums[2].astype(f32),
        late_sums[3].astype(f32),
        gate_sum.astype(f32),
        up_sum.astype(f32),
        down_sum.astype(f32),
        gain_sums[0],
        gain_sums[1],
        gain_sums[2],
        gain_sums[3],
    )


def solution(mesh):
    rows = P("ctx", None)
    gain = P("ctx")
    tokens = P("dp", "ctx", None)
    spans = P("dp", None)
    return jax.shard_map(
        on_device,
        mesh=mesh,
        in_specs=(tokens, spans, spans) + (rows,) * 7 + (gain,) * 4 + (tokens,),
        out_specs=(tokens, tokens) + (rows,) * 7 + (gain,) * 4,
        check_vma=False,
    )
```

```python
import functools

import jax
import jax.numpy as jnp
from jax import lax
from jax.experimental import pallas as pl
from jax.experimental.pallas import tpu as pltpu
from jax.sharding import PartitionSpec as P

HEADS = 8
KV_HEADS = 4
HEAD_DIM = 256
HALF = HEAD_DIM // 2

epsilon = 1e-06
soft_cap = 50.0
rope_base = 10000.0
gelu_a = 0.7978845608028654
gelu_b = 0.044715
query_scale = HEAD_DIM ** (-0.5)

bf16 = jnp.bfloat16
f32 = jnp.float32


def nt(left_side, right_side):
    return lax.dot_general(
        left_side, right_side, (((1,), (1,)), ((), ())), preferred_element_type=f32
    )


def nn(left_side, right_side):
    return lax.dot_general(
        left_side, right_side, (((1,), (0,)), ((), ())), preferred_element_type=f32
    )


def tn(left_side, right_side):
    return lax.dot_general(
        left_side, right_side, (((0,), (0,)), ((), ())), preferred_element_type=f32
    )


def inverse_root(values):
    return lax.rsqrt(jnp.mean(values * values, axis=-1, keepdims=True) + epsilon)


def norm_backward(normed, root, gain, grad):
    scaled = grad * gain
    return root * (scaled - normed * jnp.mean(scaled * normed, axis=-1, keepdims=True))


class Line:
    def __init__(self, size, index):
        self.chips = size // 2
        self.z = index // 2
        self.c = index % 2
        self.core_pairs = [(i, i ^ 1) for i in range(size)]

    def pairs(self, step, low, high):
        return [
            (2 * z + c, 2 * (z + step) + c)
            for z in range(low, high)
            for c in range(2)
            if 0 <= z + step < self.chips
        ]

    def right(self, block, low, high):
        return lax.ppermute(block, "ctx", self.pairs(1, low, high))

    def left(self, block, low, high):
        n = self.chips
        return lax.ppermute(block, "ctx", self.pairs(-1, n - high, n - low))

    def swap(self, block):
        return lax.ppermute(block, "ctx", self.core_pairs)

    def exchanged(self, items):
        last = self.z == self.chips - 1
        items = list(items)
        first, final = items[1], items[-1]
        items[1] = jnp.where(last, final, first)
        items[-1] = jnp.where(last, first, final)
        return items

    def table(self):
        order = self.exchanged([jnp.int32(k) for k in range(self.chips)])
        return [lax.rem(self.z + k, self.chips) for k in order]


def tied(*values):
    return lax.optimization_barrier(values)


class Exchange:
    def __init__(self, line, own=None, sums=True):
        self.line, self.own, self.sums = line, own, sums
        self.parts = None
        self.s = 0
        self.from_left, self.from_right = [own], [own]
        self.sum_left = self.sum_right = None

    def step(self, work=None, inputs=(), held=()):
        line, n, z = self.line, self.line.chips, self.line.z
        gathers = self.own is not None
        self.s += 1
        s = self.s
        to_right = to_left = None
        low, high = 0, n
        if gathers and s <= n - 1:
            to_right, to_left = self.from_left[s - 1], self.from_right[s - 1]
            low = s - 1
        j = s - 1 if gathers else s
        if self.sums and j >= 1:
            sum_r, sum_l = self.parts[n - j], self.parts[n - 1 if j == 1 else j]
            if j == n - 1:
                sum_l = jnp.where(z == n - 1, self.parts[1], self.parts[n - 1])
            if self.sum_left is not None:
                sum_r = (sum_r.astype(f32) + self.sum_left.astype(f32)).astype(bf16)
                sum_l = (sum_l.astype(f32) + self.sum_right.astype(f32)).astype(bf16)
            if to_right is None:
                to_right, to_left, high = sum_r, sum_l, j
            else:
                to_right = jnp.where(z >= s - 1, to_right, sum_r)
                to_left = jnp.where(n - 1 - z >= s - 1, to_left, sum_l)
                low = 0
        to_right, to_left, inputs, self.held = tied(to_right, to_left, inputs, held)
        got_left = line.right(to_right, low, high)
        got_right = line.left(to_left, low, high)
        outs = work(*inputs) if work is not None else ()
        got_left, got_right, outs = tied(got_left, got_right, outs)
        if gathers and s <= n - 1:
            self.from_left.append(got_left)
            self.from_right.append(got_right)
        if self.sums and j >= 1:
            self.sum_left, self.sum_right = got_left, got_right
        return outs

    def give(self, *halves):
        rows = halves[-1].shape[0] // (self.line.chips if len(halves) == 1 else self.line.chips - 2)
        self.first = halves[0]
        self.parts = [
            half[k * rows : (k + 1) * rows]
            for half in halves
            for k in range(half.shape[0] // rows)
        ]

    def near(self):
        last = self.line.z == self.line.chips - 1
        return [self.own, jnp.where(last, self.from_left[1], self.from_right[1])]

    def far(self):
        n, z = self.line.chips, self.line.z
        blocks = [
            jnp.where(z + k < n, self.from_right[k], self.from_left[n - k])
            for k in range(2, n - 1)
        ]
        final = jnp.where(z == 0, self.from_right[n - 1], self.from_left[1])
        return blocks + [jnp.where(z == n - 1, self.from_left[n - 1], final)]

    def terms(self):
        return (self.first, self.sum_left, self.sum_right)


def total(terms):
    rows = terms[-1].shape[0]
    return sum(t[:rows].astype(f32) for t in terms)


def spans_of(place, info, spans, none):
    label = jnp.full(place.shape, none, jnp.int32)
    for s in range(spans):
        start, stop = info[1 + s], info[1 + spans + s]
        label = jnp.where((place >= start) & (place < stop), s, label)
    return label


def seen_block(query_block, key_block, width, info, spans):
    seen = key_block <= query_block
    for s in range(spans):
        start, stop = info[1 + s], info[1 + spans + s]
        seen = seen | ((start < (query_block + 1) * width) & (stop > key_block * width))
    return seen


def block_mask(query_block, key_block, rows, info, spans):
    c = info[0]
    width = 2 * rows
    query_place = (
        query_block * width + c * rows + lax.broadcasted_iota(jnp.int32, (rows, 1), 0)
    )
    j = lax.broadcasted_iota(jnp.int32, (1, width), 1)
    key_place = key_block * width + j + jnp.where(j < rows, c * rows, -c * rows)
    query_span = spans_of(query_place, info, spans, -2)
    key_span = spans_of(key_place, info, spans, -1)
    return (key_place <= query_place) | (key_span == query_span)


def place_of(refs, kk):
    return refs[0][kk] if kk < 2 else refs[1][kk - 2]


def key_block_of(own_refs, other_refs, kk, part):
    cut = slice(part * HEAD_DIM, (part + 1) * HEAD_DIM)
    return jnp.concatenate([place_of(own_refs, kk)[:, cut], place_of(other_refs, kk)[:, cut]])


def forward_kernel(spans, heads, info, *refs):
    queries, own, other = refs[0:2], refs[2:4], refs[4:6]
    o_ref, acc_ref, sum_ref = refs[6:]
    rows = own[0].shape[1]
    chips = own[0].shape[0] + own[1].shape[0]
    width = 2 * rows
    query_block = info[1 + 2 * spans + pl.program_id(0)]
    query = jnp.where(pl.program_id(0) < 2, queries[0][0], queries[1][0])
    acc_ref[...] = jnp.zeros_like(acc_ref)
    sum_ref[...] = jnp.zeros_like(sum_ref)
    for kk in range(chips):
        key_block = info[1 + 2 * spans + kk]

        @pl.when(seen_block(query_block, key_block, width, info, spans))
        def _():
            allowed = block_mask(query_block, key_block, rows, info, spans)
            keys, values = (key_block_of(own, other, kk, part) for part in range(2))
            for h in range(heads):
                scores = nt(query[:, h * HEAD_DIM : (h + 1) * HEAD_DIM], keys)
                weights = jnp.where(
                    allowed, jnp.exp(soft_cap * jnp.tanh(scores * (1.0 / soft_cap))), 0.0
                )
                sum_ref[h] += jnp.sum(weights, axis=1, keepdims=True)
                acc_ref[h] += nn(weights.astype(bf16), values)

    for h in range(heads):
        o_ref[0, :, h * HEAD_DIM : (h + 1) * HEAD_DIM] = (acc_ref[h] / sum_ref[h]).astype(bf16)


def turned_back(vectors, cosine, sine):
    first, second = vectors[:, :HALF], vectors[:, HALF:]
    return first * cosine + second * sine, second * cosine - first * sine


def backward_kernel(spans, heads, info, *refs):
    queries, own, other = refs[0:2], refs[2:4], refs[4:6]
    g_ref, cos_ref, sin_ref, tables = refs[6], refs[7], refs[8], refs[9:13]
    dq_ref, own_ref, other_ref = refs[13:16]
    dk_ref, dv_ref, p_ref, r_ref, t_ref, sum_ref, inner_ref, acc_ref = refs[16:]
    chips, width, _ = dk_ref.shape
    rows = width // 2
    query_block = info[1 + 2 * spans + pl.program_id(0)]
    query = jnp.where(pl.program_id(0) < 2, queries[0][0], queries[1][0])

    @pl.when(pl.program_id(0) == 0)
    def _():
        dk_ref[...] = jnp.zeros_like(dk_ref)
        dv_ref[...] = jnp.zeros_like(dv_ref)

    acc_ref[...] = jnp.zeros_like(acc_ref)
    sum_ref[...] = jnp.zeros_like(sum_ref)
    inner_ref[...] = jnp.zeros_like(inner_ref)
    for kk in range(chips):
        key_block = info[1 + 2 * spans + kk]

        @pl.when(seen_block(query_block, key_block, width, info, spans))
        def _():
            allowed = block_mask(query_block, key_block, rows, info, spans)
            keys, values = (key_block_of(own, other, kk, part) for part in range(2))
            for h in range(heads):
                head = slice(h * HEAD_DIM, (h + 1) * HEAD_DIM)
                squashed = jnp.tanh(nt(query[:, head], keys) * (1.0 / soft_cap))
                weights = jnp.where(allowed, jnp.exp(soft_cap * squashed), 0.0)
                row_grad = nt(g_ref[0, :, head], values)
                sum_ref[h] += jnp.sum(weights, axis=1, keepdims=True)
                inner_ref[h] += jnp.sum(weights * row_grad, axis=1, keepdims=True)
                p_ref[kk, h] = weights
                r_ref[kk, h] = row_grad
                t_ref[kk, h] = 1.0 - squashed * squashed

    for kk in range(chips):
        key_block = info[1 + 2 * spans + kk]

        @pl.when(seen_block(query_block, key_block, width, info, spans))
        def _():
            keys = key_block_of(own, other, kk, 0)
            for h in range(heads):
                head = slice(h * HEAD_DIM, (h + 1) * HEAD_DIM)
                inverse = 1.0 / sum_ref[h]
                weights = p_ref[kk, h] * inverse
                inner = inner_ref[h] * inverse
                score_grad = (weights * (r_ref[kk, h] - inner) * t_ref[kk, h]).astype(bf16)
                acc_ref[h] += nn(score_grad, keys)
                dk_ref[kk] += tn(score_grad, query[:, head])
                dv_ref[kk] += tn(weights.astype(bf16), g_ref[0, :, head])

    for h in range(heads):
        first, second = turned_back(acc_ref[h], cos_ref[0], sin_ref[0])
        dq_ref[0, :, h * HEAD_DIM : h * HEAD_DIM + HALF] = (first * query_scale).astype(bf16)
        dq_ref[0, :, h * HEAD_DIM + HALF : (h + 1) * HEAD_DIM] = (second * query_scale).astype(bf16)

    @pl.when(pl.program_id(0) == chips - 1)
    def _():
        for kk in range(chips):
            for part, out in ((0, own_ref), (1, other_ref)):
                some = slice(part * rows, (part + 1) * rows)
                first, second = turned_back(
                    dk_ref[kk, some], tables[2 * part][kk], tables[2 * part + 1][kk]
                )
                out[kk, :, :HALF] = first.astype(out.dtype)
                out[kk, :, HALF:HEAD_DIM] = second.astype(out.dtype)
                out[kk, :, HEAD_DIM:] = dv_ref[kk, some].astype(out.dtype)


def block_spec(shape):
    return pl.BlockSpec((1,) + tuple(shape[1:]), lambda i, info: (i, 0, 0))


def near_spec(shape):
    return pl.BlockSpec((1,) + tuple(shape[1:]), lambda i, info: (jnp.minimum(i, 1), 0, 0))


def far_spec(shape):
    return pl.BlockSpec((1,) + tuple(shape[1:]), lambda i, info: (jnp.maximum(i - 2, 0), 0, 0))


def whole_spec(shape):
    return pl.BlockSpec(tuple(shape), lambda i, info: (0,) * len(shape))


light = pl.CostEstimate(flops=1024, bytes_accessed=1024, transcendentals=0)


def attend_forward(info, queries, own, other, spans):
    (near, rows, features), far = queries[0].shape, queries[1].shape[0]
    chips, heads = near + far, features // HEAD_DIM
    arrays = (*queries, *own, *other)
    out = jax.ShapeDtypeStruct((chips, rows, features), bf16)
    return pl.pallas_call(
        functools.partial(forward_kernel, spans, heads),
        out_shape=out,
        grid_spec=pltpu.PrefetchScalarGridSpec(
            num_scalar_prefetch=1,
            grid=(chips,),
            in_specs=[near_spec(queries[0].shape), far_spec(queries[1].shape)]
            + [whole_spec(x.shape) for x in arrays[2:]],
            out_specs=block_spec(out.shape),
            scratch_shapes=[
                pltpu.VMEM((heads, rows, HEAD_DIM), f32),
                pltpu.VMEM((heads, rows, 1), f32),
            ],
        ),
        compiler_params=pltpu.CompilerParams(vmem_limit_bytes=32 * 1024 * 1024),
        cost_estimate=light,
    )(info, *arrays)


def attend_backward(info, queries, own, other, grads, tables, spans):
    chips, rows, features = grads.shape
    heads = features // HEAD_DIM
    arrays = (*queries, *own, *other, grads, tables[0], tables[1], *tables)
    square = pltpu.VMEM((chips, heads, rows, 2 * rows), f32)
    pairs = (chips, rows, 2 * HEAD_DIM)
    return pl.pallas_call(
        functools.partial(backward_kernel, spans, heads),
        out_shape=(
            jax.ShapeDtypeStruct(grads.shape, bf16),
            jax.ShapeDtypeStruct(pairs, f32),
            jax.ShapeDtypeStruct(pairs, bf16),
        ),
        grid_spec=pltpu.PrefetchScalarGridSpec(
            num_scalar_prefetch=1,
            grid=(chips,),
            in_specs=[near_spec(queries[0].shape), far_spec(queries[1].shape)]
            + [whole_spec(x.shape) for x in arrays[2:6]]
            + [block_spec(x.shape) for x in arrays[6:9]]
            + [whole_spec(x.shape) for x in arrays[9:]],
            out_specs=(block_spec(grads.shape), whole_spec(pairs), whole_spec(pairs)),
            scratch_shapes=[
                pltpu.VMEM((chips, 2 * rows, HEAD_DIM), f32),
                pltpu.VMEM((chips, 2 * rows, HEAD_DIM), f32),
                square,
                square,
                square,
                pltpu.VMEM((heads, rows, 1), f32),
                pltpu.VMEM((heads, rows, 1), f32),
                pltpu.VMEM((heads, rows, HEAD_DIM), f32),
            ],
        ),
        compiler_params=pltpu.CompilerParams(vmem_limit_bytes=48 * 1024 * 1024),
        cost_estimate=light,
    )(info, *arrays)


def row_call(kernel, grid, ins, outs, *arrays):
    return pl.pallas_call(
        kernel,
        out_shape=tuple(out[0] for out in outs),
        grid=(grid,),
        in_specs=[pl.BlockSpec(*spec) for spec in ins],
        out_specs=tuple(pl.BlockSpec(*out[1:]) for out in outs),
        compiler_params=pltpu.CompilerParams(vmem_limit_bytes=40 * 1024 * 1024),
        cost_estimate=light,
    )(*arrays)


def add_rows(ref, rows):
    @pl.when(pl.program_id(0) == 0)
    def _():
        ref[...] = jnp.zeros_like(ref)

    ref[...] += jnp.sum(rows, axis=0, keepdims=True)


def summed(refs):
    return sum(ref[...].astype(f32) for ref in refs)


def project_kernel(heads, x_ref, gain_ref, w_ref, cos_ref, sin_ref, hidden_ref, q_ref, kv_ref):
    values = x_ref[...].astype(f32)
    hidden = (values * inverse_root(values) * gain_ref[0:1]).astype(bf16)
    hidden_ref[...] = hidden
    raw = nt(hidden, w_ref[...])
    cosine, sine = cos_ref[...], sin_ref[...]
    for h in range(heads + 1):
        start = h * HEAD_DIM
        first, second = raw[:, start : start + HALF], raw[:, start + HALF : start + HEAD_DIM]
        turned = first * cosine - second * sine, second * cosine + first * sine
        if h < heads:
            q_ref[:, start : start + HALF] = (turned[0] * query_scale).astype(bf16)
            q_ref[:, start + HALF : start + HEAD_DIM] = (turned[1] * query_scale).astype(bf16)
        else:
            kv_ref[:, :HALF] = turned[0].astype(bf16)
            kv_ref[:, HALF:HEAD_DIM] = turned[1].astype(bf16)
    kv_ref[:, HEAD_DIM:] = raw[:, (heads + 1) * HEAD_DIM :].astype(bf16)


def project(tokens, gains, weight, cosine, sine, rows):
    m, width = tokens.shape
    features = weight.shape[0] - 2 * HEAD_DIM
    whole = lambda i: (0, 0)
    block = lambda i: (i, 0)
    return row_call(
        functools.partial(project_kernel, features // HEAD_DIM),
        m // rows,
        [
            ((rows, width), block),
            (gains.shape, whole),
            (weight.shape, whole),
            ((rows, HALF), block),
            ((rows, HALF), block),
        ],
        [
            (jax.ShapeDtypeStruct((m, n), bf16), (rows, n), block)
            for n in (width, features, 2 * HEAD_DIM)
        ],
        tokens,
        gains,
        weight,
        cosine,
        sine,
    )


def project_back_kernel(dq_ref, own_ref, got_ref, w_ref, near_ref, far_ref, *outs):
    grad_ref, back_ref, inbound_ref = outs
    pairs = (own_ref[...] + got_ref[...].astype(f32)).astype(bf16)
    back = jnp.concatenate([dq_ref[...], pairs], axis=1)
    back_ref[...] = back
    grad = nn(back, w_ref[...])
    grad_ref[...] = grad.astype(bf16)
    values = jnp.where(pl.program_id(0) < 2, near_ref[...], far_ref[...]).astype(f32)
    add_rows(inbound_ref, grad * (values * inverse_root(values)))


def project_back(query_back, own, got, weight, near, far, rows):
    m, features = query_back.shape
    count, width = weight.shape
    block = lambda i: (i, 0)
    whole = lambda i: (0, 0)
    pairs = ((rows, 2 * HEAD_DIM), block)
    return row_call(
        project_back_kernel,
        m // rows,
        [
            ((rows, features), block),
            pairs,
            pairs,
            (weight.shape, whole),
            ((rows, width), lambda i: (jnp.minimum(i, 1), 0)),
            ((rows, width), lambda i: (jnp.maximum(i - 2, 0), 0)),
        ],
        [
            (jax.ShapeDtypeStruct((m, width), bf16), (rows, width), block),
            (jax.ShapeDtypeStruct((m, count), bf16), (rows, count), block),
            (jax.ShapeDtypeStruct((1, width), f32), (1, width), whole),
        ],
        query_back,
        own,
        got,
        weight,
        near,
        far,
    )


def branch_kernel(p_ref, l_ref, r_ref, own_ref, gain_ref, branch_ref, middle_ref, hidden_ref):
    branch = summed((p_ref, l_ref, r_ref))
    branch_ref[...] = branch
    middle = own_ref[...].astype(f32) + branch * inverse_root(branch) * gain_ref[1:2]
    middle_ref[...] = middle
    hidden_ref[...] = (middle * inverse_root(middle) * gain_ref[2:3]).astype(bf16)


def feed_kernel(p_ref, l_ref, r_ref, middle_ref, cot_ref, gain_ref, out_ref, low_ref, term_ref):
    feed = summed((p_ref, l_ref, r_ref))
    root = inverse_root(feed)
    normed = feed * root
    gain = gain_ref[3:4]
    upstream = cot_ref[...].astype(f32)
    out_ref[...] = (middle_ref[...] + normed * gain).astype(bf16)
    low_ref[...] = norm_backward(normed, root, gain, upstream).astype(bf16)
    add_rows(term_ref, upstream * normed)


def feed_back_norm_kernel(p_ref, l_ref, r_ref, middle_ref, branch_ref, cot_ref, gain_ref, *outs):
    grad_ref, low_ref, prefeed_ref, attended_ref = outs
    grad = summed((p_ref, l_ref, r_ref))
    middle = middle_ref[...]
    root = inverse_root(middle)
    normed = middle * root
    add_rows(prefeed_ref, grad * normed)
    middle_grad = cot_ref[...].astype(f32) + norm_backward(normed, root, gain_ref[2:3], grad)
    grad_ref[...] = middle_grad
    branch = branch_ref[...]
    root = inverse_root(branch)
    normed = branch * root
    add_rows(attended_ref, middle_grad * normed)
    low_ref[...] = norm_backward(normed, root, gain_ref[1:2], middle_grad).astype(bf16)


def norm_call(kernel, terms, arrays, gains, sequence, outs):
    rows, width = terms[1].shape
    tile = rows // 2
    block = ((tile, width), lambda i: (i, 0))
    one = ((None, tile, width), lambda i: (sequence, i, 0))
    whole = lambda i: (0, 0)
    return row_call(
        kernel,
        2,
        [block] * 3 + [one if x.ndim == 3 else block for x in arrays] + [(gains.shape, whole)],
        [
            (jax.ShapeDtypeStruct((1, width), f32), (1, width), whole)
            if kind is None
            else (jax.ShapeDtypeStruct((rows, width), kind), *block)
            for kind in outs
        ],
        *terms,
        *arrays,
        gains,
    )


def gate_up_kernel(h_ref, gate_ref, up_ref, product_ref, gelu_ref, slope_ref):
    gate = nt(h_ref[...], gate_ref[...])
    up = nt(h_ref[...], up_ref[...])
    square = gate * gate
    tanh = jnp.tanh(gate * (gelu_a + (gelu_a * gelu_b) * square))
    half = 0.5 + 0.5 * tanh
    gelu = gate * half
    slope = half + gate * (0.5 - 0.5 * tanh * tanh) * (gelu_a + (3.0 * gelu_a * gelu_b) * square)
    product_ref[...] = (gelu * up).astype(bf16)
    gelu_ref[...] = gelu.astype(bf16)
    slope_ref[...] = (up * slope).astype(bf16)


def gate_up(hidden, gate_w, up_w):
    m, width = hidden.shape
    n = gate_w.shape[0]
    tile = next(t for t in (768, 384, 256, 128) if n % t == 0)
    weight_spec = pl.BlockSpec((tile, width), lambda i: (i, 0))
    out_spec = pl.BlockSpec((m, tile), lambda i: (0, i))
    return pl.pallas_call(
        gate_up_kernel,
        out_shape=(jax.ShapeDtypeStruct((m, n), bf16),) * 3,
        grid=(n // tile,),
        in_specs=[pl.BlockSpec((m, width), lambda i: (0, 0)), weight_spec, weight_spec],
        out_specs=(out_spec,) * 3,
        compiler_params=pltpu.CompilerParams(vmem_limit_bytes=56 * 1024 * 1024),
        cost_estimate=light,
    )(hidden, gate_w, up_w)


def mix_kernel(*refs):
    count = len(refs) // 2
    out = sum(nn(refs[i][...], refs[count + i][...]) for i in range(count))
    refs[-1][...] = out.astype(bf16)


def mix(lefts, weights):
    m, depth = lefts[0].shape
    n = weights[0].shape[1]
    tile = next(t for t in (768, 384, 256, 128) if n % t == 0)
    return pl.pallas_call(
        mix_kernel,
        out_shape=jax.ShapeDtypeStruct((m, n), bf16),
        grid=(n // tile,),
        in_specs=[pl.BlockSpec((m, depth), lambda i: (0, 0))] * len(lefts)
        + [pl.BlockSpec((depth, tile), lambda i: (0, i))] * len(weights),
        out_specs=pl.BlockSpec((m, tile), lambda i: (0, i)),
        compiler_params=pltpu.CompilerParams(vmem_limit_bytes=56 * 1024 * 1024),
        cost_estimate=light,
    )(*lefts, *weights)


def feed_back_kernel(low_ref, down_ref, gelu_ref, slope_ref, gate_back_ref, up_back_ref):
    grad = nt(low_ref[...], down_ref[...])
    gate_back_ref[...] = (grad * slope_ref[...].astype(f32)).astype(bf16)
    up_back_ref[...] = (grad * gelu_ref[...].astype(f32)).astype(bf16)


def feed_back(low, down_w, gelu, slope):
    m, width = low.shape
    n = down_w.shape[0]
    tile = next(t for t in (768, 384, 256, 128) if n % t == 0)
    spec = pl.BlockSpec((m, tile), lambda i: (0, i))
    return pl.pallas_call(
        feed_back_kernel,
        out_shape=(jax.ShapeDtypeStruct((m, n), bf16),) * 2,
        grid=(n // tile,),
        in_specs=[
            pl.BlockSpec((m, width), lambda i: (0, 0)),
            pl.BlockSpec((tile, width), lambda i: (i, 0)),
            spec,
            spec,
        ],
        out_specs=(spec,) * 2,
        compiler_params=pltpu.CompilerParams(vmem_limit_bytes=56 * 1024 * 1024),
        cost_estimate=light,
    )(low, down_w, gelu, slope)


def on_device(
    tokens,
    span_start,
    span_len,
    query_weight,
    key_weight,
    value_weight,
    output_weight,
    gate_weight,
    up_weight,
    down_weight,
    inbound_gain,
    attended_gain,
    prefeed_gain,
    postfeed_gain,
    cotangent,
):
    seq_count, rows, width = tokens.shape
    size = lax.axis_size("ctx")
    index = lax.axis_index("ctx")
    line = Line(size, index)
    chips, z, c = line.chips, line.z, line.c
    spans = span_start.shape[1]
    group = size // KV_HEADS
    member = index % group
    every = chips * rows

    def pair_rows(block):
        other = line.swap(block)
        return jnp.concatenate([jnp.where(c == 0, block, other), jnp.where(c == 0, other, block)])

    def shifted(block, k):
        pairs = [(i, i - i % group + (i % group + k) % group) for i in range(size)]
        return lax.ppermute(block, "ctx", pairs)

    def group_rows(block):
        if group == 2:
            return pair_rows(block)
        count = block.shape[0]
        out = jnp.zeros((group * count, width), block.dtype)
        out = lax.dynamic_update_slice(out, block, (member * count, 0))
        for k in range(1, group):
            place = lax.rem(member + group - k, group) * count
            out = lax.dynamic_update_slice(out, shifted(block, k), (place, 0))
        return out

    def group_sum(grad):
        count = grad.shape[0] // group
        own = lax.dynamic_slice(grad, (member * count, 0), (count, width)).astype(f32)
        for k in range(1, group):
            place = lax.rem(member + k, group) * count
            sent = lax.dynamic_slice(grad, (place, 0), (count, width))
            own = own + shifted(sent.astype(bf16), k).astype(f32)
        return own

    def pair_sum(grad):
        count = grad.shape[0] // 2
        own = lax.dynamic_slice(grad, (c * count, 0), (count, width)).astype(f32)
        sent = lax.dynamic_slice(grad, ((1 - c) * count, 0), (count, width))
        return own + line.swap(sent.astype(bf16)).astype(f32)

    def both_rows(block):
        return jnp.concatenate([block, line.swap(block)])

    count = inbound_gain.shape[0]
    pad = 16
    gains_own = jnp.concatenate([inbound_gain, attended_gain, prefeed_gain, postfeed_gain])
    gains_rows = jnp.pad(gains_own[None, :], ((0, pad - 1), (0, width - 4 * count)))

    query_width = 2 * output_weight.shape[0]
    heads = query_width // HEAD_DIM

    table = jnp.stack(line.table()).astype(jnp.int32)
    places = (
        table[:, None] * (2 * rows) + c * rows + jnp.arange(rows, dtype=jnp.int32)[None, :]
    ).reshape(every)
    inverse = rope_base ** (-(jnp.arange(HALF, dtype=f32) * 2.0 / HEAD_DIM))

    def turns(places):
        angles = places.astype(f32)[:, None] * inverse[None, :]
        return jnp.cos(angles), jnp.sin(angles)

    cosine, sine = turns(places)
    tables = [
        t.reshape(chips, rows, HALF)
        for t in (cosine, sine) + turns(places + jnp.where(c == 0, rows, -rows))
    ]

    def split(block_rows):
        return [
            block_rows[k * rows : (k + 1) * rows] for k in range(block_rows.shape[0] // rows)
        ]

    def join(blocks):
        return jnp.concatenate(blocks)

    infos = [
        jnp.concatenate(
            [c[None], span_start[s], span_start[s] + span_len[s], table]
        ).astype(jnp.int32)
        for s in range(seq_count)
    ]

    class Sequence:
        def __init__(self, s):
            self.s = s
            self.own = tokens[s]

        def project(self, places, *blocks):
            count = len(blocks)
            merged = join(blocks)
            some = slice(places.start * rows, places.stop * rows)
            hidden, queries, pairs = project(
                merged, gain, qkv_weight, cosine[some], sine[some], rows
            )
            pairs = pairs.reshape(count, rows, 2 * HEAD_DIM)
            queries = queries.reshape(count, rows, query_width)
            return merged, hidden, queries, pairs, line.swap(pairs)

        def attend(self, *halves):
            queries, own, other = halves[0::3], halves[1::3], halves[2::3]
            attended = attend_forward(infos[self.s], queries, own, other, spans)
            attended = attended.reshape(every, query_width)
            return nn(attended, out_weight).astype(bf16), attended, queries, own, other

        def after_branch(self, terms):
            self.branch, self.middle, hidden = norm_call(
                branch_kernel, terms, (tokens,), gain, self.s, (f32, f32, bf16)
            )
            return hidden

        def feed(self, *blocks):
            hidden_ff = join(blocks)
            return (hidden_ff,) + tuple(gate_up(hidden_ff, gate_rows, up_rows))

        def feed_down(self, product):
            return (mix([product], [down_rows]),)

        def after_feed(self, terms):
            self.output, low, self.postfeed_term = norm_call(
                feed_kernel, terms, (self.middle, cotangent), gain, self.s, (bf16, bf16, None)
            )
            return low

        def feed_back(self, gelu, slope, *blocks):
            feed_low = join(blocks)
            return (feed_low,) + tuple(feed_back(feed_low, down_rows, gelu, slope))

        def feed_in(self, gate_back, up_back):
            return (mix([gate_back, up_back], [gate_rows, up_rows]),)

        def after_feed_back(self, terms):
            self.middle_grad, low, self.prefeed_term, self.attended_term = norm_call(
                feed_back_norm_kernel,
                terms,
                (self.middle, self.branch, cotangent),
                gain,
                self.s,
                (f32, bf16, None, None),
            )
            return low

        def attend_back(self, *blocks):
            branch_low = join(blocks)
            mixed = nt(branch_low, out_weight).astype(bf16).reshape(chips, rows, query_width)
            return (branch_low,) + tuple(
                attend_backward(
                    infos[self.s], self.queries, self.pairs, self.others, mixed, tables, spans
                )
            )

        def project_back(self, near_tokens, far_tokens, query_back, own, other):
            got = line.swap(other)
            return project_back(
                query_back.reshape(every, query_width),
                own.reshape(every, 2 * HEAD_DIM),
                got.reshape(every, 2 * HEAD_DIM),
                qkv_weight,
                near_tokens,
                far_tokens,
                rows,
            )

        def after_project_back(self, terms):
            grad = total(terms)
            values = self.own.astype(f32)
            root = inverse_root(values)
            return (self.middle_grad + norm_backward(values * root, root, gain[0:1], grad)).astype(
                bf16
            )

    def weight_grad(left_count, *pieces):
        return (tn(join(pieces[:left_count]), join(pieces[left_count:])).astype(bf16),)

    data = lax.axis_size("dp")

    def data_sum(values, order):
        groups = [[(i + order) % data for i in range(data)]]
        return lax.psum(values, "dp", axis_index_groups=groups)

    near, far = slice(0, 2), slice(2, chips)

    a, b = (Sequence(s) for s in range(seq_count))

    ex = Exchange(line, jnp.concatenate([a.own, gains_rows]), sums=False)
    def attention_weights(query_w, key_w, value_w):
        return jnp.concatenate([pair_rows(query_w), group_rows(key_w), group_rows(value_w)])

    ex.step()
    qkv_weight = ex.step(attention_weights, (query_weight, key_weight, value_weight))
    out_weight, gate_rows = ex.step(
        lambda out_w, gate_w: (pair_rows(out_w), both_rows(gate_w)), (output_weight, gate_weight)
    )
    for _ in range(chips - 4):
        ex.step()
    blocks = ex.near() + ex.far()
    gain = jnp.stack([block[rows, : 4 * count] for block in blocks])
    gain_other = line.swap(gain)
    gain = jnp.stack(
        [jnp.where(c == 0, gain, gain_other), jnp.where(c == 0, gain_other, gain)], axis=1
    ).reshape(chips, 8 * count)
    gain = line.exchanged([gain[k] for k in range(chips)])
    gain = jnp.roll(jnp.stack(gain), z, axis=0).reshape(chips, 2, 4, count)
    gain = gain.transpose(2, 0, 1, 3).reshape(4, width).astype(f32)

    def a_attention(*blocks):
        halves = [a.project(near, *blocks[near]), a.project(far, *blocks[far])]
        out, *kept = a.attend(*halves[0][2:], *halves[1][2:])
        return out, kept, [[half[i] for half in halves] for i in range(2)]

    ex = Exchange(line, b.own)
    out, (a.attended, a.queries, a.pairs, a.others), (a.tokens, a.hidden) = ex.step(
        a_attention, [block[:rows] for block in blocks]
    )
    ex.give(out)

    def b_project_near(up_w, *blocks):
        return b.project(near, *blocks), both_rows(up_w)

    b_near, up_rows = ex.step(b_project_near, [up_weight] + ex.near())
    down_rows = ex.step(both_rows, (down_weight,))
    for _ in range(chips - 4):
        ex.step()
    b_far = ex.step(functools.partial(b.project, far), ex.far())
    b.tokens, b.hidden = ([b_near[i], b_far[i]] for i in range(2))
    hidden_a = a.after_branch(ex.terms())

    def feed_phase(x, own, first, inputs):
        ex = Exchange(line, own)
        firsts = ex.step(first, inputs)
        yield firsts, ex
        hidden, product, gelu, slope = ex.step(x.feed, ex.near())
        (out,) = ex.step(x.feed_down, (product,))
        for _ in range(chips - 4):
            ex.step()
        x.out_near = out
        lasts = ex.step(x.feed, ex.far())
        x.hidden_ff, x.product, x.gelu, x.slope = (
            [u, v] for u, v in zip((hidden, product, gelu, slope), lasts)
        )
        yield lasts, ex

    steps = feed_phase(a, hidden_a, b.attend, b_near[2:] + b_far[2:])
    (out, b.attended, b.queries, b.pairs, b.others), ex = next(steps)
    ex.give(out)
    next(steps)
    hidden_b = b.after_branch(ex.terms())

    steps = feed_phase(b, hidden_b, a.feed_down, (a.product[1],))
    (out,), ex = next(steps)
    ex.give(a.out_near, out)
    next(steps)
    low_a = a.after_feed(ex.terms())

    def back_phase(x, own, first, inputs):
        ex = Exchange(line, own)
        firsts = ex.step(first, inputs)
        yield firsts, ex
        low, gate_back, up_back = ex.step(
            functools.partial(x.feed_back, x.gelu[0], x.slope[0]), ex.near()
        )
        (x.out_near,) = ex.step(x.feed_in, (gate_back, up_back))
        for _ in range(chips - 4):
            ex.step()

        lasts = ex.step(functools.partial(x.feed_back, x.gelu[1], x.slope[1]), ex.far())
        x.feed_low, x.gate_back, x.up_back = (
            [u, v] for u, v in zip((low, gate_back, up_back), lasts)
        )
        yield lasts, ex

    steps = back_phase(a, low_a, b.feed_down, (b.product[1],))
    (out,), ex = next(steps)
    ex.give(b.out_near, out)
    next(steps)
    low_b = b.after_feed(ex.terms())

    def grad_part(left, right):
        return tn(join(left), join(right)).astype(bf16)

    def grad_other(left, right, part):
        count = left.shape[1] // 2
        return (tn(left[:, count:], right) + part[count:].astype(f32)).astype(bf16)

    def grad_own(left, right, part, other):
        count = left.shape[1] // 2
        got = line.swap(other).astype(f32)
        return (tn(left[:, :count], right) + part[:count].astype(f32) + got).astype(bf16)

    ex = Exchange(line, low_b)
    (out,) = ex.step(a.feed_in, (a.gate_back[1], a.up_back[1]))
    ex.give(a.out_near, out)

    def part_work(*pieces):
        return grad_part(pieces[:2], pieces[2:4]), grad_part(pieces[4:6], pieces[6:])

    part_down, part_gate = ex.step(
        part_work, a.product + a.feed_low + a.gate_back + a.hidden_ff
    )

    def part_more(*pieces):
        return (grad_part(pieces[:2], pieces[2:4]),) + tuple(
            join(pieces[i : i + 2]) for i in range(4, 12, 2)
        )

    part_up, b_gelu, b_slope, b_product, b_hidden_ff = ex.step(
        part_more, a.up_back + a.hidden_ff + b.gelu + b.slope + b.product + b.hidden_ff
    )
    for _ in range(chips - 4):
        ex.step()

    def b_feed_back(part, *blocks):
        low, gate_back, up_back = b.feed_back(b_gelu, b_slope, *blocks)
        return low, gate_back, up_back, grad_other(b_product, low, part)

    b_low, b_gate_back, b_up_back, down_other = ex.step(
        b_feed_back, [part_down] + ex.near() + ex.far()
    )
    branch_a = a.after_feed_back(ex.terms())

    def b_feed_in(gate_back, up_back, down_other):
        return b.feed_in(gate_back, up_back) + (
            grad_other(gate_back, b_hidden_ff, part_gate),
            grad_own(b_product, b_low, part_down, down_other),
        )

    ex = Exchange(line, branch_a)
    out, gate_other, down_grad = ex.step(b_feed_in, (b_gate_back, b_up_back, down_other))
    ex.give(out)

    def gate_work(gate_back, up_back, gate_other):
        return (
            grad_other(up_back, b_hidden_ff, part_up),
            grad_own(gate_back, b_hidden_ff, part_gate, gate_other),
        )

    up_other, gate_grad = ex.step(gate_work, (b_gate_back, b_up_back, gate_other))

    def up_work(up_back, up_other):
        return (grad_own(up_back, b_hidden_ff, part_up, up_other),)

    (up_grad,) = ex.step(up_work, (b_up_back, up_other))
    early_sums = data_sum((down_grad, gate_grad), 0)
    up_sum = data_sum(up_grad, 1)
    for _ in range(chips - 4):
        ex.step()
    a.branch_low, *a_sums = ex.step(a.attend_back, ex.near() + ex.far())
    branch_b = b.after_feed_back(ex.terms())

    ex = Exchange(line, branch_b)
    out, a.back, a.inbound_term = ex.step(a.project_back, a.tokens + a_sums)
    ex.give(out)
    ex.step()
    ex.step()
    for _ in range(chips - 4):
        ex.step()
    b.branch_low, *b_sums = ex.step(b.attend_back, ex.near() + ex.far())
    tokens_grad_a = a.after_project_back(ex.terms())

    grad, b.back, b.inbound_term = b.project_back(*b.tokens, *b_sums)
    gain_terms = jnp.concatenate(
        [
            a.inbound_term + b.inbound_term,
            a.attended_term + b.attended_term,
            a.prefeed_term + b.prefeed_term,
            a.postfeed_term + b.postfeed_term,
        ]
    ).astype(bf16)
    gain_terms = gain_terms.reshape(4, chips, 2, count).transpose(1, 2, 0, 3)
    gain_terms = jnp.roll(gain_terms.reshape(chips, 1, 8 * count), -z, axis=0)
    gain_terms = jnp.stack(line.exchanged([gain_terms[k] for k in range(chips)]))
    gain_terms = jnp.pad(gain_terms, ((0, 0), (0, pad - 1), (0, width - 8 * count)))
    ex = Exchange(line)
    ex.parts = [jnp.concatenate([part, gain_terms[k]]) for k, part in enumerate(split(grad))]
    ex.first = ex.parts[0]

    def attention_grads(back_a, back_b):
        return weight_grad(2, back_a, back_b, *a.hidden, *b.hidden) + weight_grad(
            2, a.attended, b.attended, a.branch_low, b.branch_low
        )

    def attention_sums(qkv_grad, output_grad):
        return tuple(
            value.astype(bf16)
            for value in (
                pair_sum(qkv_grad[:query_width]),
                group_sum(qkv_grad[query_width : query_width + HEAD_DIM]),
                group_sum(qkv_grad[query_width + HEAD_DIM :]),
                pair_sum(output_grad),
            )
        )

    late = ex.step(attention_grads, (a.back, b.back), held=early_sums)
    down_sum, gate_sum = ex.held

    def sums_work(down_sum, gate_sum, *late):
        return attention_sums(*late), down_sum.astype(f32), gate_sum.astype(f32)

    late, down_sum, gate_sum = ex.step(sums_work, (down_sum, gate_sum, *late))
    for _ in range(chips - 4):
        ex.step()
    ex.step(held=(up_sum,))
    (up_sum,) = ex.held
    late_sums = data_sum(late, 2)
    grad = total(ex.terms())
    tokens_grad_b = b.after_project_back([grad[:rows]])

    row = grad[rows, : 8 * count].reshape(2, 4, count)
    mine = jnp.where(c == 0, row[0], row[1])
    other = jnp.where(c == 0, row[1], row[0])
    gain_sums = lax.psum(mine + line.swap(other.astype(bf16)).astype(f32), "dp")

    done = tied(
        jnp.stack([a.output, b.output]),
        jnp.stack([tokens_grad_a, tokens_grad_b]),
        gate_sum,
        up_sum.astype(f32),
        down_sum,
        gain_sums,
        late_sums,
    )
    late_sums = [value.astype(f32) for value in done[6]]
    return (*done[:2], *late_sums, *done[2:5], *done[5])


def solution(mesh):
    rows = P("ctx", None)
    gain = P("ctx")
    tokens = P("dp", "ctx", None)
    spans = P("dp", None)
    return jax.shard_map(
        on_device,
        mesh=mesh,
        in_specs=(tokens, spans, spans) + (rows,) * 7 + (gain,) * 4 + (tokens,),
        out_specs=(tokens, tokens) + (rows,) * 7 + (gain,) * 4,
        check_vma=False,
    )
```

```python
import functools

import jax
import jax.numpy as jnp
from jax import lax
from jax.experimental import pallas as pl
from jax.experimental.pallas import tpu as pltpu
from jax.sharding import PartitionSpec as P

HEADS = 8
KV_HEADS = 4
HEAD_DIM = 256
HALF = HEAD_DIM // 2

epsilon = 1e-06
soft_cap = 50.0
rope_base = 10000.0
gelu_a = 0.7978845608028654
gelu_b = 0.044715
query_scale = HEAD_DIM ** (-0.5)

bf16 = jnp.bfloat16
f32 = jnp.float32


def nt(left_side, right_side):
    return lax.dot_general(
        left_side, right_side, (((1,), (1,)), ((), ())), preferred_element_type=f32
    )


def nn(left_side, right_side):
    return lax.dot_general(
        left_side, right_side, (((1,), (0,)), ((), ())), preferred_element_type=f32
    )


def tn(left_side, right_side):
    return lax.dot_general(
        left_side, right_side, (((0,), (0,)), ((), ())), preferred_element_type=f32
    )


def inverse_root(values):
    return lax.rsqrt(jnp.mean(values * values, axis=-1, keepdims=True) + epsilon)


def norm_backward(normed, root, gain, grad):
    scaled = grad * gain
    return root * (scaled - normed * jnp.mean(scaled * normed, axis=-1, keepdims=True))


class Line:
    def __init__(self, size, index):
        self.chips = size // 2
        self.z = index // 2
        self.c = index % 2
        self.core_pairs = [(i, i ^ 1) for i in range(size)]

    def pairs(self, step, low, high):
        return [
            (2 * z + c, 2 * (z + step) + c)
            for z in range(low, high)
            for c in range(2)
            if 0 <= z + step < self.chips
        ]

    def right(self, block, low, high):
        return lax.ppermute(block, "ctx", self.pairs(1, low, high))

    def left(self, block, low, high):
        n = self.chips
        return lax.ppermute(block, "ctx", self.pairs(-1, n - high, n - low))

    def swap(self, block):
        return lax.ppermute(block, "ctx", self.core_pairs)

    def exchanged(self, items):
        last = self.z == self.chips - 1
        items = list(items)
        first, final = items[1], items[-1]
        items[1] = jnp.where(last, final, first)
        items[-1] = jnp.where(last, first, final)
        return items

    def table(self):
        order = self.exchanged([jnp.int32(k) for k in range(self.chips)])
        return [lax.rem(self.z + k, self.chips) for k in order]


def tied(*values):
    return lax.optimization_barrier(values)


class Exchange:
    def __init__(self, line, own=None, sums=True):
        self.line, self.own, self.sums = line, own, sums
        self.parts = None
        self.s = 0
        self.from_left, self.from_right = [own], [own]
        self.sum_left = self.sum_right = None

    def step(self, work=None, inputs=(), held=()):
        line, n, z = self.line, self.line.chips, self.line.z
        gathers = self.own is not None
        self.s += 1
        s = self.s
        to_right = to_left = None
        low, high = 0, n
        if gathers and s <= n - 1:
            to_right, to_left = self.from_left[s - 1], self.from_right[s - 1]
            low = s - 1
        j = s - 1 if gathers else s
        if self.sums and j >= 1:
            sum_r, sum_l = self.parts[n - j], self.parts[n - 1 if j == 1 else j]
            if j == n - 1:
                sum_l = jnp.where(z == n - 1, self.parts[1], self.parts[n - 1])
            if self.sum_left is not None:
                sum_r = (sum_r.astype(f32) + self.sum_left.astype(f32)).astype(bf16)
                sum_l = (sum_l.astype(f32) + self.sum_right.astype(f32)).astype(bf16)
            if to_right is None:
                to_right, to_left, high = sum_r, sum_l, j
            else:
                to_right = jnp.where(z >= s - 1, to_right, sum_r)
                to_left = jnp.where(n - 1 - z >= s - 1, to_left, sum_l)
                low = 0
        to_right, to_left, inputs, self.held = tied(to_right, to_left, inputs, held)
        got_left = line.right(to_right, low, high)
        got_right = line.left(to_left, low, high)
        outs = work(*inputs) if work is not None else ()
        got_left, got_right, outs = tied(got_left, got_right, outs)
        if gathers and s <= n - 1:
            self.from_left.append(got_left)
            self.from_right.append(got_right)
        if self.sums and j >= 1:
            self.sum_left, self.sum_right = got_left, got_right
        return outs

    def give(self, *halves):
        rows = halves[-1].shape[0] // (self.line.chips if len(halves) == 1 else self.line.chips - 2)
        self.first = halves[0]
        self.parts = [
            half[k * rows : (k + 1) * rows]
            for half in halves
            for k in range(half.shape[0] // rows)
        ]

    def near(self):
        last = self.line.z == self.line.chips - 1
        return [self.own, jnp.where(last, self.from_left[1], self.from_right[1])]

    def far(self):
        n, z = self.line.chips, self.line.z
        blocks = [
            jnp.where(z + k < n, self.from_right[k], self.from_left[n - k])
            for k in range(2, n - 1)
        ]
        final = jnp.where(z == 0, self.from_right[n - 1], self.from_left[1])
        return blocks + [jnp.where(z == n - 1, self.from_left[n - 1], final)]

    def terms(self):
        return (self.first, self.sum_left, self.sum_right)


def total(terms):
    rows = terms[-1].shape[0]
    return sum(t[:rows].astype(f32) for t in terms)


def spans_of(place, info, spans, none):
    label = jnp.full(place.shape, none, jnp.int32)
    for s in range(spans):
        start, stop = info[1 + s], info[1 + spans + s]
        label = jnp.where((place >= start) & (place < stop), s, label)
    return label


def seen_block(query_block, key_block, width, info, spans):
    seen = key_block <= query_block
    for s in range(spans):
        start, stop = info[1 + s], info[1 + spans + s]
        seen = seen | ((start < (query_block + 1) * width) & (stop > key_block * width))
    return seen


def block_mask(query_block, key_block, rows, info, spans):
    c = info[0]
    width = 2 * rows
    query_place = (
        query_block * width + c * rows + lax.broadcasted_iota(jnp.int32, (rows, 1), 0)
    )
    j = lax.broadcasted_iota(jnp.int32, (1, width), 1)
    key_place = key_block * width + j + jnp.where(j < rows, c * rows, -c * rows)
    query_span = spans_of(query_place, info, spans, -2)
    key_span = spans_of(key_place, info, spans, -1)
    return (key_place <= query_place) | (key_span == query_span)


def place_of(refs, kk):
    return refs[0][kk] if kk < 2 else refs[1][kk - 2]


def key_block_of(own_refs, other_refs, kk, part):
    cut = slice(part * HEAD_DIM, (part + 1) * HEAD_DIM)
    return jnp.concatenate([place_of(own_refs, kk)[:, cut], place_of(other_refs, kk)[:, cut]])


def forward_kernel(spans, heads, info, *refs):
    queries, own, other = refs[0:2], refs[2:4], refs[4:6]
    o_ref, acc_ref, sum_ref = refs[6:]
    rows = own[0].shape[1]
    chips = own[0].shape[0] + own[1].shape[0]
    width = 2 * rows
    query_block = info[1 + 2 * spans + pl.program_id(0)]
    query = jnp.where(pl.program_id(0) < 2, queries[0][0], queries[1][0])
    acc_ref[...] = jnp.zeros_like(acc_ref)
    sum_ref[...] = jnp.zeros_like(sum_ref)
    for kk in range(chips):
        key_block = info[1 + 2 * spans + kk]

        @pl.when(seen_block(query_block, key_block, width, info, spans))
        def _():
            allowed = block_mask(query_block, key_block, rows, info, spans)
            keys, values = (key_block_of(own, other, kk, part) for part in range(2))
            for h in range(heads):
                scores = nt(query[:, h * HEAD_DIM : (h + 1) * HEAD_DIM], keys)
                weights = jnp.where(
                    allowed, jnp.exp(soft_cap * jnp.tanh(scores * (1.0 / soft_cap))), 0.0
                )
                sum_ref[h] += jnp.sum(weights, axis=1, keepdims=True)
                acc_ref[h] += nn(weights.astype(bf16), values)

    for h in range(heads):
        o_ref[0, :, h * HEAD_DIM : (h + 1) * HEAD_DIM] = (acc_ref[h] / sum_ref[h]).astype(bf16)


def turned_back(vectors, cosine, sine):
    first, second = vectors[:, :HALF], vectors[:, HALF:]
    return first * cosine + second * sine, second * cosine - first * sine


def backward_kernel(spans, heads, info, *refs):
    queries, own, other = refs[0:2], refs[2:4], refs[4:6]
    g_ref, cos_ref, sin_ref, tables = refs[6], refs[7], refs[8], refs[9:13]
    dq_ref, own_ref, other_ref = refs[13:16]
    dk_ref, dv_ref, p_ref, r_ref, t_ref, sum_ref, inner_ref, acc_ref = refs[16:]
    chips, width, _ = dk_ref.shape
    rows = width // 2
    query_block = info[1 + 2 * spans + pl.program_id(0)]
    query = jnp.where(pl.program_id(0) < 2, queries[0][0], queries[1][0])

    @pl.when(pl.program_id(0) == 0)
    def _():
        dk_ref[...] = jnp.zeros_like(dk_ref)
        dv_ref[...] = jnp.zeros_like(dv_ref)

    acc_ref[...] = jnp.zeros_like(acc_ref)
    sum_ref[...] = jnp.zeros_like(sum_ref)
    inner_ref[...] = jnp.zeros_like(inner_ref)
    for kk in range(chips):
        key_block = info[1 + 2 * spans + kk]

        @pl.when(seen_block(query_block, key_block, width, info, spans))
        def _():
            allowed = block_mask(query_block, key_block, rows, info, spans)
            keys, values = (key_block_of(own, other, kk, part) for part in range(2))
            for h in range(heads):
                head = slice(h * HEAD_DIM, (h + 1) * HEAD_DIM)
                squashed = jnp.tanh(nt(query[:, head], keys) * (1.0 / soft_cap))
                weights = jnp.where(allowed, jnp.exp(soft_cap * squashed), 0.0)
                row_grad = nt(g_ref[0, :, head], values)
                sum_ref[h] += jnp.sum(weights, axis=1, keepdims=True)
                inner_ref[h] += jnp.sum(weights * row_grad, axis=1, keepdims=True)
                p_ref[kk, h] = weights
                r_ref[kk, h] = row_grad
                t_ref[kk, h] = 1.0 - squashed * squashed

    for kk in range(chips):
        key_block = info[1 + 2 * spans + kk]

        @pl.when(seen_block(query_block, key_block, width, info, spans))
        def _():
            keys = key_block_of(own, other, kk, 0)
            for h in range(heads):
                head = slice(h * HEAD_DIM, (h + 1) * HEAD_DIM)
                inverse = 1.0 / sum_ref[h]
                weights = p_ref[kk, h] * inverse
                inner = inner_ref[h] * inverse
                score_grad = (weights * (r_ref[kk, h] - inner) * t_ref[kk, h]).astype(bf16)
                acc_ref[h] += nn(score_grad, keys)
                dk_ref[kk] += tn(score_grad, query[:, head])
                dv_ref[kk] += tn(weights.astype(bf16), g_ref[0, :, head])

    for h in range(heads):
        first, second = turned_back(acc_ref[h], cos_ref[0], sin_ref[0])
        dq_ref[0, :, h * HEAD_DIM : h * HEAD_DIM + HALF] = (first * query_scale).astype(bf16)
        dq_ref[0, :, h * HEAD_DIM + HALF : (h + 1) * HEAD_DIM] = (second * query_scale).astype(bf16)

    @pl.when(pl.program_id(0) == chips - 1)
    def _():
        for kk in range(chips):
            for part, out in ((0, own_ref), (1, other_ref)):
                some = slice(part * rows, (part + 1) * rows)
                first, second = turned_back(
                    dk_ref[kk, some], tables[2 * part][kk], tables[2 * part + 1][kk]
                )
                out[kk, :, :HALF] = first.astype(out.dtype)
                out[kk, :, HALF:HEAD_DIM] = second.astype(out.dtype)
                out[kk, :, HEAD_DIM:] = dv_ref[kk, some].astype(out.dtype)


def block_spec(shape):
    return pl.BlockSpec((1,) + tuple(shape[1:]), lambda i, info: (i, 0, 0))


def near_spec(shape):
    return pl.BlockSpec((1,) + tuple(shape[1:]), lambda i, info: (jnp.minimum(i, 1), 0, 0))


def far_spec(shape):
    return pl.BlockSpec((1,) + tuple(shape[1:]), lambda i, info: (jnp.maximum(i - 2, 0), 0, 0))


def whole_spec(shape):
    return pl.BlockSpec(tuple(shape), lambda i, info: (0,) * len(shape))


light = pl.CostEstimate(flops=1024, bytes_accessed=1024, transcendentals=0)


def attend_forward(info, queries, own, other, spans):
    (near, rows, features), far = queries[0].shape, queries[1].shape[0]
    chips, heads = near + far, features // HEAD_DIM
    arrays = (*queries, *own, *other)
    out = jax.ShapeDtypeStruct((chips, rows, features), bf16)
    return pl.pallas_call(
        functools.partial(forward_kernel, spans, heads),
        out_shape=out,
        grid_spec=pltpu.PrefetchScalarGridSpec(
            num_scalar_prefetch=1,
            grid=(chips,),
            in_specs=[near_spec(queries[0].shape), far_spec(queries[1].shape)]
            + [whole_spec(x.shape) for x in arrays[2:]],
            out_specs=block_spec(out.shape),
            scratch_shapes=[
                pltpu.VMEM((heads, rows, HEAD_DIM), f32),
                pltpu.VMEM((heads, rows, 1), f32),
            ],
        ),
        compiler_params=pltpu.CompilerParams(vmem_limit_bytes=20 * 1024 * 1024),
        cost_estimate=light,
    )(info, *arrays)


def attend_backward(info, queries, own, other, grads, tables, spans):
    chips, rows, features = grads.shape
    heads = features // HEAD_DIM
    arrays = (*queries, *own, *other, grads, tables[0], tables[1], *tables)
    square = pltpu.VMEM((chips, heads, rows, 2 * rows), f32)
    pairs = (chips, rows, 2 * HEAD_DIM)
    return pl.pallas_call(
        functools.partial(backward_kernel, spans, heads),
        out_shape=(
            jax.ShapeDtypeStruct(grads.shape, bf16),
            jax.ShapeDtypeStruct(pairs, f32),
            jax.ShapeDtypeStruct(pairs, bf16),
        ),
        grid_spec=pltpu.PrefetchScalarGridSpec(
            num_scalar_prefetch=1,
            grid=(chips,),
            in_specs=[near_spec(queries[0].shape), far_spec(queries[1].shape)]
            + [whole_spec(x.shape) for x in arrays[2:6]]
            + [block_spec(x.shape) for x in arrays[6:9]]
            + [whole_spec(x.shape) for x in arrays[9:]],
            out_specs=(block_spec(grads.shape), whole_spec(pairs), whole_spec(pairs)),
            scratch_shapes=[
                pltpu.VMEM((chips, 2 * rows, HEAD_DIM), f32),
                pltpu.VMEM((chips, 2 * rows, HEAD_DIM), f32),
                square,
                square,
                square,
                pltpu.VMEM((heads, rows, 1), f32),
                pltpu.VMEM((heads, rows, 1), f32),
                pltpu.VMEM((heads, rows, HEAD_DIM), f32),
            ],
        ),
        compiler_params=pltpu.CompilerParams(vmem_limit_bytes=30 * 1024 * 1024),
        cost_estimate=light,
    )(info, *arrays)


def row_call(kernel, grid, ins, outs, *arrays):
    return pl.pallas_call(
        kernel,
        out_shape=tuple(out[0] for out in outs),
        grid=(grid,),
        in_specs=[pl.BlockSpec(*spec) for spec in ins],
        out_specs=tuple(pl.BlockSpec(*out[1:]) for out in outs),
        compiler_params=pltpu.CompilerParams(vmem_limit_bytes=24 * 1024 * 1024),
        cost_estimate=light,
    )(*arrays)


def add_rows(ref, rows):
    @pl.when(pl.program_id(0) == 0)
    def _():
        ref[...] = jnp.zeros_like(ref)

    ref[...] += jnp.sum(rows, axis=0, keepdims=True)


def summed(refs):
    return sum(ref[...].astype(f32) for ref in refs)


def project_kernel(heads, x_ref, gain_ref, w_ref, cos_ref, sin_ref, hidden_ref, q_ref, kv_ref):
    values = x_ref[...].astype(f32)
    hidden = (values * inverse_root(values) * gain_ref[0:1]).astype(bf16)
    hidden_ref[...] = hidden
    raw = nt(hidden, w_ref[...])
    cosine, sine = cos_ref[...], sin_ref[...]
    for h in range(heads + 1):
        start = h * HEAD_DIM
        first, second = raw[:, start : start + HALF], raw[:, start + HALF : start + HEAD_DIM]
        turned = first * cosine - second * sine, second * cosine + first * sine
        if h < heads:
            q_ref[:, start : start + HALF] = (turned[0] * query_scale).astype(bf16)
            q_ref[:, start + HALF : start + HEAD_DIM] = (turned[1] * query_scale).astype(bf16)
        else:
            kv_ref[:, :HALF] = turned[0].astype(bf16)
            kv_ref[:, HALF:HEAD_DIM] = turned[1].astype(bf16)
    kv_ref[:, HEAD_DIM:] = raw[:, (heads + 1) * HEAD_DIM :].astype(bf16)


def project(tokens, gains, weight, cosine, sine, rows):
    m, width = tokens.shape
    features = weight.shape[0] - 2 * HEAD_DIM
    whole = lambda i: (0, 0)
    block = lambda i: (i, 0)
    return row_call(
        functools.partial(project_kernel, features // HEAD_DIM),
        m // rows,
        [
            ((rows, width), block),
            (gains.shape, whole),
            (weight.shape, whole),
            ((rows, HALF), block),
            ((rows, HALF), block),
        ],
        [
            (jax.ShapeDtypeStruct((m, n), bf16), (rows, n), block)
            for n in (width, features, 2 * HEAD_DIM)
        ],
        tokens,
        gains,
        weight,
        cosine,
        sine,
    )


def project_back_kernel(dq_ref, own_ref, got_ref, w_ref, near_ref, far_ref, *outs):
    grad_ref, back_ref, inbound_ref = outs
    pairs = (own_ref[...] + got_ref[...].astype(f32)).astype(bf16)
    back = jnp.concatenate([dq_ref[...], pairs], axis=1)
    back_ref[...] = back
    grad = nn(back, w_ref[...])
    grad_ref[...] = grad.astype(bf16)
    values = jnp.where(pl.program_id(0) < 2, near_ref[...], far_ref[...]).astype(f32)
    add_rows(inbound_ref, grad * (values * inverse_root(values)))


def project_back(query_back, own, got, weight, near, far, rows):
    m, features = query_back.shape
    count, width = weight.shape
    block = lambda i: (i, 0)
    whole = lambda i: (0, 0)
    pairs = ((rows, 2 * HEAD_DIM), block)
    return row_call(
        project_back_kernel,
        m // rows,
        [
            ((rows, features), block),
            pairs,
            pairs,
            (weight.shape, whole),
            ((rows, width), lambda i: (jnp.minimum(i, 1), 0)),
            ((rows, width), lambda i: (jnp.maximum(i - 2, 0), 0)),
        ],
        [
            (jax.ShapeDtypeStruct((m, width), bf16), (rows, width), block),
            (jax.ShapeDtypeStruct((m, count), bf16), (rows, count), block),
            (jax.ShapeDtypeStruct((1, width), f32), (1, width), whole),
        ],
        query_back,
        own,
        got,
        weight,
        near,
        far,
    )


def branch_kernel(p_ref, l_ref, r_ref, own_ref, gain_ref, branch_ref, middle_ref, hidden_ref):
    branch = summed((p_ref, l_ref, r_ref))
    branch_ref[...] = branch
    middle = own_ref[...].astype(f32) + branch * inverse_root(branch) * gain_ref[1:2]
    middle_ref[...] = middle
    hidden_ref[...] = (middle * inverse_root(middle) * gain_ref[2:3]).astype(bf16)


def feed_kernel(p_ref, l_ref, r_ref, middle_ref, cot_ref, gain_ref, out_ref, low_ref, term_ref):
    feed = summed((p_ref, l_ref, r_ref))
    root = inverse_root(feed)
    normed = feed * root
    gain = gain_ref[3:4]
    upstream = cot_ref[...].astype(f32)
    out_ref[...] = (middle_ref[...] + normed * gain).astype(bf16)
    low_ref[...] = norm_backward(normed, root, gain, upstream).astype(bf16)
    add_rows(term_ref, upstream * normed)


def feed_back_norm_kernel(p_ref, l_ref, r_ref, middle_ref, branch_ref, cot_ref, gain_ref, *outs):
    grad_ref, low_ref, prefeed_ref, attended_ref = outs
    grad = summed((p_ref, l_ref, r_ref))
    middle = middle_ref[...]
    root = inverse_root(middle)
    normed = middle * root
    add_rows(prefeed_ref, grad * normed)
    middle_grad = cot_ref[...].astype(f32) + norm_backward(normed, root, gain_ref[2:3], grad)
    grad_ref[...] = middle_grad
    branch = branch_ref[...]
    root = inverse_root(branch)
    normed = branch * root
    add_rows(attended_ref, middle_grad * normed)
    low_ref[...] = norm_backward(normed, root, gain_ref[1:2], middle_grad).astype(bf16)


def norm_call(kernel, terms, arrays, gains, sequence, outs):
    rows, width = terms[1].shape
    tile = rows // 2
    block = ((tile, width), lambda i: (i, 0))
    one = ((None, tile, width), lambda i: (sequence, i, 0))
    whole = lambda i: (0, 0)
    return row_call(
        kernel,
        2,
        [block] * 3 + [one if x.ndim == 3 else block for x in arrays] + [(gains.shape, whole)],
        [
            (jax.ShapeDtypeStruct((1, width), f32), (1, width), whole)
            if kind is None
            else (jax.ShapeDtypeStruct((rows, width), kind), *block)
            for kind in outs
        ],
        *terms,
        *arrays,
        gains,
    )


def gate_up_kernel(h_ref, gate_ref, up_ref, product_ref, gelu_ref, slope_ref):
    gate = nt(h_ref[...], gate_ref[...])
    up = nt(h_ref[...], up_ref[...])
    square = gate * gate
    tanh = jnp.tanh(gate * (gelu_a + (gelu_a * gelu_b) * square))
    half = 0.5 + 0.5 * tanh
    gelu = gate * half
    slope = half + gate * (0.5 - 0.5 * tanh * tanh) * (gelu_a + (3.0 * gelu_a * gelu_b) * square)
    product_ref[...] = (gelu * up).astype(bf16)
    gelu_ref[...] = gelu.astype(bf16)
    slope_ref[...] = (up * slope).astype(bf16)


def gate_up(hidden, gate_w, up_w):
    m, width = hidden.shape
    n = gate_w.shape[0]
    tile = next(t for t in (768, 384, 256, 128) if n % t == 0)
    weight_spec = pl.BlockSpec((tile, width), lambda i: (i, 0))
    out_spec = pl.BlockSpec((m, tile), lambda i: (0, i))
    return pl.pallas_call(
        gate_up_kernel,
        out_shape=(jax.ShapeDtypeStruct((m, n), bf16),) * 3,
        grid=(n // tile,),
        in_specs=[pl.BlockSpec((m, width), lambda i: (0, 0)), weight_spec, weight_spec],
        out_specs=(out_spec,) * 3,
        compiler_params=pltpu.CompilerParams(vmem_limit_bytes=30 * 1024 * 1024),
        cost_estimate=light,
    )(hidden, gate_w, up_w)


def mix_kernel(*refs):
    count = len(refs) // 2
    out = sum(nn(refs[i][...], refs[count + i][...]) for i in range(count))
    refs[-1][...] = out.astype(bf16)


def mix(lefts, weights):
    m, depth = lefts[0].shape
    n = weights[0].shape[1]
    tile = next(t for t in (768, 384, 256, 128) if n % t == 0)
    return pl.pallas_call(
        mix_kernel,
        out_shape=jax.ShapeDtypeStruct((m, n), bf16),
        grid=(n // tile,),
        in_specs=[pl.BlockSpec((m, depth), lambda i: (0, 0))] * len(lefts)
        + [pl.BlockSpec((depth, tile), lambda i: (0, i))] * len(weights),
        out_specs=pl.BlockSpec((m, tile), lambda i: (0, i)),
        compiler_params=pltpu.CompilerParams(vmem_limit_bytes=(26 if m <= 384 else 36) * 1024 * 1024),
        cost_estimate=light,
    )(*lefts, *weights)


def feed_back_kernel(low_ref, down_ref, gelu_ref, slope_ref, gate_back_ref, up_back_ref):
    grad = nt(low_ref[...], down_ref[...])
    gate_back_ref[...] = (grad * slope_ref[...].astype(f32)).astype(bf16)
    up_back_ref[...] = (grad * gelu_ref[...].astype(f32)).astype(bf16)


def feed_back(low, down_w, gelu, slope):
    m, width = low.shape
    n = down_w.shape[0]
    tile = next(t for t in (768, 384, 256, 128) if n % t == 0)
    spec = pl.BlockSpec((m, tile), lambda i: (0, i))
    return pl.pallas_call(
        feed_back_kernel,
        out_shape=(jax.ShapeDtypeStruct((m, n), bf16),) * 2,
        grid=(n // tile,),
        in_specs=[
            pl.BlockSpec((m, width), lambda i: (0, 0)),
            pl.BlockSpec((tile, width), lambda i: (i, 0)),
            spec,
            spec,
        ],
        out_specs=(spec,) * 2,
        compiler_params=pltpu.CompilerParams(vmem_limit_bytes=30 * 1024 * 1024),
        cost_estimate=light,
    )(low, down_w, gelu, slope)


def on_device(
    tokens,
    span_start,
    span_len,
    query_weight,
    key_weight,
    value_weight,
    output_weight,
    gate_weight,
    up_weight,
    down_weight,
    inbound_gain,
    attended_gain,
    prefeed_gain,
    postfeed_gain,
    cotangent,
):
    seq_count, rows, width = tokens.shape
    size = lax.axis_size("ctx")
    index = lax.axis_index("ctx")
    line = Line(size, index)
    chips, z, c = line.chips, line.z, line.c
    spans = span_start.shape[1]
    group = size // KV_HEADS
    member = index % group
    every = chips * rows

    def pair_rows(block):
        other = line.swap(block)
        return jnp.concatenate([jnp.where(c == 0, block, other), jnp.where(c == 0, other, block)])

    def shifted(block, k):
        pairs = [(i, i - i % group + (i % group + k) % group) for i in range(size)]
        return lax.ppermute(block, "ctx", pairs)

    def group_rows(block):
        if group == 2:
            return pair_rows(block)
        count = block.shape[0]
        out = jnp.zeros((group * count, width), block.dtype)
        out = lax.dynamic_update_slice(out, block, (member * count, 0))
        for k in range(1, group):
            place = lax.rem(member + group - k, group) * count
            out = lax.dynamic_update_slice(out, shifted(block, k), (place, 0))
        return out

    def group_sum(grad):
        count = grad.shape[0] // group
        own = lax.dynamic_slice(grad, (member * count, 0), (count, width)).astype(f32)
        for k in range(1, group):
            place = lax.rem(member + k, group) * count
            sent = lax.dynamic_slice(grad, (place, 0), (count, width))
            own = own + shifted(sent.astype(bf16), k).astype(f32)
        return own

    def pair_sum(grad):
        count = grad.shape[0] // 2
        own = lax.dynamic_slice(grad, (c * count, 0), (count, width)).astype(f32)
        sent = lax.dynamic_slice(grad, ((1 - c) * count, 0), (count, width))
        return own + line.swap(sent.astype(bf16)).astype(f32)

    def both_rows(block):
        return jnp.concatenate([block, line.swap(block)])

    count = inbound_gain.shape[0]
    pad = 16
    gains_own = jnp.concatenate([inbound_gain, attended_gain, prefeed_gain, postfeed_gain])
    gains_rows = jnp.pad(gains_own[None, :], ((0, pad - 1), (0, width - 4 * count)))

    query_width = 2 * output_weight.shape[0]
    heads = query_width // HEAD_DIM

    table = jnp.stack(line.table()).astype(jnp.int32)
    places = (
        table[:, None] * (2 * rows) + c * rows + jnp.arange(rows, dtype=jnp.int32)[None, :]
    ).reshape(every)
    inverse = rope_base ** (-(jnp.arange(HALF, dtype=f32) * 2.0 / HEAD_DIM))

    def turns(places):
        angles = places.astype(f32)[:, None] * inverse[None, :]
        return jnp.cos(angles), jnp.sin(angles)

    cosine, sine = turns(places)
    tables = [
        t.reshape(chips, rows, HALF)
        for t in (cosine, sine) + turns(places + jnp.where(c == 0, rows, -rows))
    ]

    def split(block_rows):
        return [
            block_rows[k * rows : (k + 1) * rows] for k in range(block_rows.shape[0] // rows)
        ]

    def join(blocks):
        return jnp.concatenate(blocks)

    infos = [
        jnp.concatenate(
            [c[None], span_start[s], span_start[s] + span_len[s], table]
        ).astype(jnp.int32)
        for s in range(seq_count)
    ]

    class Sequence:
        def __init__(self, s):
            self.s = s
            self.own = tokens[s]

        def project(self, places, *blocks):
            count = len(blocks)
            merged = join(blocks)
            some = slice(places.start * rows, places.stop * rows)
            hidden, queries, pairs = project(
                merged, gain, qkv_weight, cosine[some], sine[some], rows
            )
            pairs = pairs.reshape(count, rows, 2 * HEAD_DIM)
            queries = queries.reshape(count, rows, query_width)
            return merged, hidden, queries, pairs, line.swap(pairs)

        def attend(self, *halves):
            queries, own, other = halves[0::3], halves[1::3], halves[2::3]
            attended = attend_forward(infos[self.s], queries, own, other, spans)
            attended = attended.reshape(every, query_width)
            return nn(attended, out_weight).astype(bf16), attended, queries, own, other

        def after_branch(self, terms):
            self.branch, self.middle, hidden = norm_call(
                branch_kernel, terms, (tokens,), gain, self.s, (f32, f32, bf16)
            )
            return hidden

        def feed(self, *blocks):
            hidden_ff = join(blocks)
            return (hidden_ff,) + tuple(gate_up(hidden_ff, gate_rows, up_rows))

        def feed_down(self, product):
            return (mix([product], [down_rows]),)

        def after_feed(self, terms):
            self.output, low, self.postfeed_term = norm_call(
                feed_kernel, terms, (self.middle, cotangent), gain, self.s, (bf16, bf16, None)
            )
            return low

        def feed_back(self, gelu, slope, *blocks):
            feed_low = join(blocks)
            return (feed_low,) + tuple(feed_back(feed_low, down_rows, gelu, slope))

        def feed_in(self, gate_back, up_back):
            return (mix([gate_back, up_back], [gate_rows, up_rows]),)

        def after_feed_back(self, terms):
            self.middle_grad, low, self.prefeed_term, self.attended_term = norm_call(
                feed_back_norm_kernel,
                terms,
                (self.middle, self.branch, cotangent),
                gain,
                self.s,
                (f32, bf16, None, None),
            )
            return low

        def attend_back(self, *blocks):
            branch_low = join(blocks)
            mixed = nt(branch_low, out_weight).astype(bf16).reshape(chips, rows, query_width)
            return (branch_low,) + tuple(
                attend_backward(
                    infos[self.s], self.queries, self.pairs, self.others, mixed, tables, spans
                )
            )

        def project_back(self, near_tokens, far_tokens, query_back, own, other):
            got = line.swap(other)
            return project_back(
                query_back.reshape(every, query_width),
                own.reshape(every, 2 * HEAD_DIM),
                got.reshape(every, 2 * HEAD_DIM),
                qkv_weight,
                near_tokens,
                far_tokens,
                rows,
            )

        def after_project_back(self, terms):
            grad = total(terms)
            values = self.own.astype(f32)
            root = inverse_root(values)
            return (self.middle_grad + norm_backward(values * root, root, gain[0:1], grad)).astype(
                bf16
            )

    def weight_grad(left_count, *pieces):
        return (tn(join(pieces[:left_count]), join(pieces[left_count:])).astype(bf16),)

    data = lax.axis_size("dp")

    def data_sum(values, order):
        groups = [[(i + order) % data for i in range(data)]]
        return lax.psum(values, "dp", axis_index_groups=groups)

    def swapped(block, bit):
        return lax.ppermute(block, "dp", [(i, i ^ bit) for i in range(data)])

    def data_exchange_sum(value, order):
        if data != 4:
            return data_sum(value, order).astype(f32)
        place = lax.axis_index("dp")
        ways = ((place % 2, 1), (place // 2, 2))

        def reduced(block, way):
            bit_value, bit = way
            half = block.shape[0] // 2
            kept = lax.dynamic_slice(block, (bit_value * half, 0), (half, block.shape[1]))
            sent = lax.dynamic_slice(block, ((1 - bit_value) * half, 0), (half, block.shape[1]))
            return (kept.astype(f32) + swapped(sent, bit).astype(f32)).astype(bf16)

        def gathered(block, way):
            bit_value, bit = way
            got = swapped(block, bit)
            low = bit_value == 0
            return jnp.concatenate([jnp.where(low, block, got), jnp.where(low, got, block)])

        middle = value.shape[1] // 2
        halves = [value[:, :middle], value[:, middle:]]
        orders = [ways, ways[::-1]]
        for step, pick in ((reduced, 0), (reduced, 1), (gathered, 1), (gathered, 0)):
            halves = [step(half, one[pick]) for half, one in zip(halves, orders)]
        return jnp.concatenate(halves, axis=1).astype(f32)

    near, far = slice(0, 2), slice(2, chips)

    a, b = (Sequence(s) for s in range(seq_count))

    ex = Exchange(line, jnp.concatenate([a.own, gains_rows]), sums=False)
    def attention_weights(query_w, key_w, value_w):
        return jnp.concatenate([pair_rows(query_w), group_rows(key_w), group_rows(value_w)])

    gate_other = ex.step(line.swap, (gate_weight,))

    def first_weights(gate_w, gate_other, *attention):
        return attention_weights(*attention), jnp.concatenate([gate_w, gate_other])

    qkv_weight, gate_rows = ex.step(
        first_weights, (gate_weight, gate_other, query_weight, key_weight, value_weight)
    )
    out_weight, up_rows = ex.step(
        lambda out_w, up_w: (pair_rows(out_w), both_rows(up_w)), (output_weight, up_weight)
    )
    for _ in range(chips - 4):
        ex.step()
    blocks = ex.near() + ex.far()
    gain = jnp.stack([block[rows, : 4 * count] for block in blocks])
    gain_other = line.swap(gain)
    gain = jnp.stack(
        [jnp.where(c == 0, gain, gain_other), jnp.where(c == 0, gain_other, gain)], axis=1
    ).reshape(chips, 8 * count)
    gain = line.exchanged([gain[k] for k in range(chips)])
    gain = jnp.roll(jnp.stack(gain), z, axis=0).reshape(chips, 2, 4, count)
    gain = gain.transpose(2, 0, 1, 3).reshape(4, width).astype(f32)

    def a_attention(*blocks):
        halves = [a.project(near, *blocks[near]), a.project(far, *blocks[far])]
        out, *kept = a.attend(*halves[0][2:], *halves[1][2:])
        return out, kept, [[half[i] for half in halves] for i in range(2)]

    ex = Exchange(line, b.own)
    out, (a.attended, a.queries, a.pairs, a.others), (a.tokens, a.hidden) = ex.step(
        a_attention, [block[:rows] for block in blocks]
    )
    ex.give(out)

    b_near = ex.step(functools.partial(b.project, near), ex.near())
    down_rows = ex.step(both_rows, (down_weight,))
    for _ in range(chips - 4):
        ex.step()
    b_far = ex.step(functools.partial(b.project, far), ex.far())
    b.tokens, b.hidden = ([b_near[i], b_far[i]] for i in range(2))
    hidden_a = a.after_branch(ex.terms())

    def feed_phase(x, own, first, inputs):
        ex = Exchange(line, own)
        firsts = ex.step(first, inputs)
        yield firsts, ex
        hidden, product, gelu, slope = ex.step(x.feed, ex.near())
        (out,) = ex.step(x.feed_down, (product,))
        for _ in range(chips - 4):
            ex.step()
        x.out_near = out
        lasts = ex.step(x.feed, ex.far())
        x.hidden_ff, x.product, x.gelu, x.slope = (
            [u, v] for u, v in zip((hidden, product, gelu, slope), lasts)
        )
        yield lasts, ex

    steps = feed_phase(a, hidden_a, b.attend, b_near[2:] + b_far[2:])
    (out, b.attended, b.queries, b.pairs, b.others), ex = next(steps)
    ex.give(out)
    next(steps)
    hidden_b = b.after_branch(ex.terms())

    steps = feed_phase(b, hidden_b, a.feed_down, (a.product[1],))
    (out,), ex = next(steps)
    ex.give(a.out_near, out)
    next(steps)
    low_a = a.after_feed(ex.terms())

    def back_phase(x, own, first, inputs):
        ex = Exchange(line, own)
        firsts = ex.step(first, inputs)
        yield firsts, ex
        low, gate_back, up_back = ex.step(
            functools.partial(x.feed_back, x.gelu[0], x.slope[0]), ex.near()
        )
        (x.out_near,) = ex.step(x.feed_in, (gate_back, up_back))
        for _ in range(chips - 4):
            ex.step()

        lasts = ex.step(functools.partial(x.feed_back, x.gelu[1], x.slope[1]), ex.far())
        x.feed_low, x.gate_back, x.up_back = (
            [u, v] for u, v in zip((low, gate_back, up_back), lasts)
        )
        yield lasts, ex

    steps = back_phase(a, low_a, b.feed_down, (b.product[1],))
    (out,), ex = next(steps)
    ex.give(b.out_near, out)
    next(steps)
    low_b = b.after_feed(ex.terms())

    def grad_part(left, right):
        return tn(join(left), join(right)).astype(bf16)

    def grad_other(left, right, part):
        count = left.shape[1] // 2
        return (tn(left[:, count:], right) + part[count:].astype(f32)).astype(bf16)

    def grad_own(left, right, part, other):
        count = left.shape[1] // 2
        got = line.swap(other).astype(f32)
        return (tn(left[:, :count], right) + part[:count].astype(f32) + got).astype(bf16)

    ex = Exchange(line, low_b)
    (out,) = ex.step(a.feed_in, (a.gate_back[1], a.up_back[1]))
    ex.give(a.out_near, out)

    def part_work(*pieces):
        return grad_part(pieces[:2], pieces[2:4]), grad_part(pieces[4:6], pieces[6:])

    part_down, part_gate = ex.step(
        part_work, a.product + a.feed_low + a.gate_back + a.hidden_ff
    )

    def part_more(*pieces):
        return (grad_part(pieces[:2], pieces[2:4]),) + tuple(
            join(pieces[i : i + 2]) for i in range(4, 12, 2)
        )

    part_up, b_gelu, b_slope, b_product, b_hidden_ff = ex.step(
        part_more, a.up_back + a.hidden_ff + b.gelu + b.slope + b.product + b.hidden_ff
    )
    for _ in range(chips - 4):
        ex.step()

    def b_feed_back(part, *blocks):
        low, gate_back, up_back = b.feed_back(b_gelu, b_slope, *blocks)
        return low, gate_back, up_back, grad_other(b_product, low, part)

    b_low, b_gate_back, b_up_back, down_other = ex.step(
        b_feed_back, [part_down] + ex.near() + ex.far()
    )
    branch_a = a.after_feed_back(ex.terms())

    def b_feed_in(gate_back, up_back, down_other):
        return b.feed_in(gate_back, up_back) + (
            grad_other(gate_back, b_hidden_ff, part_gate),
            grad_own(b_product, b_low, part_down, down_other),
        )

    ex = Exchange(line, branch_a)
    out, gate_other, down_grad = ex.step(b_feed_in, (b_gate_back, b_up_back, down_other))
    ex.give(out)

    def gate_work(gate_back, up_back, gate_other):
        return (
            grad_other(up_back, b_hidden_ff, part_up),
            grad_own(gate_back, b_hidden_ff, part_gate, gate_other),
        )

    up_other, gate_grad = ex.step(gate_work, (b_gate_back, b_up_back, gate_other))

    def up_work(up_back, up_other):
        return (grad_own(up_back, b_hidden_ff, part_up, up_other),)

    (up_grad,) = ex.step(up_work, (b_up_back, up_other))
    early_sums = data_sum((down_grad, gate_grad), 0)
    up_sum = data_sum(up_grad, 1)
    for _ in range(chips - 4):
        ex.step()
    a.branch_low, *a_sums = ex.step(a.attend_back, ex.near() + ex.far())
    branch_b = b.after_feed_back(ex.terms())

    ex = Exchange(line, branch_b)
    out, a.back, a.inbound_term = ex.step(a.project_back, a.tokens + a_sums)
    ex.give(out)
    ex.step()
    ex.step()
    for _ in range(chips - 4):
        ex.step()
    b.branch_low, *b_sums = ex.step(b.attend_back, ex.near() + ex.far())
    tokens_grad_a = a.after_project_back(ex.terms())

    grad, b.back, b.inbound_term = b.project_back(*b.tokens, *b_sums)
    gain_terms = jnp.concatenate(
        [
            a.inbound_term + b.inbound_term,
            a.attended_term + b.attended_term,
            a.prefeed_term + b.prefeed_term,
            a.postfeed_term + b.postfeed_term,
        ]
    ).astype(bf16)
    gain_terms = gain_terms.reshape(4, chips, 2, count).transpose(1, 2, 0, 3)
    gain_terms = jnp.roll(gain_terms.reshape(chips, 1, 8 * count), -z, axis=0)
    gain_terms = jnp.stack(line.exchanged([gain_terms[k] for k in range(chips)]))
    gain_terms = jnp.pad(gain_terms, ((0, 0), (0, pad - 1), (0, width - 8 * count)))
    ex = Exchange(line)
    ex.parts = [jnp.concatenate([part, gain_terms[k]]) for k, part in enumerate(split(grad))]
    ex.first = ex.parts[0]

    def attention_grads(back_a, back_b):
        return weight_grad(2, back_a, back_b, *a.hidden, *b.hidden) + weight_grad(
            2, a.attended, b.attended, a.branch_low, b.branch_low
        )

    def attention_sums(qkv_grad, output_grad):
        return tuple(
            value.astype(bf16)
            for value in (
                pair_sum(qkv_grad[:query_width]),
                group_sum(qkv_grad[query_width : query_width + HEAD_DIM]),
                group_sum(qkv_grad[query_width + HEAD_DIM :]),
                pair_sum(output_grad),
            )
        )

    late = ex.step(attention_grads, (a.back, b.back), held=early_sums)
    down_sum, gate_sum = ex.held

    def sums_work(down_sum, gate_sum, *late):
        return attention_sums(*late), down_sum.astype(f32), gate_sum.astype(f32)

    late, down_sum, gate_sum = ex.step(sums_work, (down_sum, gate_sum, *late))
    for _ in range(chips - 4):
        ex.step()
    ex.step()
    late_sum = data_exchange_sum(jnp.concatenate(late), 2)
    grad = total(ex.terms())
    tokens_grad_b = b.after_project_back([grad[:rows]])

    row = grad[rows, : 8 * count].reshape(2, 4, count)
    mine = jnp.where(c == 0, row[0], row[1])
    other = jnp.where(c == 0, row[1], row[0])
    gain_sums = mine + line.swap(other.astype(bf16)).astype(f32)
    if data == 4:
        for bit in (1, 2):
            gain_sums = gain_sums + swapped(gain_sums, bit)
    else:
        gain_sums = lax.psum(gain_sums, "dp")

    late_sums, row = [], 0
    for value in late:
        late_sums.append(late_sum[row : row + value.shape[0]])
        row += value.shape[0]
    *done, up_sum = tied(
        jnp.stack([a.output, b.output]),
        jnp.stack([tokens_grad_a, tokens_grad_b]),
        *late_sums,
        gate_sum,
        down_sum,
        gain_sums,
        up_sum,
    )
    up_sum = up_sum.astype(f32)
    return (*done[:7], up_sum, done[7], *done[8])


def solution(mesh):
    rows = P("ctx", None)
    gain = P("ctx")
    tokens = P("dp", "ctx", None)
    spans = P("dp", None)
    return jax.shard_map(
        on_device,
        mesh=mesh,
        in_specs=(tokens, spans, spans) + (rows,) * 7 + (gain,) * 4 + (tokens,),
        out_specs=(tokens, tokens) + (rows,) * 7 + (gain,) * 4,
        check_vma=False,
    )
```

```python
import functools

import jax
import jax.numpy as jnp
from jax import lax
from jax.experimental import pallas as pl
from jax.experimental.pallas import tpu as pltpu
from jax.sharding import PartitionSpec as P

HEADS = 8
KV_HEADS = 4
HEAD_DIM = 256
HALF = HEAD_DIM // 2

epsilon = 1e-06
soft_cap = 50.0
rope_base = 10000.0
gelu_a = 0.7978845608028654
gelu_b = 0.044715
query_scale = HEAD_DIM ** (-0.5)

bf16 = jnp.bfloat16
f32 = jnp.float32


def nt(left_side, right_side):
    return lax.dot_general(
        left_side, right_side, (((1,), (1,)), ((), ())), preferred_element_type=f32
    )


def nn(left_side, right_side):
    return lax.dot_general(
        left_side, right_side, (((1,), (0,)), ((), ())), preferred_element_type=f32
    )


def tn(left_side, right_side):
    return lax.dot_general(
        left_side, right_side, (((0,), (0,)), ((), ())), preferred_element_type=f32
    )


def inverse_root(values):
    return lax.rsqrt(jnp.mean(values * values, axis=-1, keepdims=True) + epsilon)


def norm_backward(normed, root, gain, grad):
    scaled = grad * gain
    return root * (scaled - normed * jnp.mean(scaled * normed, axis=-1, keepdims=True))


class Line:
    def __init__(self, size, index):
        self.chips = size // 2
        self.z = index // 2
        self.c = index % 2
        self.core_pairs = [(i, i ^ 1) for i in range(size)]

    def pairs(self, step, low, high):
        return [
            (2 * z + c, 2 * (z + step) + c)
            for z in range(low, high)
            for c in range(2)
            if 0 <= z + step < self.chips
        ]

    def right(self, block, low, high):
        return lax.ppermute(block, "ctx", self.pairs(1, low, high))

    def left(self, block, low, high):
        n = self.chips
        return lax.ppermute(block, "ctx", self.pairs(-1, n - high, n - low))

    def swap(self, block):
        return lax.ppermute(block, "ctx", self.core_pairs)

    def exchanged(self, items):
        last = self.z == self.chips - 1
        items = list(items)
        first, final = items[1], items[-1]
        items[1] = jnp.where(last, final, first)
        items[-1] = jnp.where(last, first, final)
        return items

    def table(self):
        order = self.exchanged([jnp.int32(k) for k in range(self.chips)])
        return [lax.rem(self.z + k, self.chips) for k in order]


def tied(*values):
    return lax.optimization_barrier(values)


class Exchange:
    def __init__(self, line, own=None, sums=True):
        self.line, self.own, self.sums = line, own, sums
        self.parts = None
        self.s = 0
        self.from_left, self.from_right = [own], [own]
        self.sum_left = self.sum_right = None

    def step(self, work=None, inputs=(), held=()):
        line, n, z = self.line, self.line.chips, self.line.z
        gathers = self.own is not None
        self.s += 1
        s = self.s
        to_right = to_left = None
        low, high = 0, n
        if gathers and s <= n - 1:
            to_right, to_left = self.from_left[s - 1], self.from_right[s - 1]
            low = s - 1
        j = s - 1 if gathers else s
        if self.sums and j >= 1:
            sum_r, sum_l = self.parts[n - j], self.parts[n - 1 if j == 1 else j]
            if j == n - 1:
                sum_l = jnp.where(z == n - 1, self.parts[1], self.parts[n - 1])
            if self.sum_left is not None:
                sum_r = (sum_r.astype(f32) + self.sum_left.astype(f32)).astype(bf16)
                sum_l = (sum_l.astype(f32) + self.sum_right.astype(f32)).astype(bf16)
            if to_right is None:
                to_right, to_left, high = sum_r, sum_l, j
            else:
                to_right = jnp.where(z >= s - 1, to_right, sum_r)
                to_left = jnp.where(n - 1 - z >= s - 1, to_left, sum_l)
                low = 0
        to_right, to_left, inputs, self.held = tied(to_right, to_left, inputs, held)
        got_left = line.right(to_right, low, high)
        got_right = line.left(to_left, low, high)
        outs = work(*inputs) if work is not None else ()
        got_left, got_right, outs = tied(got_left, got_right, outs)
        if gathers and s <= n - 1:
            self.from_left.append(got_left)
            self.from_right.append(got_right)
        if self.sums and j >= 1:
            self.sum_left, self.sum_right = got_left, got_right
        return outs

    def give(self, *halves):
        rows = halves[-1].shape[0] // (self.line.chips if len(halves) == 1 else self.line.chips - 2)
        self.first = halves[0]
        self.parts = [
            half[k * rows : (k + 1) * rows]
            for half in halves
            for k in range(half.shape[0] // rows)
        ]

    def near(self):
        last = self.line.z == self.line.chips - 1
        return [self.own, jnp.where(last, self.from_left[1], self.from_right[1])]

    def far(self):
        n, z = self.line.chips, self.line.z
        blocks = [
            jnp.where(z + k < n, self.from_right[k], self.from_left[n - k])
            for k in range(2, n - 1)
        ]
        final = jnp.where(z == 0, self.from_right[n - 1], self.from_left[1])
        return blocks + [jnp.where(z == n - 1, self.from_left[n - 1], final)]

    def terms(self):
        return (self.first, self.sum_left, self.sum_right)


def total(terms):
    rows = terms[-1].shape[0]
    return sum(t[:rows].astype(f32) for t in terms)


def spans_of(place, info, spans, none):
    label = jnp.full(place.shape, none, jnp.int32)
    for s in range(spans):
        start, stop = info[1 + s], info[1 + spans + s]
        label = jnp.where((place >= start) & (place < stop), s, label)
    return label


def seen_block(query_block, key_block, width, info, spans):
    seen = key_block <= query_block
    for s in range(spans):
        start, stop = info[1 + s], info[1 + spans + s]
        seen = seen | ((start < (query_block + 1) * width) & (stop > key_block * width))
    return seen


def block_mask(query_block, key_block, rows, info, spans):
    c = info[0]
    width = 2 * rows
    query_place = (
        query_block * width + c * rows + lax.broadcasted_iota(jnp.int32, (rows, 1), 0)
    )
    j = lax.broadcasted_iota(jnp.int32, (1, width), 1)
    key_place = key_block * width + j + jnp.where(j < rows, c * rows, -c * rows)
    query_span = spans_of(query_place, info, spans, -2)
    key_span = spans_of(key_place, info, spans, -1)
    return (key_place <= query_place) | (key_span == query_span)


def place_of(refs, kk):
    return refs[0][kk] if kk < 2 else refs[1][kk - 2]


def key_block_of(own_refs, other_refs, kk, part):
    cut = slice(part * HEAD_DIM, (part + 1) * HEAD_DIM)
    return jnp.concatenate([place_of(own_refs, kk)[:, cut], place_of(other_refs, kk)[:, cut]])


def forward_kernel(spans, heads, info, *refs):
    queries, own, other = refs[0:2], refs[2:4], refs[4:6]
    o_ref, acc_ref, sum_ref = refs[6:]
    rows = own[0].shape[1]
    chips = own[0].shape[0] + own[1].shape[0]
    width = 2 * rows
    query_block = info[1 + 2 * spans + pl.program_id(0)]
    query = jnp.where(pl.program_id(0) < 2, queries[0][0], queries[1][0])
    acc_ref[...] = jnp.zeros_like(acc_ref)
    sum_ref[...] = jnp.zeros_like(sum_ref)
    for kk in range(chips):
        key_block = info[1 + 2 * spans + kk]

        @pl.when(seen_block(query_block, key_block, width, info, spans))
        def _():
            allowed = block_mask(query_block, key_block, rows, info, spans)
            keys, values = (key_block_of(own, other, kk, part) for part in range(2))
            for h in range(heads):
                scores = nt(query[:, h * HEAD_DIM : (h + 1) * HEAD_DIM], keys)
                weights = jnp.where(
                    allowed, jnp.exp(soft_cap * jnp.tanh(scores * (1.0 / soft_cap))), 0.0
                )
                sum_ref[h] += jnp.sum(weights, axis=1, keepdims=True)
                acc_ref[h] += nn(weights.astype(bf16), values)

    for h in range(heads):
        o_ref[0, :, h * HEAD_DIM : (h + 1) * HEAD_DIM] = (acc_ref[h] / sum_ref[h]).astype(bf16)


def turned_back(vectors, cosine, sine):
    first, second = vectors[:, :HALF], vectors[:, HALF:]
    return first * cosine + second * sine, second * cosine - first * sine


def backward_kernel(spans, heads, info, *refs):
    queries, own, other = refs[0:2], refs[2:4], refs[4:6]
    g_ref, cos_ref, sin_ref, tables = refs[6], refs[7], refs[8], refs[9:13]
    dq_ref, own_ref, other_ref = refs[13:16]
    dk_ref, dv_ref, p_ref, r_ref, t_ref, sum_ref, inner_ref, acc_ref = refs[16:]
    chips, width, _ = dk_ref.shape
    rows = width // 2
    query_block = info[1 + 2 * spans + pl.program_id(0)]
    query = jnp.where(pl.program_id(0) < 2, queries[0][0], queries[1][0])

    @pl.when(pl.program_id(0) == 0)
    def _():
        dk_ref[...] = jnp.zeros_like(dk_ref)
        dv_ref[...] = jnp.zeros_like(dv_ref)

    acc_ref[...] = jnp.zeros_like(acc_ref)
    sum_ref[...] = jnp.zeros_like(sum_ref)
    inner_ref[...] = jnp.zeros_like(inner_ref)
    for kk in range(chips):
        key_block = info[1 + 2 * spans + kk]

        @pl.when(seen_block(query_block, key_block, width, info, spans))
        def _():
            allowed = block_mask(query_block, key_block, rows, info, spans)
            keys, values = (key_block_of(own, other, kk, part) for part in range(2))
            for h in range(heads):
                head = slice(h * HEAD_DIM, (h + 1) * HEAD_DIM)
                squashed = jnp.tanh(nt(query[:, head], keys) * (1.0 / soft_cap))
                weights = jnp.where(allowed, jnp.exp(soft_cap * squashed), 0.0)
                row_grad = nt(g_ref[0, :, head], values)
                sum_ref[h] += jnp.sum(weights, axis=1, keepdims=True)
                inner_ref[h] += jnp.sum(weights * row_grad, axis=1, keepdims=True)
                p_ref[kk, h] = weights
                r_ref[kk, h] = row_grad
                t_ref[kk, h] = 1.0 - squashed * squashed

    for kk in range(chips):
        key_block = info[1 + 2 * spans + kk]

        @pl.when(seen_block(query_block, key_block, width, info, spans))
        def _():
            keys = key_block_of(own, other, kk, 0)
            for h in range(heads):
                head = slice(h * HEAD_DIM, (h + 1) * HEAD_DIM)
                inverse = 1.0 / sum_ref[h]
                weights = p_ref[kk, h] * inverse
                inner = inner_ref[h] * inverse
                score_grad = (weights * (r_ref[kk, h] - inner) * t_ref[kk, h]).astype(bf16)
                acc_ref[h] += nn(score_grad, keys)
                dk_ref[kk] += tn(score_grad, query[:, head])
                dv_ref[kk] += tn(weights.astype(bf16), g_ref[0, :, head])

    for h in range(heads):
        first, second = turned_back(acc_ref[h], cos_ref[0], sin_ref[0])
        dq_ref[0, :, h * HEAD_DIM : h * HEAD_DIM + HALF] = (first * query_scale).astype(bf16)
        dq_ref[0, :, h * HEAD_DIM + HALF : (h + 1) * HEAD_DIM] = (second * query_scale).astype(bf16)

    @pl.when(pl.program_id(0) == chips - 1)
    def _():
        for kk in range(chips):
            for part, out in ((0, own_ref), (1, other_ref)):
                some = slice(part * rows, (part + 1) * rows)
                first, second = turned_back(
                    dk_ref[kk, some], tables[2 * part][kk], tables[2 * part + 1][kk]
                )
                out[kk, :, :HALF] = first.astype(out.dtype)
                out[kk, :, HALF:HEAD_DIM] = second.astype(out.dtype)
                out[kk, :, HEAD_DIM:] = dv_ref[kk, some].astype(out.dtype)


def block_spec(shape):
    return pl.BlockSpec((1,) + tuple(shape[1:]), lambda i, info: (i, 0, 0))


def near_spec(shape):
    return pl.BlockSpec((1,) + tuple(shape[1:]), lambda i, info: (jnp.minimum(i, 1), 0, 0))


def far_spec(shape):
    return pl.BlockSpec((1,) + tuple(shape[1:]), lambda i, info: (jnp.maximum(i - 2, 0), 0, 0))


def whole_spec(shape):
    return pl.BlockSpec(tuple(shape), lambda i, info: (0,) * len(shape))


light = pl.CostEstimate(flops=1024, bytes_accessed=1024, transcendentals=0)


def attend_forward(info, queries, own, other, spans):
    (near, rows, features), far = queries[0].shape, queries[1].shape[0]
    chips, heads = near + far, features // HEAD_DIM
    arrays = (*queries, *own, *other)
    out = jax.ShapeDtypeStruct((chips, rows, features), bf16)
    return pl.pallas_call(
        functools.partial(forward_kernel, spans, heads),
        out_shape=out,
        grid_spec=pltpu.PrefetchScalarGridSpec(
            num_scalar_prefetch=1,
            grid=(chips,),
            in_specs=[near_spec(queries[0].shape), far_spec(queries[1].shape)]
            + [whole_spec(x.shape) for x in arrays[2:]],
            out_specs=block_spec(out.shape),
            scratch_shapes=[
                pltpu.VMEM((heads, rows, HEAD_DIM), f32),
                pltpu.VMEM((heads, rows, 1), f32),
            ],
        ),
        compiler_params=pltpu.CompilerParams(vmem_limit_bytes=20 * 1024 * 1024),
        cost_estimate=light,
    )(info, *arrays)


def attend_backward(info, queries, own, other, grads, tables, spans):
    chips, rows, features = grads.shape
    heads = features // HEAD_DIM
    arrays = (*queries, *own, *other, grads, tables[0], tables[1], *tables)
    square = pltpu.VMEM((chips, heads, rows, 2 * rows), f32)
    pairs = (chips, rows, 2 * HEAD_DIM)
    return pl.pallas_call(
        functools.partial(backward_kernel, spans, heads),
        out_shape=(
            jax.ShapeDtypeStruct(grads.shape, bf16),
            jax.ShapeDtypeStruct(pairs, f32),
            jax.ShapeDtypeStruct(pairs, bf16),
        ),
        grid_spec=pltpu.PrefetchScalarGridSpec(
            num_scalar_prefetch=1,
            grid=(chips,),
            in_specs=[near_spec(queries[0].shape), far_spec(queries[1].shape)]
            + [whole_spec(x.shape) for x in arrays[2:6]]
            + [block_spec(x.shape) for x in arrays[6:9]]
            + [whole_spec(x.shape) for x in arrays[9:]],
            out_specs=(block_spec(grads.shape), whole_spec(pairs), whole_spec(pairs)),
            scratch_shapes=[
                pltpu.VMEM((chips, 2 * rows, HEAD_DIM), f32),
                pltpu.VMEM((chips, 2 * rows, HEAD_DIM), f32),
                square,
                square,
                square,
                pltpu.VMEM((heads, rows, 1), f32),
                pltpu.VMEM((heads, rows, 1), f32),
                pltpu.VMEM((heads, rows, HEAD_DIM), f32),
            ],
        ),
        compiler_params=pltpu.CompilerParams(vmem_limit_bytes=30 * 1024 * 1024),
        cost_estimate=light,
    )(info, *arrays)


def row_call(kernel, grid, ins, outs, *arrays):
    return pl.pallas_call(
        kernel,
        out_shape=tuple(out[0] for out in outs),
        grid=(grid,),
        in_specs=[pl.BlockSpec(*spec) for spec in ins],
        out_specs=tuple(pl.BlockSpec(*out[1:]) for out in outs),
        compiler_params=pltpu.CompilerParams(vmem_limit_bytes=24 * 1024 * 1024),
        cost_estimate=light,
    )(*arrays)


def add_rows(ref, rows):
    @pl.when(pl.program_id(0) == 0)
    def _():
        ref[...] = jnp.zeros_like(ref)

    ref[...] += jnp.sum(rows, axis=0, keepdims=True)


def summed(refs):
    return sum(ref[...].astype(f32) for ref in refs)


def project_kernel(heads, x_ref, gain_ref, w_ref, cos_ref, sin_ref, hidden_ref, q_ref, kv_ref):
    values = x_ref[...].astype(f32)
    hidden = (values * inverse_root(values) * gain_ref[0:1]).astype(bf16)
    hidden_ref[...] = hidden
    raw = nt(hidden, w_ref[...])
    cosine, sine = cos_ref[...], sin_ref[...]
    for h in range(heads + 1):
        start = h * HEAD_DIM
        first, second = raw[:, start : start + HALF], raw[:, start + HALF : start + HEAD_DIM]
        turned = first * cosine - second * sine, second * cosine + first * sine
        if h < heads:
            q_ref[:, start : start + HALF] = (turned[0] * query_scale).astype(bf16)
            q_ref[:, start + HALF : start + HEAD_DIM] = (turned[1] * query_scale).astype(bf16)
        else:
            kv_ref[:, :HALF] = turned[0].astype(bf16)
            kv_ref[:, HALF:HEAD_DIM] = turned[1].astype(bf16)
    kv_ref[:, HEAD_DIM:] = raw[:, (heads + 1) * HEAD_DIM :].astype(bf16)


def project(tokens, gains, weight, cosine, sine, rows):
    m, width = tokens.shape
    features = weight.shape[0] - 2 * HEAD_DIM
    whole = lambda i: (0, 0)
    block = lambda i: (i, 0)
    return row_call(
        functools.partial(project_kernel, features // HEAD_DIM),
        m // rows,
        [
            ((rows, width), block),
            (gains.shape, whole),
            (weight.shape, whole),
            ((rows, HALF), block),
            ((rows, HALF), block),
        ],
        [
            (jax.ShapeDtypeStruct((m, n), bf16), (rows, n), block)
            for n in (width, features, 2 * HEAD_DIM)
        ],
        tokens,
        gains,
        weight,
        cosine,
        sine,
    )


def project_back_kernel(dq_ref, own_ref, got_ref, w_ref, near_ref, far_ref, *outs):
    grad_ref, back_ref, inbound_ref = outs
    pairs = (own_ref[...] + got_ref[...].astype(f32)).astype(bf16)
    back = jnp.concatenate([dq_ref[...], pairs], axis=1)
    back_ref[...] = back
    grad = nn(back, w_ref[...])
    grad_ref[...] = grad.astype(bf16)
    values = jnp.where(pl.program_id(0) < 2, near_ref[...], far_ref[...]).astype(f32)
    add_rows(inbound_ref, grad * (values * inverse_root(values)))


def project_back(query_back, own, got, weight, near, far, rows):
    m, features = query_back.shape
    count, width = weight.shape
    block = lambda i: (i, 0)
    whole = lambda i: (0, 0)
    pairs = ((rows, 2 * HEAD_DIM), block)
    return row_call(
        project_back_kernel,
        m // rows,
        [
            ((rows, features), block),
            pairs,
            pairs,
            (weight.shape, whole),
            ((rows, width), lambda i: (jnp.minimum(i, 1), 0)),
            ((rows, width), lambda i: (jnp.maximum(i - 2, 0), 0)),
        ],
        [
            (jax.ShapeDtypeStruct((m, width), bf16), (rows, width), block),
            (jax.ShapeDtypeStruct((m, count), bf16), (rows, count), block),
            (jax.ShapeDtypeStruct((1, width), f32), (1, width), whole),
        ],
        query_back,
        own,
        got,
        weight,
        near,
        far,
    )


def branch_kernel(p_ref, l_ref, r_ref, own_ref, gain_ref, branch_ref, middle_ref, hidden_ref):
    branch = summed((p_ref, l_ref, r_ref))
    branch_ref[...] = branch
    middle = own_ref[...].astype(f32) + branch * inverse_root(branch) * gain_ref[1:2]
    middle_ref[...] = middle
    hidden_ref[...] = (middle * inverse_root(middle) * gain_ref[2:3]).astype(bf16)


def feed_kernel(p_ref, l_ref, r_ref, middle_ref, cot_ref, gain_ref, out_ref, low_ref, term_ref):
    feed = summed((p_ref, l_ref, r_ref))
    root = inverse_root(feed)
    normed = feed * root
    gain = gain_ref[3:4]
    upstream = cot_ref[...].astype(f32)
    out_ref[...] = (middle_ref[...] + normed * gain).astype(bf16)
    low_ref[...] = norm_backward(normed, root, gain, upstream).astype(bf16)
    add_rows(term_ref, upstream * normed)


def feed_back_norm_kernel(p_ref, l_ref, r_ref, middle_ref, branch_ref, cot_ref, gain_ref, *outs):
    grad_ref, low_ref, prefeed_ref, attended_ref = outs
    grad = summed((p_ref, l_ref, r_ref))
    middle = middle_ref[...]
    root = inverse_root(middle)
    normed = middle * root
    add_rows(prefeed_ref, grad * normed)
    middle_grad = cot_ref[...].astype(f32) + norm_backward(normed, root, gain_ref[2:3], grad)
    grad_ref[...] = middle_grad
    branch = branch_ref[...]
    root = inverse_root(branch)
    normed = branch * root
    add_rows(attended_ref, middle_grad * normed)
    low_ref[...] = norm_backward(normed, root, gain_ref[1:2], middle_grad).astype(bf16)


def norm_call(kernel, terms, arrays, gains, sequence, outs):
    rows, width = terms[1].shape
    tile = rows // 2
    block = ((tile, width), lambda i: (i, 0))
    one = ((None, tile, width), lambda i: (sequence, i, 0))
    whole = lambda i: (0, 0)
    return row_call(
        kernel,
        2,
        [block] * 3 + [one if x.ndim == 3 else block for x in arrays] + [(gains.shape, whole)],
        [
            (jax.ShapeDtypeStruct((1, width), f32), (1, width), whole)
            if kind is None
            else (jax.ShapeDtypeStruct((rows, width), kind), *block)
            for kind in outs
        ],
        *terms,
        *arrays,
        gains,
    )


def gate_up_kernel(h_ref, gate_ref, up_ref, product_ref, gelu_ref, slope_ref):
    gate = nt(h_ref[...], gate_ref[...])
    up = nt(h_ref[...], up_ref[...])
    square = gate * gate
    tanh = jnp.tanh(gate * (gelu_a + (gelu_a * gelu_b) * square))
    half = 0.5 + 0.5 * tanh
    gelu = gate * half
    slope = half + gate * (0.5 - 0.5 * tanh * tanh) * (gelu_a + (3.0 * gelu_a * gelu_b) * square)
    product_ref[...] = (gelu * up).astype(bf16)
    gelu_ref[...] = gelu.astype(bf16)
    slope_ref[...] = (up * slope).astype(bf16)


def gate_up(hidden, gate_w, up_w):
    m, width = hidden.shape
    n = gate_w.shape[0]
    tile = next(t for t in (768, 384, 256, 128) if n % t == 0)
    weight_spec = pl.BlockSpec((tile, width), lambda i: (i, 0))
    out_spec = pl.BlockSpec((m, tile), lambda i: (0, i))
    return pl.pallas_call(
        gate_up_kernel,
        out_shape=(jax.ShapeDtypeStruct((m, n), bf16),) * 3,
        grid=(n // tile,),
        in_specs=[pl.BlockSpec((m, width), lambda i: (0, 0)), weight_spec, weight_spec],
        out_specs=(out_spec,) * 3,
        compiler_params=pltpu.CompilerParams(vmem_limit_bytes=30 * 1024 * 1024),
        cost_estimate=light,
    )(hidden, gate_w, up_w)


def mix_kernel(*refs):
    count = len(refs) // 2
    out = sum(nn(refs[i][...], refs[count + i][...]) for i in range(count))
    refs[-1][...] = out.astype(bf16)


def mix(lefts, weights):
    m, depth = lefts[0].shape
    n = weights[0].shape[1]
    tile = next(t for t in (768, 384, 256, 128) if n % t == 0)
    return pl.pallas_call(
        mix_kernel,
        out_shape=jax.ShapeDtypeStruct((m, n), bf16),
        grid=(n // tile,),
        in_specs=[pl.BlockSpec((m, depth), lambda i: (0, 0))] * len(lefts)
        + [pl.BlockSpec((depth, tile), lambda i: (0, i))] * len(weights),
        out_specs=pl.BlockSpec((m, tile), lambda i: (0, i)),
        compiler_params=pltpu.CompilerParams(vmem_limit_bytes=(44 if m <= 384 else 36) * 1024 * 1024),
        cost_estimate=light,
    )(*lefts, *weights)


def feed_back_kernel(low_ref, down_ref, gelu_ref, slope_ref, gate_back_ref, up_back_ref):
    grad = nt(low_ref[...], down_ref[...])
    gate_back_ref[...] = (grad * slope_ref[...].astype(f32)).astype(bf16)
    up_back_ref[...] = (grad * gelu_ref[...].astype(f32)).astype(bf16)


def feed_back(low, down_w, gelu, slope):
    m, width = low.shape
    n = down_w.shape[0]
    tile = next(t for t in (768, 384, 256, 128) if n % t == 0)
    spec = pl.BlockSpec((m, tile), lambda i: (0, i))
    return pl.pallas_call(
        feed_back_kernel,
        out_shape=(jax.ShapeDtypeStruct((m, n), bf16),) * 2,
        grid=(n // tile,),
        in_specs=[
            pl.BlockSpec((m, width), lambda i: (0, 0)),
            pl.BlockSpec((tile, width), lambda i: (i, 0)),
            spec,
            spec,
        ],
        out_specs=(spec,) * 2,
        compiler_params=pltpu.CompilerParams(vmem_limit_bytes=30 * 1024 * 1024),
        cost_estimate=light,
    )(low, down_w, gelu, slope)


def on_device(
    tokens,
    span_start,
    span_len,
    query_weight,
    key_weight,
    value_weight,
    output_weight,
    gate_weight,
    up_weight,
    down_weight,
    inbound_gain,
    attended_gain,
    prefeed_gain,
    postfeed_gain,
    cotangent,
):
    seq_count, rows, width = tokens.shape
    size = lax.axis_size("ctx")
    index = lax.axis_index("ctx")
    line = Line(size, index)
    chips, z, c = line.chips, line.z, line.c
    spans = span_start.shape[1]
    group = size // KV_HEADS
    member = index % group
    every = chips * rows

    def pair_rows(block):
        other = line.swap(block)
        return jnp.concatenate([jnp.where(c == 0, block, other), jnp.where(c == 0, other, block)])

    def shifted(block, k):
        pairs = [(i, i - i % group + (i % group + k) % group) for i in range(size)]
        return lax.ppermute(block, "ctx", pairs)

    def group_rows(block):
        if group == 2:
            return pair_rows(block)
        count = block.shape[0]
        out = jnp.zeros((group * count, width), block.dtype)
        out = lax.dynamic_update_slice(out, block, (member * count, 0))
        for k in range(1, group):
            place = lax.rem(member + group - k, group) * count
            out = lax.dynamic_update_slice(out, shifted(block, k), (place, 0))
        return out

    def group_sum(grad):
        count = grad.shape[0] // group
        own = lax.dynamic_slice(grad, (member * count, 0), (count, width)).astype(f32)
        for k in range(1, group):
            place = lax.rem(member + k, group) * count
            sent = lax.dynamic_slice(grad, (place, 0), (count, width))
            own = own + shifted(sent.astype(bf16), k).astype(f32)
        return own

    def pair_sum(grad):
        count = grad.shape[0] // 2
        own = lax.dynamic_slice(grad, (c * count, 0), (count, width)).astype(f32)
        sent = lax.dynamic_slice(grad, ((1 - c) * count, 0), (count, width))
        return own + line.swap(sent.astype(bf16)).astype(f32)

    def both_rows(block):
        return jnp.concatenate([block, line.swap(block)])

    count = inbound_gain.shape[0]
    pad = 16
    gains_own = jnp.concatenate([inbound_gain, attended_gain, prefeed_gain, postfeed_gain])
    gains_rows = jnp.pad(gains_own[None, :], ((0, pad - 1), (0, width - 4 * count)))

    query_width = 2 * output_weight.shape[0]
    heads = query_width // HEAD_DIM

    table = jnp.stack(line.table()).astype(jnp.int32)
    places = (
        table[:, None] * (2 * rows) + c * rows + jnp.arange(rows, dtype=jnp.int32)[None, :]
    ).reshape(every)
    inverse = rope_base ** (-(jnp.arange(HALF, dtype=f32) * 2.0 / HEAD_DIM))

    def turns(places):
        angles = places.astype(f32)[:, None] * inverse[None, :]
        return jnp.cos(angles), jnp.sin(angles)

    cosine, sine = turns(places)
    tables = [
        t.reshape(chips, rows, HALF)
        for t in (cosine, sine) + turns(places + jnp.where(c == 0, rows, -rows))
    ]

    def split(block_rows):
        return [
            block_rows[k * rows : (k + 1) * rows] for k in range(block_rows.shape[0] // rows)
        ]

    def join(blocks):
        return jnp.concatenate(blocks)

    infos = [
        jnp.concatenate(
            [c[None], span_start[s], span_start[s] + span_len[s], table]
        ).astype(jnp.int32)
        for s in range(seq_count)
    ]

    class Sequence:
        def __init__(self, s):
            self.s = s
            self.own = tokens[s]

        def project(self, places, *blocks):
            count = len(blocks)
            merged = join(blocks)
            some = slice(places.start * rows, places.stop * rows)
            hidden, queries, pairs = project(
                merged, gain, qkv_weight, cosine[some], sine[some], rows
            )
            pairs = pairs.reshape(count, rows, 2 * HEAD_DIM)
            queries = queries.reshape(count, rows, query_width)
            return merged, hidden, queries, pairs, line.swap(pairs)

        def attend(self, *halves):
            queries, own, other = halves[0::3], halves[1::3], halves[2::3]
            attended = attend_forward(infos[self.s], queries, own, other, spans)
            attended = attended.reshape(every, query_width)
            return nn(attended, out_weight).astype(bf16), attended, queries, own, other

        def after_branch(self, terms):
            self.branch, self.middle, hidden = norm_call(
                branch_kernel, terms, (tokens,), gain, self.s, (f32, f32, bf16)
            )
            return hidden

        def feed(self, *blocks):
            hidden_ff = join(blocks)
            return (hidden_ff,) + tuple(gate_up(hidden_ff, gate_rows, up_rows))

        def feed_down(self, product):
            return (mix([product], [down_rows]),)

        def after_feed(self, terms):
            self.output, low, self.postfeed_term = norm_call(
                feed_kernel, terms, (self.middle, cotangent), gain, self.s, (bf16, bf16, None)
            )
            return low

        def feed_back(self, gelu, slope, *blocks):
            feed_low = join(blocks)
            return (feed_low,) + tuple(feed_back(feed_low, down_rows, gelu, slope))

        def feed_in(self, gate_back, up_back):
            return (mix([gate_back, up_back], [gate_rows, up_rows]),)

        def after_feed_back(self, terms):
            self.middle_grad, low, self.prefeed_term, self.attended_term = norm_call(
                feed_back_norm_kernel,
                terms,
                (self.middle, self.branch, cotangent),
                gain,
                self.s,
                (f32, bf16, None, None),
            )
            return low

        def attend_back(self, *blocks):
            branch_low = join(blocks)
            mixed = nt(branch_low, out_weight).astype(bf16).reshape(chips, rows, query_width)
            return (branch_low,) + tuple(
                attend_backward(
                    infos[self.s], self.queries, self.pairs, self.others, mixed, tables, spans
                )
            )

        def project_back(self, near_tokens, far_tokens, query_back, own, other):
            got = line.swap(other)
            return project_back(
                query_back.reshape(every, query_width),
                own.reshape(every, 2 * HEAD_DIM),
                got.reshape(every, 2 * HEAD_DIM),
                qkv_weight,
                near_tokens,
                far_tokens,
                rows,
            )

        def after_project_back(self, terms):
            grad = total(terms)
            values = self.own.astype(f32)
            root = inverse_root(values)
            return (self.middle_grad + norm_backward(values * root, root, gain[0:1], grad)).astype(
                bf16
            )

    def weight_grad(left_count, *pieces):
        return (tn(join(pieces[:left_count]), join(pieces[left_count:])).astype(bf16),)

    data = lax.axis_size("dp")

    def data_sum(values, order):
        groups = [[(i + order) % data for i in range(data)]]
        return lax.psum(values, "dp", axis_index_groups=groups)

    def swapped(block, bit):
        return lax.ppermute(block, "dp", [(i, i ^ bit) for i in range(data)])

    def data_exchange_sum(value, order):
        if data != 4:
            return data_sum(value, order).astype(f32)
        place = lax.axis_index("dp")
        ways = ((place % 2, 1), (place // 2, 2))

        def reduced(block, way):
            bit_value, bit = way
            half = block.shape[0] // 2
            kept = lax.dynamic_slice(block, (bit_value * half, 0), (half, block.shape[1]))
            sent = lax.dynamic_slice(block, ((1 - bit_value) * half, 0), (half, block.shape[1]))
            return (kept.astype(f32) + swapped(sent, bit).astype(f32)).astype(bf16)

        def gathered(block, way):
            bit_value, bit = way
            got = swapped(block, bit)
            low = bit_value == 0
            return jnp.concatenate([jnp.where(low, block, got), jnp.where(low, got, block)])

        middle = value.shape[1] // 2
        halves = [value[:, :middle], value[:, middle:]]
        orders = [ways, ways[::-1]]
        for step, pick in ((reduced, 0), (reduced, 1), (gathered, 1), (gathered, 0)):
            halves = [step(half, one[pick]) for half, one in zip(halves, orders)]
        return jnp.concatenate(halves, axis=1).astype(f32)

    near, far = slice(0, 2), slice(2, chips)

    a, b = (Sequence(s) for s in range(seq_count))

    ex = Exchange(line, jnp.concatenate([a.own, gains_rows]), sums=False)
    def attention_weights(query_w, key_w, value_w):
        return jnp.concatenate([pair_rows(query_w), group_rows(key_w), group_rows(value_w)])

    gate_other = ex.step(line.swap, (gate_weight,))

    def first_weights(gate_w, gate_other, *attention):
        return attention_weights(*attention), jnp.concatenate([gate_w, gate_other])

    qkv_weight, gate_rows = ex.step(
        first_weights, (gate_weight, gate_other, query_weight, key_weight, value_weight)
    )
    out_weight, up_rows = ex.step(
        lambda out_w, up_w: (pair_rows(out_w), both_rows(up_w)), (output_weight, up_weight)
    )
    for _ in range(chips - 4):
        ex.step()
    blocks = ex.near() + ex.far()
    gain = jnp.stack([block[rows, : 4 * count] for block in blocks])
    gain_other = line.swap(gain)
    gain = jnp.stack(
        [jnp.where(c == 0, gain, gain_other), jnp.where(c == 0, gain_other, gain)], axis=1
    ).reshape(chips, 8 * count)
    gain = line.exchanged([gain[k] for k in range(chips)])
    gain = jnp.roll(jnp.stack(gain), z, axis=0).reshape(chips, 2, 4, count)
    gain = gain.transpose(2, 0, 1, 3).reshape(4, width).astype(f32)

    def a_attention(*blocks):
        halves = [a.project(near, *blocks[near]), a.project(far, *blocks[far])]
        out, *kept = a.attend(*halves[0][2:], *halves[1][2:])
        return out, kept, [[half[i] for half in halves] for i in range(2)]

    ex = Exchange(line, b.own)
    out, (a.attended, a.queries, a.pairs, a.others), (a.tokens, a.hidden) = ex.step(
        a_attention, [block[:rows] for block in blocks]
    )
    ex.give(out)

    b_near = ex.step(functools.partial(b.project, near), ex.near())
    down_rows = ex.step(both_rows, (down_weight,))
    for _ in range(chips - 4):
        ex.step()
    b_far = ex.step(functools.partial(b.project, far), ex.far())
    b.tokens, b.hidden = ([b_near[i], b_far[i]] for i in range(2))
    hidden_a = a.after_branch(ex.terms())

    def feed_phase(x, own, first, inputs):
        ex = Exchange(line, own)
        firsts = ex.step(first, inputs)
        yield firsts, ex
        hidden, product, gelu, slope = ex.step(x.feed, ex.near())
        (out,) = ex.step(x.feed_down, (product,))
        for _ in range(chips - 4):
            ex.step()
        x.out_near = out
        lasts = ex.step(x.feed, ex.far())
        x.hidden_ff, x.product, x.gelu, x.slope = (
            [u, v] for u, v in zip((hidden, product, gelu, slope), lasts)
        )
        yield lasts, ex

    steps = feed_phase(a, hidden_a, b.attend, b_near[2:] + b_far[2:])
    (out, b.attended, b.queries, b.pairs, b.others), ex = next(steps)
    ex.give(out)
    next(steps)
    hidden_b = b.after_branch(ex.terms())

    steps = feed_phase(b, hidden_b, a.feed_down, (a.product[1],))
    (out,), ex = next(steps)
    ex.give(a.out_near, out)
    next(steps)
    low_a = a.after_feed(ex.terms())

    def back_phase(x, own, first, inputs):
        ex = Exchange(line, own)
        firsts = ex.step(first, inputs)
        yield firsts, ex
        low, gate_back, up_back = ex.step(
            functools.partial(x.feed_back, x.gelu[0], x.slope[0]), ex.near()
        )
        (x.out_near,) = ex.step(x.feed_in, (gate_back, up_back))
        for _ in range(chips - 4):
            ex.step()

        lasts = ex.step(functools.partial(x.feed_back, x.gelu[1], x.slope[1]), ex.far())
        x.feed_low, x.gate_back, x.up_back = (
            [u, v] for u, v in zip((low, gate_back, up_back), lasts)
        )
        yield lasts, ex

    def b_down(product, *pieces):
        merged = [join(pieces[i : i + 2]) for i in range(0, len(pieces), 2)]
        return (*b.feed_down(product), *merged)

    steps = back_phase(
        a, low_a, b_down, [b.product[1]] + b.gelu + b.slope + b.product + b.hidden_ff
    )
    (out, b_gelu, b_slope, b_product, b_hidden_ff), ex = next(steps)
    ex.give(b.out_near, out)
    next(steps)
    low_b = b.after_feed(ex.terms())

    def grad_part(left, right):
        return tn(join(left), join(right)).astype(bf16)

    def grad_other(left, right, part):
        count = left.shape[1] // 2
        return (tn(left[:, count:], right) + part[count:].astype(f32)).astype(bf16)

    def grad_own(left, right, part, other):
        count = left.shape[1] // 2
        got = line.swap(other).astype(f32)
        return (tn(left[:, :count], right) + part[:count].astype(f32) + got).astype(bf16)

    ex = Exchange(line, low_b)
    (out,) = ex.step(a.feed_in, (a.gate_back[1], a.up_back[1]))
    ex.give(a.out_near, out)

    def part_work(*pieces):
        return tuple(
            grad_part(pieces[i : i + 2], pieces[i + 2 : i + 4]) for i in range(0, len(pieces), 4)
        )

    (part_down,) = ex.step(part_work, a.product + a.feed_low)
    part_gate, part_up = ex.step(
        part_work, a.gate_back + a.hidden_ff + a.up_back + a.hidden_ff
    )
    for _ in range(chips - 4):
        ex.step()

    def b_feed_back(part, *blocks):
        low, gate_back, up_back = b.feed_back(b_gelu, b_slope, *blocks)
        return low, gate_back, up_back, grad_other(b_product, low, part)

    b_low, b_gate_back, b_up_back, down_other = ex.step(
        b_feed_back, [part_down] + ex.near() + ex.far()
    )
    branch_a = a.after_feed_back(ex.terms())

    def b_feed_in(gate_back, up_back, down_other):
        return b.feed_in(gate_back, up_back) + (
            grad_other(gate_back, b_hidden_ff, part_gate),
            grad_own(b_product, b_low, part_down, down_other),
        )

    ex = Exchange(line, branch_a)
    out, gate_other, down_grad = ex.step(b_feed_in, (b_gate_back, b_up_back, down_other))
    ex.give(out)

    def gate_work(gate_back, gate_other):
        return (grad_own(gate_back, b_hidden_ff, part_gate, gate_other),)

    (gate_grad,) = ex.step(gate_work, (b_gate_back, gate_other))

    def up_work(up_back, part):
        other = grad_other(up_back, b_hidden_ff, part)
        return (grad_own(up_back, b_hidden_ff, part, other),)

    (up_grad,) = ex.step(up_work, (b_up_back, part_up))
    early_sums = data_sum((down_grad, gate_grad), 0)
    up_sum = data_sum(up_grad, 1)
    for _ in range(chips - 4):
        ex.step()
    a.branch_low, *a_sums = ex.step(a.attend_back, ex.near() + ex.far())
    branch_b = b.after_feed_back(ex.terms())

    ex = Exchange(line, branch_b)
    out, a.back, a.inbound_term = ex.step(a.project_back, a.tokens + a_sums)
    ex.give(out)
    ex.step()
    ex.step()
    for _ in range(chips - 4):
        ex.step()
    b.branch_low, *b_sums = ex.step(b.attend_back, ex.near() + ex.far())
    tokens_grad_a = a.after_project_back(ex.terms())

    grad, b.back, b.inbound_term = b.project_back(*b.tokens, *b_sums)
    gain_terms = jnp.concatenate(
        [
            a.inbound_term + b.inbound_term,
            a.attended_term + b.attended_term,
            a.prefeed_term + b.prefeed_term,
            a.postfeed_term + b.postfeed_term,
        ]
    ).astype(bf16)
    gain_terms = gain_terms.reshape(4, chips, 2, count).transpose(1, 2, 0, 3)
    gain_terms = jnp.roll(gain_terms.reshape(chips, 1, 8 * count), -z, axis=0)
    gain_terms = jnp.stack(line.exchanged([gain_terms[k] for k in range(chips)]))
    gain_terms = jnp.pad(gain_terms, ((0, 0), (0, pad - 1), (0, width - 8 * count)))
    ex = Exchange(line)
    ex.parts = [jnp.concatenate([part, gain_terms[k]]) for k, part in enumerate(split(grad))]
    ex.first = ex.parts[0]

    def attention_grads(back_a, back_b):
        return weight_grad(2, back_a, back_b, *a.hidden, *b.hidden) + weight_grad(
            2, a.attended, b.attended, a.branch_low, b.branch_low
        )

    def attention_sums(qkv_grad, output_grad):
        return tuple(
            value.astype(bf16)
            for value in (
                pair_sum(qkv_grad[:query_width]),
                group_sum(qkv_grad[query_width : query_width + HEAD_DIM]),
                group_sum(qkv_grad[query_width + HEAD_DIM :]),
                pair_sum(output_grad),
            )
        )

    late = ex.step(attention_grads, (a.back, b.back), held=early_sums)
    down_sum, gate_sum = ex.held

    def sums_work(down_sum, gate_sum, *late):
        return attention_sums(*late), down_sum.astype(f32), gate_sum.astype(f32)

    late, down_sum, gate_sum = ex.step(sums_work, (down_sum, gate_sum, *late))
    for _ in range(chips - 4):
        ex.step()
    ex.step()
    late_sum = data_exchange_sum(jnp.concatenate(late), 2)
    grad = total(ex.terms())
    tokens_grad_b = b.after_project_back([grad[:rows]])

    row = grad[rows, : 8 * count].reshape(2, 4, count)
    mine = jnp.where(c == 0, row[0], row[1])
    other = jnp.where(c == 0, row[1], row[0])
    gain_sums = mine + line.swap(other.astype(bf16)).astype(f32)
    if data == 4:
        for bit in (1, 2):
            gain_sums = gain_sums + swapped(gain_sums, bit)
    else:
        gain_sums = lax.psum(gain_sums, "dp")

    late_sums, row = [], 0
    for value in late:
        late_sums.append(late_sum[row : row + value.shape[0]])
        row += value.shape[0]
    *done, up_sum = tied(
        jnp.stack([a.output, b.output]),
        jnp.stack([tokens_grad_a, tokens_grad_b]),
        *late_sums,
        gate_sum,
        down_sum,
        gain_sums,
        up_sum,
    )
    up_sum = up_sum.astype(f32)
    return (*done[:7], up_sum, done[7], *done[8])


def solution(mesh):
    rows = P("ctx", None)
    gain = P("ctx")
    tokens = P("dp", "ctx", None)
    spans = P("dp", None)
    return jax.shard_map(
        on_device,
        mesh=mesh,
        in_specs=(tokens, spans, spans) + (rows,) * 7 + (gain,) * 4 + (tokens,),
        out_specs=(tokens, tokens) + (rows,) * 7 + (gain,) * 4,
        check_vma=False,
    )
```
